128 devices in a mesh: frame: 4 (over z), batch: 32 (over x, y, core).
Axes of the slice: x: 4, y: 4, z: 4, core: 2. Of those that a mesh axis runs over, the one named last changes fastest.
Arguments:
- frames: bfloat16 [32, 4, 1024, 256], P('batch', None, 'frame'), may hold values from -6 to 6
- utt_len: int32 [32, 4], P('batch'), may hold values from 103 to 1024, as said below
- token_ids: int32 [32, 4, 128], P('batch', 'frame'), may hold values from 0 to 4999
- tok_len: int32 [32, 4], P('batch', 'frame'), may hold values from 38 to 128, as said below
- step: int32 [1], replicated, may hold values from 12500 to 99999
- embed: bfloat16 [5000, 256], replicated, may hold values from -0.375 to 0.375
- norm_gain: float32 [5, 256], replicated, may hold values from 0.5 to 1.5
- norm_bias: float32 [5, 256], replicated, may hold values from -1.25 to 1.25
- attn_in: bfloat16 [3, 256, 768], replicated, may hold values from -0.375 to 0.375
- attn_in_bias: float32 [3, 512], replicated, may hold values from -1.25 to 1.25
- attn_out: bfloat16 [3, 256, 256], replicated, may hold values from -1.5 to 1.5
- attn_out_bias: float32 [3, 256], replicated, may hold values from -1.25 to 1.25
- ff_in: bfloat16 [2, 256, 2048], replicated, may hold values from -0.375 to 0.375
- ff_in_bias: float32 [2, 2048], replicated, may hold values from -1.25 to 1.25
- ff_out: bfloat16 [2, 2048, 256], replicated, may hold values from -0.125 to 0.125
- ff_out_bias: float32 [2, 256], replicated, may hold values from -1.25 to 1.25
- cotangent: bfloat16 [32, 4, 128, 256], P('batch', 'frame'), may hold values from -6 to 6
Outputs:
- dec_out: bfloat16 [32, 4, 128, 256], P('batch', 'frame')
- frames_grad: float32 [32, 4, 1024, 256], P('batch', None, 'frame')
- embed_grad: float32 [5000, 256], replicated
- norm_gain_grad: float32 [5, 256], replicated
- norm_bias_grad: float32 [5, 256], replicated
- attn_in_grad: float32 [3, 256, 768], replicated
- attn_in_bias_grad: float32 [3, 512], replicated
- attn_out_grad: float32 [3, 256, 256], replicated
- attn_out_bias_grad: float32 [3, 256], replicated
- ff_in_grad: float32 [2, 256, 2048], replicated
- ff_in_bias_grad: float32 [2, 2048], replicated
- ff_out_grad: float32 [2, 2048, 256], replicated
- ff_out_bias_grad: float32 [2, 256], replicated
The draws below stay inside these ranges and needn't reach their ends.
Inputs may be any that keep to these rules, and one draw needn't show every extreme that they name: `utt_len`: in every group one utterance, drawn from the seed, has exactly 1024 frames. `tok_len`: in every group one transcript, drawn from the seed, has exactly 128 tokens.
All inputs are finite; a program needn't handle non-finite values.
Results may differ from the reference program's by a relative error of at most 0.018.
Values may be sent and summed in bfloat16 or wider, within the bound.
No kernel may reach another device: no remote copies, remote signals or barrier semaphores. Data moves between devices by JAX's collectives and lax.ppermute only.
A program may use at most 192 MiB of HBM per device.

```python
import math
import jax
import jax.numpy as jnp
import numpy as np
from jax import lax

D = 256
HEADS = 4
HEAD_DIM = 64
FF = 2048
VOCAB = 5000
LEN = 1024
TLEN = 128
WARMUP = 25000
UTT = 4
GROUPS = 32


def draw_lengths(key, lowest, highest):
    key_values, key_full = jax.random.split(key)
    picked = jax.random.randint(key_values, (GROUPS, UTT), lowest, highest + 1)
    chosen = jax.random.randint(key_full, (GROUPS,), 0, UTT)
    return jnp.where(jnp.arange(UTT)[None, :] == chosen[:, None], highest, picked).astype(jnp.int32)


def draw_utt_len(key, part):
    key = jax.random.fold_in(key, 11)
    return draw_lengths(key, LEN // 10 + 1, LEN)


def draw_tok_len(key, part):
    key = jax.random.fold_in(key, 23)
    return draw_lengths(key, TLEN * 3 // 10, TLEN)


def with_ends(drawn, rng, least, largest):
    extent = drawn.shape
    spot = [jax.random.randint(jax.random.fold_in(rng, axis), (), 0, extent[axis]) for axis in range(len(extent))]
    drawn = drawn.at[tuple(spot)].set(least)
    longest = extent.index(max(extent))
    spot[longest] = (spot[longest] + 1) % extent[longest]
    return drawn.at[tuple(spot)].set(largest)


def level_of(own_key, dims, cuts, low, largest):
    factor_of = 1.0
    for dim, parts in cuts:
        draws = jax.random.uniform(jax.random.fold_in(jax.random.fold_in(own_key, 6), dim), (parts,), jnp.float32, low / len(cuts), largest / len(cuts))
        factor_of = factor_of * jnp.repeat(jnp.exp(draws), dims[dim] // parts).reshape((-1,) + (1,) * (len(dims) - 1 - dim))
    return factor_of


def cumulative_ranks(number_of, slope):
    weights = [(1 << 20) // math.isqrt(standing ** slope) + 1 for standing in range(1, number_of + 1)]
    deviation = 1 + sum(weights) // (1 << 30)
    return np.cumsum(np.array([max(1, weight // deviation) for weight in weights]))


def ranked(stream_key, dims, number_of, slope):
    listing = cumulative_ranks(number_of, slope)
    pick = jax.random.randint(jax.random.fold_in(stream_key, 1), dims, 0, int(listing[number_of - 1]))
    grade = jnp.searchsorted(jnp.asarray(listing, jnp.int32), pick, side="right")
    return jax.random.permutation(jax.random.fold_in(stream_key, 2), number_of)[grade].astype(jnp.int32)


def normal_values(own_key, extent, scale, reach, cuts=(), held_as=jnp.bfloat16):
    factor_of = level_of(own_key, extent, cuts, -0.22, 0.18) if cuts else 1.0
    array = jax.random.normal(own_key, extent, jnp.float32) * scale * factor_of
    return jnp.minimum(jnp.maximum(array, -reach), reach).astype(held_as)


def setup_inputs(seed: int = 0) -> dict:
    key_list = jax.random.split(jax.random.key(seed), 18)
    frames = normal_values(key_list[0], (GROUPS, UTT, LEN, D), 1.0, 6.0, ((0, 32), (2, 4)))
    utt_len = draw_utt_len(jax.random.fold_in(key_list[17], 71), 0)
    token_ids = with_ends(ranked(key_list[2], (GROUPS, UTT, TLEN), VOCAB, 2), jax.random.fold_in(key_list[2], 3), 0, VOCAB - 1).astype(jnp.int32)
    tok_len = draw_tok_len(jax.random.fold_in(key_list[17], 71), 0)
    step = jax.random.randint(key_list[4], (1,), WARMUP // 2, WARMUP * 4).astype(jnp.int32)
    embed = normal_values(key_list[5], (VOCAB, D), (D ** -0.5), 0.375)
    norm_gain = jnp.clip(1.0 + 0.1 * jax.random.normal(key_list[6], (5, D), jnp.float32), 0.5, 1.5)
    norm_bias = normal_values(key_list[7], (5, D), 0.2, 1.25, (), jnp.float32)
    attn_in = normal_values(key_list[8], (3, D, 3 * D), D ** -0.5, 0.375)
    attn_in_bias = normal_values(key_list[9], (3, 2 * D), 0.2, 1.25, (), jnp.float32)
    attn_out = normal_values(key_list[10], (3, D, D), (D // 16) ** -0.5, 1.5)
    attn_out_bias = normal_values(key_list[11], (3, D), 0.2, 1.25, (), jnp.float32)
    ff_in = normal_values(key_list[12], (2, D, FF), D ** -0.5, 0.375)
    ff_in_bias = normal_values(key_list[13], (2, FF), 0.2, 1.25, (), jnp.float32)
    ff_out = normal_values(key_list[14], (2, FF, D), FF ** -0.5, 0.125)
    ff_out_bias = normal_values(key_list[15], (2, D), 0.2, 1.25, (), jnp.float32)
    cotangent = normal_values(key_list[16], (GROUPS, UTT, TLEN, D), 1.0, 6.0, ((0, 32), (1, 4)))
    return {"frames": frames, "utt_len": utt_len, "token_ids": token_ids, "tok_len": tok_len, "step": step, "embed": embed, "norm_gain": norm_gain, "norm_bias": norm_bias, "attn_in": attn_in, "attn_in_bias": attn_in_bias, "attn_out": attn_out, "attn_out_bias": attn_out_bias, "ff_in": ff_in, "ff_in_bias": ff_in_bias, "ff_out": ff_out, "ff_out_bias": ff_out_bias, "cotangent": cotangent}


@jax.custom_vjp
def low(v):
    return lax.optimization_barrier(v.astype(jnp.bfloat16)).astype(jnp.float32)

@jax.custom_vjp
def low_back(v):
    return v

def low_keep(v):
    return (low(v), None)

def low_pass(kept, grad):
    return (grad,)

def back_keep(v):
    return (v, None)

def back_low(kept, grad):
    return (low(grad),)
low.defvjp(low_keep, low_pass)
low_back.defvjp(back_keep, back_low)
EPSILON = 1e-05
MASKED = -1e+30

def highest_dot(left, right):
    return jnp.matmul(left, right, precision=lax.Precision.HIGHEST)

def layer_norm(states, gain, shift):
    average = lax.optimization_barrier(jnp.mean(states, axis=-1, keepdims=True))
    centred = states - average
    variance = lax.optimization_barrier(jnp.mean(centred * centred, axis=-1, keepdims=True))
    return centred * lax.rsqrt(variance + EPSILON) * gain + shift

def split_heads(matrix):
    return matrix.reshape(matrix.shape[0], matrix.shape[1], HEADS, HEAD_DIM)

def attend(normed, source, w_in, b_in, w_out, b_out, key_mask):
    width = normed.shape[-1]
    queries = low_back(low(highest_dot(normed, w_in[:, :width]) + b_in[:width]))
    key_rows = low_back(low(highest_dot(source, w_in[:, width:2 * width])))
    values = low_back(low(highest_dot(source, w_in[:, 2 * width:]) + b_in[width:]))
    raw_scores = low_back(jnp.einsum('bqhd,bkhd->bhqk', split_heads(queries), split_heads(key_rows), precision=lax.Precision.HIGHEST))
    scores = jnp.where(key_mask[:, None], raw_scores * HEAD_DIM ** (-0.5), MASKED)
    weights = low(jax.nn.softmax(scores, axis=-1))
    context = jnp.einsum('bhqk,bkhd->bqhd', weights, split_heads(values), precision=lax.Precision.HIGHEST)
    context = low_back(low(context.reshape(normed.shape)))
    return low_back(highest_dot(context, w_out) + b_out)

def feed_forward(normed, w_first, b_first, w_second, b_second):
    hidden = low_back(highest_dot(normed, w_first) + b_first)
    active = low(jax.nn.gelu(hidden))
    return low_back(highest_dot(active, w_second) + b_second)

def group_forward(params, table, inputs, utt_group, ids_group, tok_group):
    gains, shifts, w_in, b_in, w_out, b_out, w_first, b_first, w_second, b_second = params
    frame_valid = jnp.arange(LEN)[None, :] < utt_group[:, None]
    enc_mask = frame_valid[:, None, :]
    normed = low(layer_norm(inputs, gains[0], shifts[0]))
    hidden_state = inputs + attend(normed, normed, w_in[0], b_in[0], w_out[0], b_out[0], enc_mask)
    normed = low(layer_norm(hidden_state, gains[1], shifts[1]))
    memory = low_back(low(hidden_state + feed_forward(normed, w_first[0], b_first[0], w_second[0], b_second[0])))
    places = jnp.arange(TLEN)
    token_valid = places[None, :] < tok_group[:, None]
    self_mask = (places[:, None] >= places[None, :])[None] & token_valid[:, None, :]
    states = table[ids_group] * math.sqrt(D)
    normed = low(layer_norm(states, gains[2], shifts[2]))
    states = states + attend(normed, normed, w_in[1], b_in[1], w_out[1], b_out[1], self_mask)
    normed = low(layer_norm(states, gains[3], shifts[3]))
    states = states + attend(normed, memory, w_in[2], b_in[2], w_out[2], b_out[2], enc_mask)
    normed = low(layer_norm(states, gains[4], shifts[4]))
    states = states + feed_forward(normed, w_first[1], b_first[1], w_second[1], b_second[1])
    return jnp.where(token_valid[..., None], states, 0.0)

def reference(frames, utt_len, token_ids, tok_len, step, embed, norm_gain, norm_bias, attn_in, attn_in_bias, attn_out, attn_out_bias, ff_in, ff_in_bias, ff_out, ff_out_bias, cotangent):
    params = tuple((item.astype(jnp.float32) for item in (norm_gain, norm_bias, attn_in, attn_in_bias, attn_out, attn_out_bias, ff_in, ff_in_bias, ff_out, ff_out_bias)))
    table = embed.astype(jnp.float32)

    def per_group(totals, slices):
        frames_group, utt_group, ids_group, tok_group, cot_group = slices

        def forward(weights, lookup, inputs):
            return group_forward(weights, lookup, inputs, utt_group, ids_group, tok_group)
        output, pullback = jax.vjp(forward, params, table, frames_group.astype(jnp.float32))
        grad_weights, grad_table, grad_frames = pullback(cot_group.astype(jnp.float32))
        totals = jax.tree.map(jnp.add, totals, (grad_weights, grad_table))
        return (totals, (output.astype(jnp.bfloat16), grad_frames))
    zeros = jax.tree.map(jnp.zeros_like, (params, table))
    totals, (outputs, frame_grads) = lax.scan(per_group, zeros, (frames, utt_len, token_ids, tok_len, cotangent))
    weight_grads, table_grad = totals
    count_step = step[0].astype(jnp.float32)
    rate = jnp.minimum(lax.rsqrt(count_step), count_step * WARMUP ** (-1.5)) * WARMUP ** 0.5
    return (outputs, frame_grads, table_grad * rate, weight_grads[0] * rate, weight_grads[1] * rate, weight_grads[2] * rate, weight_grads[3] * rate, weight_grads[4] * rate, weight_grads[5] * rate, weight_grads[6] * rate, weight_grads[7] * rate, weight_grads[8] * rate, weight_grads[9] * rate)
```

```python
import math

import jax
import jax.numpy as jnp
from jax import lax
from jax.sharding import PartitionSpec as P

HEADS = 4
HEAD_DIM = 64
WARMUP = 25000


EPSILON = 1e-05
MASKED = -1e30


def layer_norm(states, gain, shift):
    average = jnp.mean(states, axis=-1, keepdims=True)
    centred = states - average
    variance = jnp.mean(centred * centred, axis=-1, keepdims=True)
    return centred * lax.rsqrt(variance + EPSILON) * gain + shift


def norm_forward(states, gain, shift):
    normed, pullback = jax.vjp(layer_norm, states, gain, shift)
    return (normed.astype(jnp.bfloat16), pullback)


def matmul(left, right):
    return jnp.dot(left, right, preferred_element_type=jnp.float32)


def rows_product(left, right):
    return lax.dot_general(
        left, right, (((0,), (0,)), ((), ())), preferred_element_type=jnp.float32
    )


def cols_product(left, right):
    return lax.dot_general(
        left, right, (((1,), (1,)), ((), ())), preferred_element_type=jnp.float32
    )


def column_sum(matrix):
    return jnp.sum(matrix.astype(jnp.float32), axis=0)


def split_heads(matrix):
    return matrix.reshape(matrix.shape[0], matrix.shape[1], HEADS, HEAD_DIM)


def attention_scores(queries, key_rows, key_mask):
    raw_scores = jnp.einsum(
        "bqhd,bkhd->bhqk",
        split_heads(queries),
        split_heads(key_rows),
        preferred_element_type=jnp.float32,
    )
    return jnp.where(key_mask[:, None], raw_scores * HEAD_DIM ** (-0.5), MASKED)


def attention_forward(queries, key_rows, values, key_mask):
    scores = attention_scores(queries, key_rows, key_mask)
    highest = jnp.max(scores, axis=-1, keepdims=True)
    weights = jnp.exp(scores - highest)
    totals = jnp.sum(weights, axis=-1, keepdims=True)
    probability = (weights / totals).astype(jnp.bfloat16)
    context = jnp.einsum(
        "bhqk,bkhd->bqhd", probability, split_heads(values), preferred_element_type=jnp.float32
    )
    return (context.astype(jnp.bfloat16).reshape(queries.shape), highest + jnp.log(totals))


def attention_backward(queries, key_rows, values, key_mask, log_total, grad_context):
    scores = attention_scores(queries, key_rows, key_mask)
    probability = jnp.exp(scores - log_total)
    grad_heads = split_heads(grad_context)
    grad_values = jnp.einsum(
        "bhqk,bqhd->bkhd",
        probability.astype(jnp.bfloat16),
        grad_heads,
        preferred_element_type=jnp.float32,
    )
    grad_probs = jnp.einsum(
        "bqhd,bkhd->bhqk", grad_heads, split_heads(values), preferred_element_type=jnp.float32
    )
    inner = jnp.sum(grad_probs * probability, axis=-1, keepdims=True)
    grad_raw = (probability * (grad_probs - inner) * HEAD_DIM ** (-0.5)).astype(jnp.bfloat16)
    grad_queries = jnp.einsum(
        "bhqk,bkhd->bqhd", grad_raw, split_heads(key_rows), preferred_element_type=jnp.float32
    )
    grad_keys = jnp.einsum(
        "bhqk,bqhd->bkhd", grad_raw, split_heads(queries), preferred_element_type=jnp.float32
    )
    return (
        grad_queries.reshape(queries.shape),
        grad_keys.reshape(key_rows.shape),
        grad_values.reshape(values.shape),
    )


def feed_forward(normed, w_first, b_first, w_second, b_second):
    hidden = matmul(normed, w_first) + b_first
    active = jax.nn.gelu(hidden).astype(jnp.bfloat16)
    return (matmul(active, w_second) + b_second, hidden, active)


def feed_backward(normed, hidden, active, w_first, w_second, grad_out):
    grad_rounded = grad_out.astype(jnp.bfloat16)
    grad_b_second = column_sum(grad_rounded)
    grad_w_second = rows_product(active, grad_rounded)
    grad_active = cols_product(grad_rounded, w_second)
    gelu_value, gelu_pull = jax.vjp(jax.nn.gelu, hidden)
    grad_hidden = gelu_pull(grad_active)[0].astype(jnp.bfloat16)
    grad_b_first = column_sum(grad_hidden)
    grad_w_first = rows_product(normed, grad_hidden)
    grad_normed = cols_product(grad_hidden, w_first)
    return (grad_normed, grad_w_first, grad_b_first, grad_w_second, grad_b_second)


def branch_backward(context_rows, w_out, grad_state):
    grad_branch = grad_state.astype(jnp.bfloat16)
    grad_bias = column_sum(grad_branch)
    grad_weight = rows_product(context_rows, grad_branch)
    grad_context = cols_product(grad_branch, w_out).astype(jnp.bfloat16)
    return (grad_context, grad_weight, grad_bias)


def body(
    frames,
    utt_len,
    token_ids,
    tok_len,
    step,
    embed,
    norm_gain,
    norm_bias,
    attn_in,
    attn_in_bias,
    attn_out,
    attn_out_bias,
    ff_in,
    ff_in_bias,
    ff_out,
    ff_out_bias,
    cotangent,
):
    width = embed.shape[1]
    frame_count = lax.axis_size("frame")
    frame_index = lax.axis_index("frame")
    utterances = frames.shape[1]
    local_len = frames.shape[2]
    full_len = local_len * frame_count
    per_device = token_ids.shape[1]
    text_len = token_ids.shape[2]
    dec_rows = per_device * text_len
    lengths = lax.dynamic_slice_in_dim(utt_len[0], frame_index, 1)
    key_mask = (jnp.arange(full_len)[None, :] < lengths[:, None])[:, None, :]
    enc_mask = key_mask
    cross_mask = key_mask
    whole = lax.all_to_all(frames[0], "frame", split_axis=0, concat_axis=1, tiled=True)
    enc_rows = full_len
    enc_input = whole.reshape(enc_rows, width).astype(jnp.float32)
    normed_a, pull_a = norm_forward(enc_input, norm_gain[0], norm_bias[0])
    projected = matmul(normed_a, attn_in[0])
    enc_queries = (projected[:, :width] + attn_in_bias[0, :width]).astype(jnp.bfloat16)[None]
    all_keys = projected[:, width : 2 * width].astype(jnp.bfloat16)[None]
    all_values = (projected[:, 2 * width :] + attn_in_bias[0, width:]).astype(jnp.bfloat16)[None]
    enc_context, enc_total = attention_forward(enc_queries, all_keys, all_values, enc_mask)
    enc_context = enc_context.reshape(enc_rows, width)
    after_attn = enc_input + matmul(enc_context, attn_out[0]) + attn_out_bias[0]
    normed_b, pull_b = norm_forward(after_attn, norm_gain[1], norm_bias[1])
    enc_ff, enc_hidden, enc_active = feed_forward(
        normed_b, ff_in[0], ff_in_bias[0], ff_out[0], ff_out_bias[0]
    )
    memory = (after_attn + enc_ff).astype(jnp.bfloat16)
    cross_weight = attn_in[2, :, width:]
    cross_bias = attn_in_bias[2, width:]
    local_cross = matmul(memory, cross_weight)
    cross_keys = local_cross[None, :, :width].astype(jnp.bfloat16)
    cross_values = (local_cross[None, :, width:] + cross_bias).astype(jnp.bfloat16)
    ids_flat = token_ids[0].reshape(dec_rows)
    dec_input = embed[ids_flat].astype(jnp.float32) * math.sqrt(width)
    places = jnp.arange(text_len)
    text_valid = places[None, :] < tok_len[0][:, None]
    self_mask = (places[:, None] >= places[None, :])[None] & text_valid[:, None, :]
    normed_c, pull_c = norm_forward(dec_input, norm_gain[2], norm_bias[2])
    projected_c = matmul(normed_c, attn_in[1])
    self_queries = (
        (projected_c[:, :width] + attn_in_bias[1, :width])
        .astype(jnp.bfloat16)
        .reshape(per_device, text_len, width)
    )
    self_keys = (
        projected_c[:, width : 2 * width].astype(jnp.bfloat16).reshape(per_device, text_len, width)
    )
    self_values = (
        (projected_c[:, 2 * width :] + attn_in_bias[1, width:])
        .astype(jnp.bfloat16)
        .reshape(per_device, text_len, width)
    )
    self_context, self_total = attention_forward(self_queries, self_keys, self_values, self_mask)
    self_context = self_context.reshape(dec_rows, width)
    after_self = dec_input + matmul(self_context, attn_out[1]) + attn_out_bias[1]
    normed_d, pull_d = norm_forward(after_self, norm_gain[3], norm_bias[3])
    cross_queries = (
        (matmul(normed_d, attn_in[2, :, :width]) + attn_in_bias[2, :width])
        .astype(jnp.bfloat16)
        .reshape(per_device, text_len, width)
    )
    cross_context, cross_total = attention_forward(
        cross_queries, cross_keys, cross_values, cross_mask
    )
    cross_context = cross_context.reshape(dec_rows, width)
    after_cross = after_self + matmul(cross_context, attn_out[2]) + attn_out_bias[2]
    normed_e, pull_e = norm_forward(after_cross, norm_gain[4], norm_bias[4])
    dec_ff, dec_hidden, dec_active = feed_forward(
        normed_e, ff_in[1], ff_in_bias[1], ff_out[1], ff_out_bias[1]
    )
    row_valid = text_valid.reshape(dec_rows, 1)
    dec_out = (
        jnp.where(row_valid, after_cross + dec_ff, 0.0)
        .astype(jnp.bfloat16)
        .reshape(1, per_device, text_len, width)
    )
    grad_state = jnp.where(
        row_valid, cotangent[0].reshape(dec_rows, width).astype(jnp.float32), 0.0
    )
    grad_normed, dec_w_first, dec_b_first, dec_w_second, dec_b_second = feed_backward(
        normed_e, dec_hidden, dec_active, ff_in[1], ff_out[1], grad_state
    )
    grad_x, gain_e, shift_e = pull_e(grad_normed)
    grad_state = grad_state + grad_x
    grad_context, cross_out_w, cross_out_b = branch_backward(cross_context, attn_out[2], grad_state)
    grad_q, grad_k, grad_v = attention_backward(
        cross_queries,
        cross_keys,
        cross_values,
        cross_mask,
        cross_total,
        grad_context.reshape(per_device, text_len, width),
    )
    grad_q_rows = grad_q.reshape(dec_rows, width).astype(jnp.bfloat16)
    grad_pairs = jnp.concatenate([grad_k, grad_v], axis=2).astype(jnp.bfloat16)
    cross_in_b = jnp.concatenate(
        [column_sum(grad_q_rows), column_sum(grad_pairs[:, :, width:].reshape(-1, width))]
    )
    cross_w_query = rows_product(normed_d, grad_q_rows)
    grad_x, gain_d, shift_d = pull_d(cols_product(grad_q_rows, attn_in[2, :, :width]))
    grad_state = grad_state + grad_x
    returned = grad_pairs.reshape(enc_rows, 2 * width)
    cross_w_pairs = rows_product(memory, returned)
    grad_memory = cols_product(returned, cross_weight).astype(jnp.bfloat16)
    cross_in_w = jnp.concatenate([cross_w_query, cross_w_pairs], axis=1)
    grad_context, self_out_w, self_out_b = branch_backward(self_context, attn_out[1], grad_state)
    grad_q, grad_k, grad_v = attention_backward(
        self_queries,
        self_keys,
        self_values,
        self_mask,
        self_total,
        grad_context.reshape(per_device, text_len, width),
    )
    grad_triple = (
        jnp.concatenate([grad_q, grad_k, grad_v], axis=2)
        .reshape(dec_rows, 3 * width)
        .astype(jnp.bfloat16)
    )
    self_in_b = jnp.concatenate(
        [column_sum(grad_triple[:, :width]), column_sum(grad_triple[:, 2 * width :])]
    )
    self_in_w = rows_product(normed_c, grad_triple)
    grad_x, gain_c, shift_c = pull_c(cols_product(grad_triple, attn_in[1]))
    grad_state = grad_state + grad_x
    embed_grad = jax.ops.segment_sum(
        grad_state * math.sqrt(width), ids_flat, num_segments=embed.shape[0]
    )
    dec_norms = jnp.stack([gain_c, gain_d, gain_e, shift_c, shift_d, shift_e])
    dec_out_w = jnp.stack([self_out_w, cross_out_w])
    dec_out_b = jnp.stack([self_out_b, cross_out_b])
    grad_enc = grad_memory.astype(jnp.float32)
    grad_normed, enc_w_first, enc_b_first, enc_w_second, enc_b_second = feed_backward(
        normed_b, enc_hidden, enc_active, ff_in[0], ff_out[0], grad_enc
    )
    grad_x, gain_b, shift_b = pull_b(grad_normed)
    grad_enc = grad_enc + grad_x
    grad_context, enc_out_w, enc_out_b = branch_backward(enc_context, attn_out[0], grad_enc)
    grad_q, grad_k, grad_v = attention_backward(
        enc_queries,
        all_keys,
        all_values,
        enc_mask,
        enc_total,
        grad_context.reshape(1, enc_rows, width),
    )
    grad_triple = jnp.concatenate(
        [grad_q[0], grad_k[0], grad_v[0]], axis=1
    ).astype(jnp.bfloat16)
    enc_in_b = jnp.stack(
        [
            jnp.concatenate(
                [column_sum(grad_triple[:, :width]), column_sum(grad_triple[:, 2 * width :])]
            ),
            cross_in_b,
        ]
    )
    enc_in_w = rows_product(normed_a, grad_triple)
    grad_x, gain_a, shift_a = pull_a(cols_product(grad_triple, attn_in[0]))
    grad_enc = grad_enc + grad_x
    frames_grad = lax.all_to_all(
        grad_enc.astype(jnp.bfloat16).reshape(utterances, local_len, width),
        "frame",
        split_axis=0,
        concat_axis=0,
        tiled=True,
    ).astype(jnp.float32)[None]
    gains = jnp.stack([gain_a, gain_b, gain_c, gain_d, gain_e])
    shifts = jnp.stack([shift_a, shift_b, shift_c, shift_d, shift_e])
    in_b = jnp.stack([enc_in_b[0], self_in_b, enc_in_b[1]])
    out_b = jnp.stack([enc_out_b, self_out_b, cross_out_b])
    first_b = jnp.stack([enc_b_first, dec_b_first])
    second_b = jnp.stack([enc_b_second, dec_b_second])
    smalls = (gains, shifts, in_b, out_b, first_b, second_b)
    small = jnp.concatenate([item.reshape(-1, width) for item in smalls])
    large = (
        embed_grad, enc_in_w, self_in_w, cross_in_w, enc_out_w, self_out_w, cross_out_w,
        enc_w_first, dec_w_first, enc_w_second, dec_w_second,
    )
    low = tuple(item.astype(jnp.bfloat16) for item in large)
    low = (jnp.concatenate([low[0], small.astype(jnp.bfloat16)]),) + low[1:]
    summed = lax.psum(low, ("frame", "batch"))
    count_step = step[0].astype(jnp.float32)
    rate = jnp.minimum(lax.rsqrt(count_step), count_step * WARMUP ** (-1.5)) * WARMUP**0.5
    full = tuple(item.astype(jnp.float32) * rate for item in summed)
    small = full[0][embed.shape[0] :]
    pieces = []
    start = 0
    for item in smalls:
        rows = item.size // width
        pieces.append(small[start : start + rows].reshape(item.shape))
        start += rows
    return (
        dec_out,
        frames_grad,
        full[0][: embed.shape[0]],
        pieces[0],
        pieces[1],
        jnp.stack(full[1:4]),
        pieces[2],
        jnp.stack(full[4:7]),
        pieces[3],
        jnp.stack(full[7:9]),
        pieces[4],
        jnp.stack(full[9:11]),
        pieces[5],
    )


def solution(mesh):
    placed = (
        P("batch", None, "frame", None),
        P("batch", None),
        P("batch", "frame", None),
        P("batch", "frame"),
        P(),
        P(),
        P(),
        P(),
        P(),
        P(),
        P(),
        P(),
        P(),
        P(),
        P(),
        P(),
        P("batch", "frame", None, None),
    )
    return jax.shard_map(
        body,
        mesh=mesh,
        in_specs=placed,
        out_specs=(
            P("batch", "frame", None, None),
            P("batch", None, "frame", None),
            P(),
            P(),
            P(),
            P(),
            P(),
            P(),
            P(),
            P(),
            P(),
            P(),
            P(),
        ),
        check_vma=False,
    )
```

```python
import functools
import math

import jax
import jax.numpy as jnp
from jax import lax
from jax.experimental import pallas as pl
from jax.experimental.pallas import tpu as pltpu
from jax.sharding import PartitionSpec as P

HEADS = 4
HEAD_DIM = 64
WARMUP = 25000
EPSILON = 1e-05
MASKED = -1e30
BF = jnp.bfloat16
F32 = jnp.float32
GELU_A = math.sqrt(2.0 / math.pi)
GELU_B = GELU_A * 0.044715
VMEM_LIMIT = 56 * 1024 * 1024


def nn(left, right):
    return lax.dot_general(left, right, (((1,), (0,)), ((), ())), preferred_element_type=F32)


def nt(left, right):
    return lax.dot_general(left, right, (((1,), (1,)), ((), ())), preferred_element_type=F32)


def normalise(states):
    average = jnp.mean(states, axis=-1, keepdims=True)
    centred = states - average
    scale = lax.rsqrt(jnp.mean(centred * centred, axis=-1, keepdims=True) + EPSILON)
    return centred * scale, scale


def norm_backward(grad, unit, scale, gain):
    grad_unit = grad * gain
    mean_grad = jnp.mean(grad_unit, axis=-1, keepdims=True)
    mean_along = jnp.mean(grad_unit * unit, axis=-1, keepdims=True)
    grad_states = scale * (grad_unit - mean_grad - unit * mean_along)
    return grad_states, col_sum(grad * unit), col_sum(grad)


def col_sum(matrix):
    return jnp.sum(matrix.astype(F32), axis=0, keepdims=True)


def gelu_value(hidden):
    inner = hidden * (GELU_A + GELU_B * (hidden * hidden))
    return hidden * (0.5 + 0.5 * jnp.tanh(inner))


def gelu_both(hidden):
    square = hidden * hidden
    bent = jnp.tanh(hidden * (GELU_A + GELU_B * square))
    half = 0.5 + 0.5 * bent
    slope = half + (0.5 * hidden) * (1.0 - bent * bent) * (GELU_A + 3.0 * GELU_B * square)
    return hidden * half, slope


def lanes_of(head):
    return slice(128 * (head // 2), 128 * (head // 2) + 128)


def rows_of(head):
    return slice(HEAD_DIM * head, HEAD_DIM * head + HEAD_DIM)


def own_lanes(pair, head):
    lane = lax.broadcasted_iota(jnp.int32, pair.shape, 1)
    mine = (lane < HEAD_DIM) if head % 2 == 0 else (lane >= HEAD_DIM)
    return jnp.where(mine, pair, jnp.zeros_like(pair))


def spare_lane(head):
    return HEAD_DIM if head % 2 == 0 else 0


def with_one(query, head):
    lane = lax.broadcasted_iota(jnp.int32, query.shape, 1)
    return jnp.where(lane == spare_lane(head), jnp.ones_like(query), query)


def with_mask(key_pair, head, length):
    lane = lax.broadcasted_iota(jnp.int32, key_pair.shape, 1)
    row = lax.broadcasted_iota(jnp.int32, key_pair.shape, 0)
    bias = jnp.where(row < length, 0.0, MASKED).astype(BF)
    return jnp.where(lane == spare_lane(head), bias, key_pair)


def layer_spec(array, layer):
    shape = (None,) + array.shape[1:]
    return pl.BlockSpec(shape, lambda i: (layer,) + (0,) * (len(shape) - 1), pipeline_mode=pl.Buffered(1))


def whole_spec(shape):
    return pl.BlockSpec(shape, lambda i: (0,) * len(shape), pipeline_mode=pl.Buffered(1))


def call(kernel, outs, args, scalars=(), scratch=(), flops=0):
    in_specs = [pl.BlockSpec(memory_space=pltpu.SMEM) for _ in scalars]
    in_specs += [layer_spec(*a) if isinstance(a, tuple) else whole_spec(a.shape) for a in args]
    args = [a[0] if isinstance(a, tuple) else a for a in args]
    size = sum(a.size * a.dtype.itemsize for a in args)
    size += sum(math.prod(s) * jnp.dtype(d).itemsize for s, d in outs)
    return pl.pallas_call(
        kernel,
        grid=(1,),
        out_shape=[jax.ShapeDtypeStruct(shape, dtype) for shape, dtype in outs],
        in_specs=in_specs,
        out_specs=[whole_spec(shape) for shape, _ in outs],
        scratch_shapes=list(scratch),
        compiler_params=pltpu.CompilerParams(vmem_limit_bytes=VMEM_LIMIT),
        cost_estimate=pl.CostEstimate(flops=flops, bytes_accessed=size, transcendentals=0),
        name=kernel.__name__,
    )(*scalars, *args)


def decoder_start(
    tok_ref, emb_ref, gain_ref, shift_ref, in_ref, in_b_ref, out_ref, out_b_ref, cross_ref,
    y1_ref, norm_c_ref, qkv_ref, ctx_t_ref, prob_ref, norm_d_ref, cross_q_ref,
):
    text = emb_ref.shape[0]
    width = emb_ref.shape[1]
    start = emb_ref[...].astype(F32) * math.sqrt(width)
    unit, _ = normalise(start)
    norm_c = (unit * gain_ref[2:3] + shift_ref[2:3]).astype(BF)
    norm_c_ref[...] = norm_c
    flat = nn(norm_c, in_ref[...])
    query = (flat[:, :width] + in_b_ref[1:2, :width]).astype(BF)
    key = flat[:, width : 2 * width].astype(BF)
    value = (flat[:, 2 * width :] + in_b_ref[1:2, width:]).astype(BF)
    qkv_ref[:, :width] = query
    qkv_ref[:, width : 2 * width] = key
    qkv_ref[:, 2 * width :] = value
    value_t = value.astype(F32).T.astype(BF)
    key_at = lax.broadcasted_iota(jnp.int32, (text, text), 0)
    query_at = lax.broadcasted_iota(jnp.int32, (text, text), 1)
    seen = jnp.logical_and(key_at <= query_at, key_at < tok_ref[0])
    scaled = query * jnp.asarray(HEAD_DIM**-0.5, BF)
    parts = []
    for head in range(HEADS):
        lanes = lanes_of(head)
        score = nt(key[:, lanes], own_lanes(scaled[:, lanes], head))
        score = jnp.where(seen, score, MASKED)
        weight = jnp.exp(score - jnp.max(score, axis=0, keepdims=True))
        prob = weight / jnp.sum(weight, axis=0, keepdims=True)
        prob_ref[head] = prob
        parts.append(nn(value_t[rows_of(head)], prob.astype(BF)))
    ctx_t = jnp.concatenate(parts, axis=0)
    ctx_t_ref[...] = ctx_t.astype(BF)
    y1 = start + nn(ctx_t.T.astype(BF), out_ref[...]) + out_b_ref[1:2]
    y1_ref[...] = y1
    unit, _ = normalise(y1)
    norm_d = (unit * gain_ref[3:4] + shift_ref[3:4]).astype(BF)
    norm_d_ref[...] = norm_d
    cross_q_ref[...] = (nn(norm_d, cross_ref[:, :width]) + in_b_ref[2:3, :width]).astype(BF)


def encoder_forward(
    len_ref, x_ref, gain_ref, shift_ref, in_ref, in_b_ref, out_ref, out_b_ref,
    w1_ref, b1_ref, w2_ref, b2_ref, cin_ref,
    qkv_ref, ctx_t_ref, lse_ref, h1_ref, mem_ref, cross_ref,
    key_aug, value_t, act,
):
    rows, width = x_ref.shape
    unit, _ = normalise(x_ref[...].astype(F32))
    norm_a = (unit * gain_ref[0:1] + shift_ref[0:1]).astype(BF)
    qkv_ref[:, :width] = (nn(norm_a, in_ref[:, :width]) + in_b_ref[0:1, :width]).astype(BF)
    key = nn(norm_a, in_ref[:, width : 2 * width]).astype(BF)
    qkv_ref[:, width : 2 * width] = key
    value = (nn(norm_a, in_ref[:, 2 * width :]) + in_b_ref[0:1, width:]).astype(BF)
    qkv_ref[:, 2 * width :] = value
    value_t[...] = value.astype(F32).T.astype(BF)
    for head in range(HEADS):
        key_aug[head] = with_mask(key[:, lanes_of(head)], head, len_ref[0])
    step = 256

    def block(index, carry):
        at = pl.multiple_of(index * step, step)
        for head in range(HEADS):
            query = qkv_ref[pl.ds(at, step), lanes_of(head)] * jnp.asarray(HEAD_DIM**-0.5, BF)
            query = with_one(own_lanes(query, head), head)
            score = nt(key_aug[head], query)
            highest = jnp.max(score, axis=0, keepdims=True)
            weight = jnp.exp(score - highest)
            total = jnp.sum(weight, axis=0, keepdims=True)
            context = nn(value_t[rows_of(head)], weight.astype(BF)) * (1.0 / total)
            ctx_t_ref[rows_of(head), pl.ds(at, step)] = context.astype(BF)
            lse_ref[head : head + 1, pl.ds(at, step)] = highest + jnp.log(total)
        return carry

    lax.fori_loop(0, rows // step, block, 0)
    context = ctx_t_ref[...].astype(F32).T.astype(BF)
    h1 = x_ref[...].astype(F32) + nn(context, out_ref[...]) + out_b_ref[0:1]
    h1_ref[...] = h1
    unit, _ = normalise(h1)
    norm_b = (unit * gain_ref[1:2] + shift_ref[1:2]).astype(BF)

    def hidden_block(index, carry):
        at = pl.multiple_of(index * step, step)
        hidden = nn(norm_b, w1_ref[:, pl.ds(at, step)]) + b1_ref[0:1, pl.ds(at, step)]
        act[:, pl.ds(at, step)] = gelu_value(hidden).astype(BF)
        return carry

    lax.fori_loop(0, w1_ref.shape[1] // step, hidden_block, 0)
    memory = (h1_ref[...] + nn(act[...], w2_ref[...]) + b2_ref[0:1]).astype(BF)
    mem_ref[...] = memory
    cross_ref[:, :width] = nn(memory, cin_ref[:, width : 2 * width]).astype(BF)
    cross_ref[:, width:] = (nn(memory, cin_ref[:, 2 * width :]) + in_b_ref[2:3, width:]).astype(BF)


def decoder_main(
    tok_ref, len_ref,
    emb_ref, y1_ref, norm_c_ref, qkv_ref, ctx_t_ref, prob_ref, norm_d_ref, cross_q_ref,
    cross_ref, mem_ref, cot_ref, gain_ref, shift_ref,
    in1_ref, out1_ref, in2_ref, out2_ref, out_b_ref, w1_ref, b1_ref, w2_ref, b2_ref,
    dec_ref, dmem_ref, y0_ref, din1_ref, din2_ref, dout1_ref, dout2_ref, dw1_ref, dw2_ref,
    small_ref, db1_ref,
    probs,
):
    text, width = emb_ref.shape
    small_ref[...] = jnp.zeros_like(small_ref)
    scaled = cross_q_ref[...] * jnp.asarray(HEAD_DIM**-0.5, BF)
    value_t = cross_ref[:, width:].astype(F32).T.astype(BF)
    parts = []
    for head in range(HEADS):
        lanes = lanes_of(head)
        key = with_mask(cross_ref[:, lanes], head, len_ref[0])
        score = nt(key, with_one(own_lanes(scaled[:, lanes], head), head))
        weight = jnp.exp(score - jnp.max(score, axis=0, keepdims=True))
        prob = weight * (1.0 / jnp.sum(weight, axis=0, keepdims=True))
        probs[head] = prob
        parts.append(nn(value_t[rows_of(head)], prob.astype(BF)))
    cross_t = jnp.concatenate(parts, axis=0)
    y2 = y1_ref[...] + nn(cross_t.T.astype(BF), out2_ref[...]) + out_b_ref[2:3]
    unit_e, scale_e = normalise(y2)
    norm_e = (unit_e * gain_ref[4:5] + shift_ref[4:5]).astype(BF)
    norm_e_t = norm_e.astype(F32).T.astype(BF)
    valid = lax.broadcasted_iota(jnp.int32, (text, 1), 0) < tok_ref[0]
    grad_low = jnp.where(valid, cot_ref[...], jnp.zeros_like(cot_ref))
    grad = grad_low.astype(F32)
    grad_low_t = grad.T.astype(BF)
    y3 = y2 + b2_ref[1:2]
    grad_norm = jnp.zeros((text, width), F32)
    chunk = 512
    for at in range(0, w1_ref.shape[1], chunk):
        part = slice(at, at + chunk)
        hidden = nn(norm_e, w1_ref[:, part]) + b1_ref[1:2, part]
        value, slope = gelu_both(hidden)
        active = value.astype(BF)
        y3 = y3 + nn(active, w2_ref[part])
        grad_hidden = (nt(grad_low, w2_ref[part]) * slope).astype(BF)
        db1_ref[:, part] = col_sum(grad_hidden)
        dw1_ref[:, part] = nn(norm_e_t, grad_hidden).astype(BF)
        dw2_ref[part] = nn(grad_low_t, active).T.astype(BF)
        grad_norm = grad_norm + nt(grad_hidden, w1_ref[:, part])
    dec_ref[...] = jnp.where(valid, y3, 0.0).astype(BF)
    small_ref[4:5] = col_sum(grad)
    grad_x, small_ref[0:1], small_ref[1:2] = norm_backward(grad_norm, unit_e, scale_e, gain_ref[4:5])
    grad = grad + grad_x
    grad_low = grad.astype(BF)
    small_ref[5:6] = col_sum(grad_low)
    dout2_ref[...] = nn(cross_t.astype(BF), grad_low).astype(BF)
    grad_ctx = nt(grad_low, out2_ref[...]).astype(BF)
    key_t = cross_ref[:, :width].astype(F32).T.astype(BF)
    mem_t = mem_ref[...].astype(F32).T.astype(BF)
    dkeys = []
    dvalues = []
    dquery = []
    for pair in range(HEADS // 2):
        dkey = 0.0
        dvalue = 0.0
        for head in (2 * pair, 2 * pair + 1):
            lanes = lanes_of(head)
            own_grad = own_lanes(grad_ctx[:, lanes], head)
            prob = probs[head]
            dprob = nt(cross_ref[:, slice(width + lanes.start, width + lanes.stop)], own_grad)
            inner = jnp.sum(dprob * prob, axis=0, keepdims=True)
            dscore = (prob * (dprob - inner)).astype(BF)
            dvalue = dvalue + nn(prob.astype(BF), own_grad)
            dkey = dkey + nn(dscore, own_lanes(scaled[:, lanes], head))
            dquery.append(nn(key_t[rows_of(head)], dscore))
        dkeys.append(dkey.astype(BF))
        dvalues.append(dvalue.astype(BF))
    dq_t = jnp.concatenate(dquery, axis=0) * HEAD_DIM**-0.5
    dq = dq_t.T.astype(BF)
    dkv = jnp.concatenate(dkeys + dvalues, axis=1)
    small_ref[6:7] = col_sum(dq)
    small_ref[7:8] = col_sum(dkv[:, width:])
    norm_d = norm_d_ref[...]
    din2_ref[:, :width] = nn(norm_d.astype(F32).T.astype(BF), dq).astype(BF)
    din2_ref[:, width:] = nn(mem_t, dkv).astype(BF)
    dmem_ref[...] = nt(dkv, in2_ref[:, width:]).astype(BF)
    unit, scale = normalise(y1_ref[...])
    grad_x, small_ref[8:9], small_ref[9:10] = norm_backward(
        nt(dq, in2_ref[:, :width]), unit, scale, gain_ref[3:4]
    )
    grad = grad + grad_x
    grad_low = grad.astype(BF)
    small_ref[10:11] = col_sum(grad_low)
    dout1_ref[...] = nn(ctx_t_ref[...], grad_low).astype(BF)
    grad_ctx = nt(grad_low, out1_ref[...]).astype(BF)
    key_t = qkv_ref[:, width : 2 * width].astype(F32).T.astype(BF)
    scaled = qkv_ref[:, :width] * jnp.asarray(HEAD_DIM**-0.5, BF)
    dkeys = []
    dvalues = []
    dquery = []
    for pair in range(HEADS // 2):
        dkey = 0.0
        dvalue = 0.0
        for head in (2 * pair, 2 * pair + 1):
            lanes = lanes_of(head)
            own_grad = own_lanes(grad_ctx[:, lanes], head)
            prob = prob_ref[head]
            dprob = nt(qkv_ref[:, slice(2 * width + lanes.start, 2 * width + lanes.stop)], own_grad)
            inner = jnp.sum(dprob * prob, axis=0, keepdims=True)
            dscore = (prob * (dprob - inner)).astype(BF)
            dvalue = dvalue + nn(prob.astype(BF), own_grad)
            dkey = dkey + nn(dscore, own_lanes(scaled[:, lanes], head))
            dquery.append(nn(key_t[rows_of(head)], dscore))
        dkeys.append(dkey.astype(BF))
        dvalues.append(dvalue.astype(BF))
    dq_t = jnp.concatenate(dquery, axis=0) * HEAD_DIM**-0.5
    dqkv = jnp.concatenate([dq_t.T.astype(BF)] + dkeys + dvalues, axis=1)
    small_ref[11:12] = col_sum(dqkv[:, :width])
    small_ref[12:13] = col_sum(dqkv[:, 2 * width :])
    din1_ref[...] = nn(norm_c_ref[...].astype(F32).T.astype(BF), dqkv).astype(BF)
    unit, scale = normalise(emb_ref[...].astype(F32) * math.sqrt(width))
    grad_x, small_ref[13:14], small_ref[14:15] = norm_backward(
        nt(dqkv, in1_ref[...]), unit, scale, gain_ref[2:3]
    )
    y0_ref[...] = ((grad + grad_x) * math.sqrt(width)).astype(BF)


def embed_backward(ids_ref, grad_ref, attn_ref, feed_ref, dec_ref, db0_ref, db1_ref, out_ref):
    text = ids_ref.shape[1]
    small = (attn_ref, feed_ref, dec_ref, db0_ref, db1_ref)
    table = out_ref.shape[0] - sum(ref.shape[0] for ref in small)
    chunk = table // 4
    for at in range(0, table, chunk):
        row = lax.broadcasted_iota(jnp.int32, (chunk, text), 0) + at
        hot = jnp.where(row == ids_ref[...], 1.0, 0.0).astype(BF)
        out_ref[at : at + chunk] = nn(hot, grad_ref[...]).astype(BF)
    out_ref[table:] = jnp.concatenate([ref[...] for ref in small], axis=0).astype(BF)


def encoder_feed_backward(
    h1_ref, dmem_ref, ctx_t_ref, gain_ref, shift_ref, w1_ref, b1_ref, w2_ref, out_ref,
    dh1_ref, dctx_ref, dw1_ref, dw2_ref, dout_ref, small_ref, db1_ref,
    grad_hid,
):
    small_ref[...] = jnp.zeros_like(small_ref)
    unit, _ = normalise(h1_ref[...])
    norm_b = unit * gain_ref[1:2] + shift_ref[1:2]
    norm_b_t = norm_b.T.astype(BF)
    norm_b = norm_b.astype(BF)
    grad_low = dmem_ref[...]
    grad_low_t = grad_low.astype(F32).T.astype(BF)
    step = 256

    def block(index, carry):
        part = pl.ds(pl.multiple_of(index * step, step), step)
        hidden = nn(norm_b, w1_ref[:, part]) + b1_ref[0:1, part]
        value, slope = gelu_both(hidden)
        grad_hidden = (nt(grad_low, w2_ref[part]) * slope).astype(BF)
        grad_hid[:, part] = grad_hidden
        db1_ref[:, part] = col_sum(grad_hidden)
        dw1_ref[:, part] = nn(norm_b_t, grad_hidden).astype(BF)
        dw2_ref[part] = nn(grad_low_t, value.astype(BF)).T.astype(BF)
        return carry

    lax.fori_loop(0, w1_ref.shape[1] // step, block, 0)
    grad = grad_low.astype(F32)
    small_ref[2:3] = col_sum(grad)
    unit, scale = normalise(h1_ref[...])
    grad_x, small_ref[0:1], small_ref[1:2] = norm_backward(
        nt(grad_hid[...], w1_ref[...]), unit, scale, gain_ref[1:2]
    )
    grad = grad + grad_x
    dh1_ref[...] = grad
    grad_low = grad.astype(BF)
    small_ref[3:4] = col_sum(grad_low)
    dout_ref[...] = nn(ctx_t_ref[...], grad_low).astype(BF)
    dctx_ref[...] = nt(grad_low, out_ref[...]).astype(BF)


def encoder_attention_backward(
    len_ref, x_ref, qkv_ref, lse_ref, dctx_ref, dh1_ref, gain_ref, shift_ref, in_ref,
    dx_ref, din_ref, small_ref,
    key_aug, key_t, dkv, dq_t, dqkv,
):
    rows, width = x_ref.shape
    small_ref[...] = jnp.zeros_like(small_ref)
    for head in range(HEADS):
        lanes = lanes_of(head)
        key_aug[head] = with_mask(qkv_ref[:, slice(width + lanes.start, width + lanes.stop)], head, len_ref[0])
    key_t[...] = qkv_ref[:, width : 2 * width].astype(F32).T.astype(BF)
    dkv[...] = jnp.zeros_like(dkv)
    step = 256

    def block(index, carry):
        at = pl.multiple_of(index * step, step)
        for head in range(HEADS):
            lanes = lanes_of(head)
            query = own_lanes(qkv_ref[pl.ds(at, step), lanes] * jnp.asarray(HEAD_DIM**-0.5, BF), head)
            score = nt(key_aug[head], with_one(query, head))
            prob = jnp.exp(score - lse_ref[head : head + 1, pl.ds(at, step)])
            own_grad = own_lanes(dctx_ref[pl.ds(at, step), lanes], head)
            dprob = nt(qkv_ref[:, slice(2 * width + lanes.start, 2 * width + lanes.stop)], own_grad)
            inner = jnp.sum(dprob * prob, axis=0, keepdims=True)
            dscore = (prob * (dprob - inner)).astype(BF)
            dkv[:, lanes] += nn(dscore, query)
            dkv[:, slice(width + lanes.start, width + lanes.stop)] += nn(prob.astype(BF), own_grad)
            dq_t[rows_of(head), pl.ds(at, step)] = nn(key_t[rows_of(head)], dscore)
        return carry

    lax.fori_loop(0, rows // step, block, 0)
    dqkv[:, :width] = (dq_t[...].T * HEAD_DIM**-0.5).astype(BF)
    dqkv[:, width:] = dkv[...].astype(BF)
    small_ref[2:3] = col_sum(dqkv[:, :width])
    small_ref[3:4] = col_sum(dqkv[:, 2 * width :])
    unit, scale = normalise(x_ref[...].astype(F32))
    norm_a = unit * gain_ref[0:1] + shift_ref[0:1]
    din_ref[...] = nn(norm_a.T.astype(BF), dqkv[...]).astype(BF)
    grad_x, small_ref[0:1], small_ref[1:2] = norm_backward(
        nt(dqkv[...], in_ref[...]), unit, scale, gain_ref[0:1]
    )
    dx_ref[...] = (dh1_ref[...] + grad_x).astype(BF)


def body(
    frames, utt_len, token_ids, tok_len, step, embed, norm_gain, norm_bias, attn_in, attn_in_bias,
    attn_out, attn_out_bias, ff_in, ff_in_bias, ff_out, ff_out_bias, cotangent,
):
    width = embed.shape[1]
    hidden = ff_in.shape[2]
    frame_count = lax.axis_size("frame")
    local_len = frames.shape[2]
    rows = local_len * frame_count
    text = token_ids.shape[2]
    my_len = lax.dynamic_slice_in_dim(utt_len[0], lax.axis_index("frame"), 1)
    my_tok = tok_len[0]
    arrived = lax.all_to_all(frames[0], "frame", split_axis=0, concat_axis=1, tiled=True)
    source = arrived.reshape(rows, width)
    ids = token_ids[0, 0]
    rows_in = embed[ids]

    y1, norm_c, dec_qkv, dec_ctx_t, dec_prob, norm_d, cross_q = call(
        decoder_start,
        [
            ((text, width), F32), ((text, width), BF), ((text, 3 * width), BF), ((width, text), BF),
            ((HEADS, text, text), F32), ((text, width), BF), ((text, width), BF),
        ],
        [
            rows_in, norm_gain, norm_bias, (attn_in, 1), attn_in_bias, (attn_out, 1),
            attn_out_bias, (attn_in, 2),
        ],
        [my_tok],
        flops=2 * text * width * width * 5,
    )
    enc_qkv, enc_ctx_t, lse, h1, memory, cross_kv = call(
        encoder_forward,
        [
            ((rows, 3 * width), BF), ((width, rows), BF), ((8, rows), F32), ((rows, width), F32),
            ((rows, width), BF), ((rows, 2 * width), BF),
        ],
        [
            source, norm_gain, norm_bias, (attn_in, 0), attn_in_bias, (attn_out, 0),
            attn_out_bias, (ff_in, 0), ff_in_bias, (ff_out, 0), ff_out_bias, (attn_in, 2),
        ],
        [my_len],
        [
            pltpu.VMEM((HEADS, rows, 128), BF), pltpu.VMEM((width, rows), BF),
            pltpu.VMEM((rows, hidden), BF),
        ],
        flops=2 * rows * width * (6 * width + 2 * rows + 2 * hidden),
    )
    (
        dec_out, dmem, y0_grad, din1, din2, dout1, dout2, dec_dw1, dec_dw2, dec_small, dec_db1,
    ) = call(
        decoder_main,
        [
            ((text, width), BF), ((rows, width), BF), ((text, width), BF),
            ((width, 3 * width), BF), ((width, 3 * width), BF), ((width, width), BF),
            ((width, width), BF), ((width, hidden), BF), ((hidden, width), BF),
            ((16, width), F32), ((1, hidden), F32),
        ],
        [
            rows_in, y1, norm_c, dec_qkv, dec_ctx_t, dec_prob, norm_d, cross_q, cross_kv, memory,
            cotangent[0, 0], norm_gain, norm_bias, (attn_in, 1), (attn_out, 1), (attn_in, 2),
            (attn_out, 2), attn_out_bias, (ff_in, 1), ff_in_bias, (ff_out, 1), ff_out_bias,
        ],
        [my_tok, my_len],
        [pltpu.VMEM((HEADS, rows, text), F32)],
        flops=2 * text * width * (6 * hidden + 7 * rows + 16 * width) + 2 * rows * width * 4 * width,
    )
    dh1, dctx, enc_dw1, enc_dw2, dout0, feed_small, enc_db1 = call(
        encoder_feed_backward,
        [
            ((rows, width), F32), ((rows, width), BF), ((width, hidden), BF), ((hidden, width), BF),
            ((width, width), BF), ((8, width), F32), ((1, hidden), F32),
        ],
        [
            h1, dmem, enc_ctx_t, norm_gain, norm_bias, (ff_in, 0), ff_in_bias, (ff_out, 0),
            (attn_out, 0),
        ],
        scratch=[pltpu.VMEM((rows, hidden), BF)],
        flops=2 * rows * width * (5 * hidden + 2 * width),
    )
    dx, din0, attn_small = call(
        encoder_attention_backward,
        [((rows, width), BF), ((width, 3 * width), BF), ((8, width), F32)],
        [source, enc_qkv, lse, dctx, dh1, norm_gain, norm_bias, (attn_in, 0)],
        [my_len],
        [
            pltpu.VMEM((HEADS, rows, 128), BF), pltpu.VMEM((width, rows), BF),
            pltpu.VMEM((rows, 2 * width), F32), pltpu.VMEM((width, rows), F32),
            pltpu.VMEM((rows, 3 * width), BF),
        ],
        flops=2 * rows * width * (5 * rows + 6 * width),
    )
    vocab = embed.shape[0]
    table = -(-vocab // 64) * 64
    (table_grad,) = call(
        embed_backward,
        [((table + 48, width), BF)],
        [
            ids[None], y0_grad, attn_small, feed_small, dec_small,
            enc_db1.reshape(-1, width), dec_db1.reshape(-1, width),
        ],
        flops=2 * table * width * text,
    )
    frames_grad = lax.all_to_all(
        dx.reshape(frame_count, local_len, width), "frame", split_axis=0, concat_axis=0, tiled=True
    ).astype(F32)[None]
    low = (table_grad, din0, din1, din2, dout0, dout1, dout2, enc_dw1, dec_dw1, enc_dw2, dec_dw2)
    summed = lax.psum(low, ("frame", "batch"))
    count_step = step[0].astype(F32)
    rate = jnp.minimum(lax.rsqrt(count_step), count_step * WARMUP ** (-1.5)) * WARMUP**0.5
    full = tuple(item.astype(F32) * rate for item in summed)
    small = full[0][table:]
    pick = lambda *at: jnp.concatenate([small[i : i + 1] for i in at])
    return (
        dec_out[None, None],
        frames_grad,
        full[0][:vocab],
        pick(0, 8, 29, 24, 16),
        pick(1, 9, 30, 25, 17),
        jnp.stack(full[1:4]),
        pick(2, 3, 27, 28, 22, 23).reshape(3, 2 * width),
        jnp.stack(full[4:7]),
        pick(11, 26, 21),
        jnp.stack(full[7:9]),
        small[32:].reshape(2, hidden),
        jnp.stack(full[9:11]),
        pick(10, 20),
    )


def solution(mesh):
    placed = (
        P("batch", None, "frame", None),
        P("batch", None),
        P("batch", "frame", None),
        P("batch", "frame"),
        P(),
        P(),
        P(),
        P(),
        P(),
        P(),
        P(),
        P(),
        P(),
        P(),
        P(),
        P(),
        P("batch", "frame", None, None),
    )
    return jax.shard_map(
        body,
        mesh=mesh,
        in_specs=placed,
        out_specs=(
            P("batch", "frame", None, None),
            P("batch", None, "frame", None),
            P(),
            P(),
            P(),
            P(),
            P(),
            P(),
            P(),
            P(),
            P(),
            P(),
            P(),
        ),
        check_vma=False,
    )
```

```python
import functools
import math

import jax
import jax.numpy as jnp
from jax import lax
from jax.experimental import pallas as pl
from jax.experimental.pallas import tpu as pltpu
from jax.sharding import Mesh, PartitionSpec as P

HEADS = 4
HEAD_DIM = 64
WARMUP = 25000
EPSILON = 1e-05
MASKED = -1e30
BF = jnp.bfloat16
F32 = jnp.float32
GELU_A = math.sqrt(2.0 / math.pi)
GELU_B = GELU_A * 0.044715
VMEM_LIMIT = 56 * 1024 * 1024
SMALL = 32
SPILL = 64


def nn(left, right):
    return lax.dot_general(left, right, (((1,), (0,)), ((), ())), preferred_element_type=F32)


def nt(left, right):
    return lax.dot_general(left, right, (((1,), (1,)), ((), ())), preferred_element_type=F32)


def normalise(states):
    average = jnp.mean(states, axis=-1, keepdims=True)
    centred = states - average
    scale = lax.rsqrt(jnp.mean(centred * centred, axis=-1, keepdims=True) + EPSILON)
    return centred * scale, scale


def norm_backward(grad, unit, scale, gain):
    grad_unit = grad * gain
    mean_grad = jnp.mean(grad_unit, axis=-1, keepdims=True)
    mean_along = jnp.mean(grad_unit * unit, axis=-1, keepdims=True)
    grad_states = scale * (grad_unit - mean_grad - unit * mean_along)
    return grad_states, col_sum(grad * unit), col_sum(grad)


def col_sum(matrix):
    return jnp.sum(matrix.astype(F32), axis=0, keepdims=True)


def gelu_value(hidden):
    inner = hidden * (GELU_A + GELU_B * (hidden * hidden))
    return hidden * (0.5 + 0.5 * jnp.tanh(inner))


def gelu_both(hidden):
    square = hidden * hidden
    bent = jnp.tanh(hidden * (GELU_A + GELU_B * square))
    half = 0.5 + 0.5 * bent
    slope = half + (0.5 * hidden) * (1.0 - bent * bent) * (GELU_A + 3.0 * GELU_B * square)
    return hidden * half, slope


def lanes_of(head):
    return slice(128 * (head // 2), 128 * (head // 2) + 128)


def rows_of(head):
    return slice(HEAD_DIM * head, HEAD_DIM * head + HEAD_DIM)


def own_lanes(pair, head):
    lane = lax.broadcasted_iota(jnp.int32, pair.shape, 1)
    mine = (lane < HEAD_DIM) if head % 2 == 0 else (lane >= HEAD_DIM)
    return jnp.where(mine, pair, jnp.zeros_like(pair))


def spare_lane(head):
    return HEAD_DIM if head % 2 == 0 else 0


def with_one(query, head):
    lane = lax.broadcasted_iota(jnp.int32, query.shape, 1)
    return jnp.where(lane == spare_lane(head), jnp.ones_like(query), query)


def with_mask(key_pair, head, length):
    lane = lax.broadcasted_iota(jnp.int32, key_pair.shape, 1)
    row = lax.broadcasted_iota(jnp.int32, key_pair.shape, 0)
    bias = jnp.where(row < length, 0.0, MASKED).astype(BF)
    return jnp.where(lane == spare_lane(head), bias, key_pair)


def part_spec(shape, layers, at):
    zeros = (0,) * (len(shape) - 1)
    pick = (lambda i, *s: (s[at[0]][0],) + zeros) if isinstance(at, list) else (lambda i, *s: (at,) + zeros)
    return pl.BlockSpec((layers,) + shape[1:], pick, pipeline_mode=pl.Buffered(1))


def call(kernel, outs, args, scalars=(), scratch=(), flops=0, aliases=None):
    in_specs = []
    for a in args:
        if isinstance(a, tuple) and a[1] is None:
            in_specs.append(pl.BlockSpec(memory_space=pl.ANY))
        elif isinstance(a, tuple):
            in_specs.append(part_spec(a[0].shape, None, a[1]))
        else:
            in_specs.append(part_spec(a.shape, a.shape[0], 0))
    args = [a[0] if isinstance(a, tuple) else a for a in args]
    out_specs = [part_spec(out[0], *(out[2:] or (out[0][0], 0))) for out in outs]
    size = sum(a.size * a.dtype.itemsize for a in args)
    size += sum(math.prod(out[0]) * jnp.dtype(out[1]).itemsize for out in outs)
    return pl.pallas_call(
        kernel,
        grid_spec=pltpu.PrefetchScalarGridSpec(
            num_scalar_prefetch=len(scalars),
            grid=(1,),
            in_specs=in_specs,
            out_specs=out_specs,
            scratch_shapes=list(scratch),
        ),
        out_shape=[jax.ShapeDtypeStruct(out[0], out[1]) for out in outs],
        input_output_aliases=aliases or {},
        compiler_params=pltpu.CompilerParams(vmem_limit_bytes=VMEM_LIMIT),
        cost_estimate=pl.CostEstimate(flops=flops, bytes_accessed=size, transcendentals=0),
        name=kernel.__name__,
    )(*scalars, *args)


def decoder_start(
    tok_ref, emb_ref, gain_ref, shift_ref, in_ref, in_b_ref, out_ref, out_b_ref, cross_ref,
    y1_ref, norm_c_ref, qkv_ref, ctx_t_ref, prob_ref, norm_d_ref, cross_q_ref,
):
    text = emb_ref.shape[0]
    width = emb_ref.shape[1]
    start = emb_ref[...].astype(F32) * math.sqrt(width)
    unit, _ = normalise(start)
    norm_c = (unit * gain_ref[2:3] + shift_ref[2:3]).astype(BF)
    norm_c_ref[...] = norm_c
    flat = nn(norm_c, in_ref[...])
    query = (flat[:, :width] + in_b_ref[1:2, :width]).astype(BF)
    key = flat[:, width : 2 * width].astype(BF)
    value = (flat[:, 2 * width :] + in_b_ref[1:2, width:]).astype(BF)
    qkv_ref[:, :width] = query
    qkv_ref[:, width : 2 * width] = key
    qkv_ref[:, 2 * width :] = value
    value_t = value.astype(F32).T.astype(BF)
    key_at = lax.broadcasted_iota(jnp.int32, (text, text), 0)
    query_at = lax.broadcasted_iota(jnp.int32, (text, text), 1)
    seen = jnp.logical_and(key_at <= query_at, key_at < tok_ref[0])
    scaled = query * jnp.asarray(HEAD_DIM**-0.5, BF)
    parts = []
    for head in range(HEADS):
        lanes = lanes_of(head)
        score = nt(key[:, lanes], own_lanes(scaled[:, lanes], head))
        score = jnp.where(seen, score, MASKED)
        weight = jnp.exp(score - jnp.max(score, axis=0, keepdims=True))
        prob = weight / jnp.sum(weight, axis=0, keepdims=True)
        prob_ref[head] = prob
        parts.append(nn(value_t[rows_of(head)], prob.astype(BF)))
    ctx_t = jnp.concatenate(parts, axis=0)
    ctx_t_ref[...] = ctx_t.astype(BF)
    y1 = start + nn(ctx_t.T.astype(BF), out_ref[...]) + out_b_ref[1:2]
    y1_ref[...] = y1
    unit, _ = normalise(y1)
    norm_d = (unit * gain_ref[3:4] + shift_ref[3:4]).astype(BF)
    norm_d_ref[...] = norm_d
    cross_q_ref[...] = (nn(norm_d, cross_ref[:, :width]) + in_b_ref[2:3, :width]).astype(BF)


def encoder_forward(
    len_ref, x_ref, gain_ref, shift_ref, in_ref, in_b_ref, out_ref, out_b_ref,
    w1_ref, b1_ref, w2_ref, b2_ref, cin_ref,
    qkv_ref, ctx_t_ref, lse_ref, h1_ref, mem_ref, cross_ref,
    key_aug, value_t, act,
):
    rows, width = x_ref.shape
    unit, _ = normalise(x_ref[...].astype(F32))
    norm_a = (unit * gain_ref[0:1] + shift_ref[0:1]).astype(BF)
    qkv_ref[:, :width] = (nn(norm_a, in_ref[:, :width]) + in_b_ref[0:1, :width]).astype(BF)
    key = nn(norm_a, in_ref[:, width : 2 * width]).astype(BF)
    qkv_ref[:, width : 2 * width] = key
    value = (nn(norm_a, in_ref[:, 2 * width :]) + in_b_ref[0:1, width:]).astype(BF)
    qkv_ref[:, 2 * width :] = value
    value_t[...] = value.astype(F32).T.astype(BF)
    for head in range(HEADS):
        key_aug[head] = with_mask(key[:, lanes_of(head)], head, len_ref[0])
    step = 256

    def block(index, carry):
        at = pl.multiple_of(index * step, step)
        for head in range(HEADS):
            query = qkv_ref[pl.ds(at, step), lanes_of(head)] * jnp.asarray(HEAD_DIM**-0.5, BF)
            query = with_one(own_lanes(query, head), head)
            score = nt(key_aug[head], query)
            highest = jnp.max(score, axis=0, keepdims=True)
            weight = jnp.exp(score - highest)
            total = jnp.sum(weight, axis=0, keepdims=True)
            context = nn(value_t[rows_of(head)], weight.astype(BF)) * (1.0 / total)
            ctx_t_ref[rows_of(head), pl.ds(at, step)] = context.astype(BF)
            lse_ref[head : head + 1, pl.ds(at, step)] = highest + jnp.log(total)
        return carry

    lax.fori_loop(0, rows // step, block, 0)
    context = ctx_t_ref[...].astype(F32).T.astype(BF)
    h1 = x_ref[...].astype(F32) + nn(context, out_ref[...]) + out_b_ref[0:1]
    h1_ref[...] = h1
    unit, _ = normalise(h1)
    norm_b = (unit * gain_ref[1:2] + shift_ref[1:2]).astype(BF)

    def hidden_block(index, carry):
        at = pl.multiple_of(index * step, step)
        hidden = nn(norm_b, w1_ref[:, pl.ds(at, step)]) + b1_ref[0:1, pl.ds(at, step)]
        act[:, pl.ds(at, step)] = gelu_value(hidden).astype(BF)
        return carry

    lax.fori_loop(0, w1_ref.shape[1] // step, hidden_block, 0)
    memory = (h1_ref[...] + nn(act[...], w2_ref[...]) + b2_ref[0:1]).astype(BF)
    mem_ref[...] = memory
    cross_ref[:, :width] = nn(memory, cin_ref[:, width : 2 * width]).astype(BF)
    cross_ref[:, width:] = (nn(memory, cin_ref[:, 2 * width :]) + in_b_ref[2:3, width:]).astype(BF)


def decoder_main(
    tok_ref, len_ref,
    emb_ref, y1_ref, norm_c_ref, qkv_ref, ctx_t_ref, prob_ref, norm_d_ref, cross_q_ref,
    cross_ref, mem_ref, cot_ref, gain_ref, shift_ref,
    in1_ref, out1_ref, in2_ref, out2_ref, out_b_ref, w1_ref, b1_ref, w2_ref, b2_ref,
    dec_ref, dmem_ref, early_ref, late_ref, swap_ref,
    probs, small_ref,
):
    text, width = emb_ref.shape
    blocks = w1_ref.shape[1] // width
    small_ref[...] = jnp.zeros_like(small_ref)
    scaled = cross_q_ref[...] * jnp.asarray(HEAD_DIM**-0.5, BF)
    value_t = cross_ref[:, width:].astype(F32).T.astype(BF)
    parts = []
    for head in range(HEADS):
        lanes = lanes_of(head)
        key = with_mask(cross_ref[:, lanes], head, len_ref[0])
        score = nt(key, with_one(own_lanes(scaled[:, lanes], head), head))
        weight = jnp.exp(score - jnp.max(score, axis=0, keepdims=True))
        prob = weight * (1.0 / jnp.sum(weight, axis=0, keepdims=True))
        probs[head] = prob
        parts.append(nn(value_t[rows_of(head)], prob.astype(BF)))
    cross_t = jnp.concatenate(parts, axis=0)
    y2 = y1_ref[...] + nn(cross_t.T.astype(BF), out2_ref[...]) + out_b_ref[2:3]
    unit_e, scale_e = normalise(y2)
    norm_e = (unit_e * gain_ref[4:5] + shift_ref[4:5]).astype(BF)
    norm_e_t = norm_e.astype(F32).T.astype(BF)
    valid = lax.broadcasted_iota(jnp.int32, (text, 1), 0) < tok_ref[0]
    grad_low = jnp.where(valid, cot_ref[...], jnp.zeros_like(cot_ref))
    grad = grad_low.astype(F32)
    grad_low_t = grad.T.astype(BF)
    y3 = y2 + b2_ref[1:2]
    grad_norm = jnp.zeros((text, width), F32)
    chunk = 512
    for at in range(0, w1_ref.shape[1], chunk):
        part = slice(at, at + chunk)
        hidden = nn(norm_e, w1_ref[:, part]) + b1_ref[1:2, part]
        value, slope = gelu_both(hidden)
        active = value.astype(BF)
        y3 = y3 + nn(active, w2_ref[part])
        grad_hidden = (nt(grad_low, w2_ref[part]) * slope).astype(BF)
        bias = col_sum(grad_hidden)
        first = nn(norm_e_t, grad_hidden).astype(BF)
        for sub in range(0, chunk, width):
            row = (at + sub) // width
            small_ref[16 + row : 17 + row] = bias[:, sub : sub + width]
            early_ref[width * row : width * row + width] = first[:, sub : sub + width]
        early_ref[width * blocks + at : width * blocks + at + chunk] = nn(grad_low_t, active).T.astype(BF)
        grad_norm = grad_norm + nt(grad_hidden, w1_ref[:, part])
    dec_ref[...] = jnp.where(valid, y3, 0.0).astype(BF)
    small_ref[4:5] = col_sum(grad)
    grad_x, small_ref[0:1], small_ref[1:2] = norm_backward(grad_norm, unit_e, scale_e, gain_ref[4:5])
    grad = grad + grad_x
    grad_low = grad.astype(BF)
    small_ref[5:6] = col_sum(grad_low)
    early_ref[width * (2 * blocks + 3) :] = nn(cross_t.astype(BF), grad_low).astype(BF)
    grad_ctx = nt(grad_low, out2_ref[...]).astype(BF)
    key_t = cross_ref[:, :width].astype(F32).T.astype(BF)
    mem_t = mem_ref[...].astype(F32).T.astype(BF)
    dkeys = []
    dvalues = []
    dquery = []
    for pair in range(HEADS // 2):
        dkey = 0.0
        dvalue = 0.0
        for head in (2 * pair, 2 * pair + 1):
            lanes = lanes_of(head)
            own_grad = own_lanes(grad_ctx[:, lanes], head)
            prob = probs[head]
            dprob = nt(cross_ref[:, slice(width + lanes.start, width + lanes.stop)], own_grad)
            inner = jnp.sum(dprob * prob, axis=0, keepdims=True)
            dscore = (prob * (dprob - inner)).astype(BF)
            dvalue = dvalue + nn(prob.astype(BF), own_grad)
            dkey = dkey + nn(dscore, own_lanes(scaled[:, lanes], head))
            dquery.append(nn(key_t[rows_of(head)], dscore))
        dkeys.append(dkey.astype(BF))
        dvalues.append(dvalue.astype(BF))
    dq_t = jnp.concatenate(dquery, axis=0) * HEAD_DIM**-0.5
    dq = dq_t.T.astype(BF)
    dkv = jnp.concatenate(dkeys + dvalues, axis=1)
    small_ref[6:7] = col_sum(dq)
    small_ref[7:8] = col_sum(dkv[:, width:])
    norm_d = norm_d_ref[...]
    base = 2 * width * blocks
    early_ref[base : base + width] = nn(norm_d.astype(F32).T.astype(BF), dq).astype(BF)
    pairs = nn(mem_t, dkv).astype(BF)
    early_ref[base + width : base + 2 * width] = pairs[:, :width]
    early_ref[base + 2 * width : base + 3 * width] = pairs[:, width:]
    dmem_ref[...] = nt(dkv, in2_ref[:, width:]).astype(BF)
    unit, scale = normalise(y1_ref[...])
    grad_x, small_ref[8:9], small_ref[9:10] = norm_backward(
        nt(dq, in2_ref[:, :width]), unit, scale, gain_ref[3:4]
    )
    grad = grad + grad_x
    grad_low = grad.astype(BF)
    small_ref[10:11] = col_sum(grad_low)
    dout1 = nn(ctx_t_ref[...], grad_low).astype(BF)
    late_ref[3 * width :] = dout1[: width - SPILL]
    swap_ref[text + SMALL :] = dout1[width - SPILL :]
    grad_ctx = nt(grad_low, out1_ref[...]).astype(BF)
    key_t = qkv_ref[:, width : 2 * width].astype(F32).T.astype(BF)
    scaled = qkv_ref[:, :width] * jnp.asarray(HEAD_DIM**-0.5, BF)
    dkeys = []
    dvalues = []
    dquery = []
    for pair in range(HEADS // 2):
        dkey = 0.0
        dvalue = 0.0
        for head in (2 * pair, 2 * pair + 1):
            lanes = lanes_of(head)
            own_grad = own_lanes(grad_ctx[:, lanes], head)
            prob = prob_ref[head]
            dprob = nt(qkv_ref[:, slice(2 * width + lanes.start, 2 * width + lanes.stop)], own_grad)
            inner = jnp.sum(dprob * prob, axis=0, keepdims=True)
            dscore = (prob * (dprob - inner)).astype(BF)
            dvalue = dvalue + nn(prob.astype(BF), own_grad)
            dkey = dkey + nn(dscore, own_lanes(scaled[:, lanes], head))
            dquery.append(nn(key_t[rows_of(head)], dscore))
        dkeys.append(dkey.astype(BF))
        dvalues.append(dvalue.astype(BF))
    dq_t = jnp.concatenate(dquery, axis=0) * HEAD_DIM**-0.5
    dqkv = jnp.concatenate([dq_t.T.astype(BF)] + dkeys + dvalues, axis=1)
    small_ref[11:12] = col_sum(dqkv[:, :width])
    small_ref[12:13] = col_sum(dqkv[:, 2 * width :])
    din1 = nn(norm_c_ref[...].astype(F32).T.astype(BF), dqkv).astype(BF)
    for part in range(3):
        late_ref[width * part : width * part + width] = din1[:, width * part : width * part + width]
    unit, scale = normalise(emb_ref[...].astype(F32) * math.sqrt(width))
    grad_x, small_ref[13:14], small_ref[14:15] = norm_backward(
        nt(dqkv, in1_ref[...]), unit, scale, gain_ref[2:3]
    )
    swap_ref[:text] = ((grad + grad_x) * math.sqrt(width)).astype(BF)
    swap_ref[text : text + SMALL] = small_ref[...].astype(BF)


def early_merge(core_ref, ids_ref, early_ref, other_ref, swap_ref, swapped_ref, out_ref):
    core = core_ref[0]
    text = ids_ref.shape[1] // 2
    half = other_ref.shape[0]
    out_ref[:half] = (early_ref[...].astype(F32) + other_ref[...].astype(F32)).astype(BF)
    grad = jnp.concatenate([swap_ref[:text], swapped_ref[:text]], axis=0)
    chunk = half // 4
    for at in range(0, half, chunk):
        row = lax.broadcasted_iota(jnp.int32, (chunk, 2 * text), 0) + (at + core * half)
        hot = jnp.where(row == ids_ref[...], 1.0, 0.0).astype(BF)
        out_ref[half + at : half + at + chunk] = nn(hot, grad).astype(BF)

    @pl.when(core == 1)
    def _():
        rest = swap_ref[text:].astype(F32) + swapped_ref[text:].astype(F32)
        out_ref[2 * half - rest.shape[0] :] = rest.astype(BF)


def late_merge(core_ref, feed_ref, feed_other_ref, attn_ref, attn_other_ref, early_ref, out_ref):
    count = out_ref.shape[0]
    size = early_ref.shape[1]
    feed = feed_ref[...].astype(F32) + feed_other_ref[...].astype(F32)
    attn = attn_ref[...].astype(F32) + attn_other_ref[...].astype(F32)
    late = jnp.concatenate([feed.astype(BF), attn.astype(BF)], axis=0)
    out_ref[:, size:] = late.reshape(count, -1, late.shape[1])
    early = jnp.sum(early_ref[...].astype(F32), axis=0).astype(BF)
    for place in range(count):
        out_ref[place, :size] = early


def late_split(parts_ref, early_ref, late_ref):
    size = early_ref.shape[1]
    early_ref[...] = parts_ref[:, :size]
    late = jnp.sum(parts_ref[:, size:].astype(F32), axis=0).astype(BF)
    for place in range(late_ref.shape[0]):
        late_ref[place] = late


def early_outputs(core_ref, rate_ref, mine_ref, other_ref, table_ref, in_ref, out_ref, w1_ref, w2_ref, rest_ref):
    rate = rate_ref[0]
    first = core_ref[0] == 0
    half = mine_ref.shape[0] // 2
    width = mine_ref.shape[1]
    blocks = w1_ref.shape[1] // width

    def rows(core, at, size):
        mine, other = mine_ref[at : at + size], other_ref[at : at + size]
        return jnp.where(first, mine, other) if core == 0 else jnp.where(first, other, mine)

    table_ref[:half] = rows(0, half, half).astype(F32) * rate
    rest = rows(1, half, half)
    table_ref[half:] = rest[: table_ref.shape[0] - half].astype(F32) * rate
    rest_ref[...] = rest[half - rest_ref.shape[0] :]
    grads = jnp.concatenate([rows(0, 0, half), rows(1, 0, half)], axis=0).astype(F32) * rate
    for block in range(blocks):
        w1_ref[:, width * block : width * block + width] = grads[width * block : width * block + width]
    w2_ref[...] = grads[width * blocks : 2 * width * blocks]
    base = 2 * width * blocks
    for part in range(3):
        in_ref[:, width * part : width * part + width] = grads[base + width * part : base + width * part + width]
    out_ref[...] = grads[base + 3 * width :]


def late_outputs(
    core_ref, rate_ref, mine_ref, other_ref, early_ref, in_in, out_in, w1_in, w2_in,
    in_ref, out_ref, w1_ref, w2_ref, small_ref,
):
    rate = rate_ref[0]
    first = core_ref[0] == 0
    width = mine_ref.shape[1]
    hidden = w2_ref.shape[0]
    blocks = hidden // width
    cut = (width - SPILL) // 2
    base = hidden + 2 * width

    def rows(core, at, size):
        mine, other = mine_ref[at : at + size], other_ref[at : at + size]
        picked = jnp.where(first, mine, other) if core == 0 else jnp.where(first, other, mine)
        return picked.astype(F32) * rate

    for block in range(blocks):
        w1_ref[:, width * block : width * block + width] = rows(0, width * block, width)
    w2_ref[...] = rows(1, 0, hidden)
    in_ref[1, :, :width] = rows(0, hidden, width)
    in_ref[1, :, width : 2 * width] = rows(0, hidden + width, width)
    in_ref[1, :, 2 * width :] = rows(1, hidden, width)
    out_ref[0] = rows(1, hidden + width, width)
    out_ref[1, :cut] = rows(0, base, cut)
    out_ref[1, cut : 2 * cut] = rows(1, base, cut)
    out_ref[1, 2 * cut :] = early_ref[SMALL:].astype(F32) * rate
    attn = jnp.concatenate([rows(core, base + cut, mine_ref.shape[0] - base - cut) for core in range(2)], axis=0)
    for part in range(3):
        in_ref[0, :, width * part : width * part + width] = attn[width * part : width * part + width]
    small_ref[:SMALL] = attn[3 * width : 3 * width + SMALL]
    small_ref[SMALL:] = early_ref[:SMALL].astype(F32) * rate


def frames_back(place_ref, own_ref, next_ref, second_ref, third_ref, out_ref):
    count = out_ref.shape[0]
    for shift, ref in enumerate((own_ref, next_ref, second_ref, third_ref)):
        out_ref[lax.rem(place_ref[0] + (count - shift), count)] = ref[...].astype(F32)


def encoder_feed_backward(
    h1_ref, dmem_ref, ctx_t_ref, gain_ref, shift_ref, w1_ref, b1_ref, w2_ref, out_ref, late_ref,
    dh1_ref, dctx_ref, feed_ref, small_ref,
    grad_hid,
):
    width = h1_ref.shape[1]
    hidden_size = w1_ref.shape[1]
    cut = (width - SPILL) // 2
    feed_ref[0, hidden_size : hidden_size + 2 * width] = late_ref[: 2 * width]
    feed_ref[1, hidden_size : hidden_size + width] = late_ref[2 * width : 3 * width]
    feed_ref[0, hidden_size + 2 * width :] = late_ref[3 * width : 3 * width + cut]
    feed_ref[1, hidden_size + 2 * width :] = late_ref[3 * width + cut :]
    small_ref[...] = jnp.zeros_like(small_ref)
    unit, _ = normalise(h1_ref[...])
    norm_b = unit * gain_ref[1:2] + shift_ref[1:2]
    norm_b_t = norm_b.T.astype(BF)
    norm_b = norm_b.astype(BF)
    grad_low = dmem_ref[...]
    grad_low_t = grad_low.astype(F32).T.astype(BF)
    step = 256

    def block(index, carry):
        part = pl.ds(pl.multiple_of(index * step, step), step)
        hidden = nn(norm_b, w1_ref[:, part]) + b1_ref[0:1, part]
        value, slope = gelu_both(hidden)
        grad_hidden = (nt(grad_low, w2_ref[part]) * slope).astype(BF)
        grad_hid[:, part] = grad_hidden
        small_ref[pl.ds(8 + index, 1)] = col_sum(grad_hidden)
        feed_ref[0, part] = nn(norm_b_t, grad_hidden).astype(BF)
        feed_ref[1, part] = nn(grad_low_t, value.astype(BF)).T.astype(BF)
        return carry

    lax.fori_loop(0, w1_ref.shape[1] // step, block, 0)
    grad = grad_low.astype(F32)
    small_ref[2:3] = col_sum(grad)
    unit, scale = normalise(h1_ref[...])
    grad_x, small_ref[0:1], small_ref[1:2] = norm_backward(
        nt(grad_hid[...], w1_ref[...]), unit, scale, gain_ref[1:2]
    )
    grad = grad + grad_x
    dh1_ref[...] = grad
    grad_low = grad.astype(BF)
    small_ref[3:4] = col_sum(grad_low)
    feed_ref[1, hidden_size + width : hidden_size + 2 * width] = nn(ctx_t_ref[...], grad_low).astype(BF)
    dctx_ref[...] = nt(grad_low, out_ref[...]).astype(BF)


def encoder_attention_backward(
    len_ref, x_ref, qkv_ref, lse_ref, dctx_ref, dh1_ref, gain_ref, shift_ref, in_ref, feed_small_ref,
    dx_ref, attn_ref,
    key_aug, key_t, dkv, dq_t, dqkv, small_ref,
):
    rows, width = x_ref.shape
    small_ref[...] = jnp.zeros_like(small_ref)
    small_ref[8:24] = feed_small_ref[...]
    for head in range(HEADS):
        lanes = lanes_of(head)
        key_aug[head] = with_mask(qkv_ref[:, slice(width + lanes.start, width + lanes.stop)], head, len_ref[0])
    key_t[...] = qkv_ref[:, width : 2 * width].astype(F32).T.astype(BF)
    dkv[...] = jnp.zeros_like(dkv)
    step = 256

    def block(index, carry):
        at = pl.multiple_of(index * step, step)
        for head in range(HEADS):
            lanes = lanes_of(head)
            query = own_lanes(qkv_ref[pl.ds(at, step), lanes] * jnp.asarray(HEAD_DIM**-0.5, BF), head)
            score = nt(key_aug[head], with_one(query, head))
            prob = jnp.exp(score - lse_ref[head : head + 1, pl.ds(at, step)])
            own_grad = own_lanes(dctx_ref[pl.ds(at, step), lanes], head)
            dprob = nt(qkv_ref[:, slice(2 * width + lanes.start, 2 * width + lanes.stop)], own_grad)
            inner = jnp.sum(dprob * prob, axis=0, keepdims=True)
            dscore = (prob * (dprob - inner)).astype(BF)
            dkv[:, lanes] += nn(dscore, query)
            dkv[:, slice(width + lanes.start, width + lanes.stop)] += nn(prob.astype(BF), own_grad)
            dq_t[rows_of(head), pl.ds(at, step)] = nn(key_t[rows_of(head)], dscore)
        return carry

    lax.fori_loop(0, rows // step, block, 0)
    dqkv[:, :width] = (dq_t[...].T * HEAD_DIM**-0.5).astype(BF)
    dqkv[:, width:] = dkv[...].astype(BF)
    small_ref[2:3] = col_sum(dqkv[:, :width])
    small_ref[3:4] = col_sum(dqkv[:, 2 * width :])
    unit, scale = normalise(x_ref[...].astype(F32))
    norm_a = unit * gain_ref[0:1] + shift_ref[0:1]
    din = nn(norm_a.T.astype(BF), dqkv[...]).astype(BF)
    for part in range(3):
        attn_ref[width * part : width * part + width] = din[:, width * part : width * part + width]
    grad_x, small_ref[0:1], small_ref[1:2] = norm_backward(
        nt(dqkv[...], in_ref[...]), unit, scale, gain_ref[0:1]
    )
    dx_ref[...] = (dh1_ref[...] + grad_x).astype(BF)
    attn_ref[3 * width :] = jnp.zeros_like(attn_ref[3 * width :])
    attn_ref[3 * width : 3 * width + SMALL] = small_ref[...].astype(BF)


def swap_cores(array):
    return lax.ppermute(array, "core", [(0, 1), (1, 0)])


def other_half(halves, core):
    return swap_cores(lax.dynamic_index_in_dim(halves, 1 - core, keepdims=False))


def body(
    frames, utt_len, token_ids, tok_len, step, embed, norm_gain, norm_bias, attn_in, attn_in_bias,
    attn_out, attn_out_bias, ff_in, ff_in_bias, ff_out, ff_out_bias, cotangent,
):
    ring = ("frame", "pair")
    devices = lax.axis_size(ring)
    core = lax.axis_index("core")
    core_at = core[None]
    frame_at = lax.axis_index("frame")
    vocab, width = embed.shape
    hidden = ff_in.shape[2]
    frame_count = lax.axis_size("frame")
    local_len = frames.shape[2]
    rows = local_len * frame_count
    text = token_ids.shape[2]
    my_len = lax.dynamic_slice_in_dim(utt_len[0], frame_at, 1)
    my_tok = tok_len[0]
    arrived = lax.all_to_all(frames[0], "frame", split_axis=0, concat_axis=1, tiled=True)
    source = arrived.reshape(rows, width)
    ids = token_ids[0, 0]
    both_ids = jnp.concatenate([ids, swap_cores(ids)])[None]
    rows_in = embed[ids]
    count_step = step[0].astype(F32)
    rate = jnp.minimum(lax.rsqrt(count_step), count_step * WARMUP ** (-1.5)) * WARMUP**0.5
    rate = rate[None]

    y1, norm_c, dec_qkv, dec_ctx_t, dec_prob, norm_d, cross_q = call(
        decoder_start,
        [
            ((text, width), F32), ((text, width), BF), ((text, 3 * width), BF), ((width, text), BF),
            ((HEADS, text, text), F32), ((text, width), BF), ((text, width), BF),
        ],
        [
            rows_in, norm_gain, norm_bias, (attn_in, 1), attn_in_bias, (attn_out, 1),
            attn_out_bias, (attn_in, 2),
        ],
        [my_tok],
        flops=2 * text * width * width * 5,
    )
    enc_qkv, enc_ctx_t, lse, h1, memory, cross_kv = call(
        encoder_forward,
        [
            ((rows, 3 * width), BF), ((width, rows), BF), ((8, rows), F32), ((rows, width), F32),
            ((rows, width), BF), ((rows, 2 * width), BF),
        ],
        [
            source, norm_gain, norm_bias, (attn_in, 0), attn_in_bias, (attn_out, 0),
            attn_out_bias, (ff_in, 0), ff_in_bias, (ff_out, 0), ff_out_bias, (attn_in, 2),
        ],
        [my_len],
        [
            pltpu.VMEM((HEADS, rows, 128), BF), pltpu.VMEM((width, rows), BF),
            pltpu.VMEM((rows, hidden), BF),
        ],
        flops=2 * rows * width * (6 * width + 2 * rows + 2 * hidden),
    )
    dec_out, dmem, early, late, swap = call(
        decoder_main,
        [
            ((text, width), BF), ((rows, width), BF), ((4 * width + 2 * hidden, width), BF),
            ((4 * width - SPILL, width), BF), ((text + SMALL + SPILL, width), BF),
        ],
        [
            rows_in, y1, norm_c, dec_qkv, dec_ctx_t, dec_prob, norm_d, cross_q, cross_kv, memory,
            cotangent[0, 0], norm_gain, norm_bias, (attn_in, 1), (attn_out, 1), (attn_in, 2),
            (attn_out, 2), attn_out_bias, (ff_in, 1), ff_in_bias, (ff_out, 1), ff_out_bias,
        ],
        [my_tok, my_len],
        [pltpu.VMEM((HEADS, rows, text), F32), pltpu.VMEM((SMALL, width), F32)],
        flops=2 * text * width * (6 * hidden + 7 * rows + 16 * width) + 2 * rows * width * 4 * width,
    )
    swapped = swap_cores(swap)
    half = early.shape[0] // 2
    early = early.reshape(2, half, width)
    (early_sum,) = call(
        early_merge,
        [((2 * half, width), BF)],
        [both_ids, (early, [0]), other_half(early, core), swap, swapped],
        [core_at],
        flops=4 * half * width * text,
    )
    early_sum, dmem = lax.optimization_barrier((early_sum, dmem))
    early_parts = lax.all_to_all(
        early_sum.reshape(devices, -1, width), ring, split_axis=0, concat_axis=0, tiled=True
    )
    early_own = jnp.sum(early_parts.astype(F32), axis=0).astype(BF)

    dh1, dctx, feed, feed_small = call(
        encoder_feed_backward,
        [
            ((rows, width), F32), ((rows, width), BF), ((2, (5 * width - SPILL) // 2 + hidden, width), BF),
            ((16, width), F32),
        ],
        [
            h1, dmem, enc_ctx_t, norm_gain, norm_bias, (ff_in, 0), ff_in_bias, (ff_out, 0),
            (attn_out, 0), late,
        ],
        scratch=[pltpu.VMEM((rows, hidden), BF)],
        flops=2 * rows * width * (5 * hidden + 2 * width),
    )
    feed_other = other_half(feed, core)
    dx, attn = call(
        encoder_attention_backward,
        [((rows, width), BF), ((3 * width + 2 * SMALL, width), BF)],
        [source, enc_qkv, lse, dctx, dh1, norm_gain, norm_bias, (attn_in, 0), feed_small],
        [my_len],
        [
            pltpu.VMEM((HEADS, rows, 128), BF), pltpu.VMEM((width, rows), BF),
            pltpu.VMEM((rows, 2 * width), F32), pltpu.VMEM((width, rows), F32),
            pltpu.VMEM((rows, 3 * width), BF), pltpu.VMEM((SMALL, width), F32),
        ],
        flops=2 * rows * width * (5 * rows + 6 * width),
    )
    attn = attn.reshape(2, -1, width)
    late_half = feed.shape[1] + attn.shape[1]
    (mixed,) = call(
        late_merge,
        [((devices, (2 * half + late_half) // devices, width), BF)],
        [(feed, [0]), feed_other, (attn, [0]), other_half(attn, core), early_parts],
        [core_at],
    )
    mixed = lax.all_to_all(mixed, ring, split_axis=0, concat_axis=0, tiled=True)
    chunks = dx.reshape(frame_count, local_len, width)
    moved = []
    for shift in range(frame_count):
        target = lax.rem(frame_at + shift, frame_count)
        chunk = lax.dynamic_index_in_dim(chunks, target, keepdims=False)
        if shift:
            chunk = lax.ppermute(chunk, "frame", [(i, (i + shift) % frame_count) for i in range(frame_count)])
        moved.append(chunk)
    (frames_grad,) = call(
        frames_back, [((frame_count, local_len, width), F32)], moved, [frame_at[None]]
    )
    mixed, frames_grad = lax.optimization_barrier((mixed, frames_grad))
    early_mine, late_own = call(
        late_split,
        [((devices, 2 * half // devices, width), BF), ((devices, late_half // devices, width), BF)],
        [mixed],
    )
    early_mine = early_mine.reshape(2 * half, width)
    early_other = swap_cores(early_mine)
    late_mine = lax.all_to_all(late_own, ring, split_axis=0, concat_axis=0, tiled=True)
    in_shape = (3, width, 3 * width)
    out_shape = (3, width, width)
    w1_shape = (2, width, hidden)
    w2_shape = (2, hidden, width)
    table_grad, in_grad, out_grad, w1_grad, w2_grad, early_rest = call(
        early_outputs,
        [
            ((vocab, width), F32), (in_shape, F32, None, 2), (out_shape, F32, None, 2),
            (w1_shape, F32, None, 1), (w2_shape, F32, None, 1), ((SMALL + SPILL, width), BF),
        ],
        [early_mine, early_other],
        [core_at, rate],
    )
    late_mine, early_rest = lax.optimization_barrier((late_mine, early_rest))
    late_mine = late_mine.reshape(late_half, width)
    late_other = swap_cores(late_mine)

    in_grad, out_grad, w1_grad, w2_grad, small = call(
        late_outputs,
        [
            (in_shape, F32, 2, 0), (out_shape, F32, 2, 0), (w1_shape, F32, None, 0),
            (w2_shape, F32, None, 0), ((2 * SMALL, width), F32),
        ],
        [
            late_mine, late_other, early_rest, (in_grad, None), (out_grad, None), (w1_grad, None),
            (w2_grad, None),
        ],
        [core_at, rate],
        aliases={5: 0, 6: 1, 7: 2, 8: 3},
    )
    pick = lambda *at: jnp.concatenate([small[i : i + 1] for i in at])
    dec = lambda i: SMALL + i
    bias = lambda at: small[at : at + hidden // width].reshape(1, hidden)
    return (
        dec_out[None, None],
        frames_grad[None],
        table_grad,
        pick(0, 8, dec(13), dec(8), dec(0)),
        pick(1, 9, dec(14), dec(9), dec(1)),
        in_grad,
        pick(2, 3, dec(11), dec(12), dec(6), dec(7)).reshape(3, 2 * width),
        out_grad,
        pick(11, dec(10), dec(5)),
        w1_grad,
        jnp.concatenate([bias(16), bias(dec(16))]),
        w2_grad,
        pick(10, dec(4)),
    )


def solution(mesh):
    groups = ("pair", "core")
    frames, batch = mesh.devices.shape
    split = Mesh(mesh.devices.reshape(frames, batch // 2, 2), ("frame",) + groups)
    placed = (
        P(groups, None, "frame", None),
        P(groups, None),
        P(groups, "frame", None),
        P(groups, "frame"),
    ) + (P(),) * 12 + (P(groups, "frame", None, None),)
    results = (P(groups, "frame", None, None), P(groups, None, "frame", None)) + (P(),) * 11
    return jax.shard_map(body, mesh=split, in_specs=placed, out_specs=results, check_vma=False)
```

```python
import functools
import math

import jax
import jax.numpy as jnp
from jax import lax
from jax.experimental import pallas as pl
from jax.experimental.pallas import tpu as pltpu
from jax.sharding import Mesh, PartitionSpec as P

HEADS = 4
HEAD_DIM = 64
WARMUP = 25000
EPSILON = 1e-05
MASKED = -1e30
BF = jnp.bfloat16
F32 = jnp.float32
GELU_A = math.sqrt(2.0 / math.pi)
GELU_B = GELU_A * 0.044715
SMALL = 32
SPILL = 64


def nn(left, right):
    return lax.dot_general(left, right, (((1,), (0,)), ((), ())), preferred_element_type=F32)


def nt(left, right):
    return lax.dot_general(left, right, (((1,), (1,)), ((), ())), preferred_element_type=F32)


def hand_out(sems, *pairs):
    copies = [pltpu.make_async_copy(held, ref, sems.at[i]) for i, (held, ref) in enumerate(pairs)]
    for copy in copies:
        copy.start()
    for copy in copies:
        copy.wait()


def normalise(states):
    average = jnp.mean(states, axis=-1, keepdims=True)
    centred = states - average
    scale = lax.rsqrt(jnp.mean(centred * centred, axis=-1, keepdims=True) + EPSILON)
    return centred * scale, scale


def norm_backward(grad, unit, scale, gain):
    grad_unit = grad * gain
    mean_grad = jnp.mean(grad_unit, axis=-1, keepdims=True)
    mean_along = jnp.mean(grad_unit * unit, axis=-1, keepdims=True)
    grad_states = scale * (grad_unit - mean_grad - unit * mean_along)
    return grad_states, col_sum(grad * unit), col_sum(grad)


def col_sum(matrix):
    return jnp.sum(matrix.astype(F32), axis=0, keepdims=True)


def gelu_value(hidden):
    inner = hidden * (GELU_A + GELU_B * (hidden * hidden))
    return hidden * (0.5 + 0.5 * jnp.tanh(inner))


def gelu_both(hidden):
    square = hidden * hidden
    bent = jnp.tanh(hidden * (GELU_A + GELU_B * square))
    half = 0.5 + 0.5 * bent
    slope = half + (0.5 * hidden) * (1.0 - bent * bent) * (GELU_A + 3.0 * GELU_B * square)
    return hidden * half, slope


def lanes_of(head):
    return slice(128 * (head // 2), 128 * (head // 2) + 128)


def rows_of(head):
    return slice(HEAD_DIM * head, HEAD_DIM * head + HEAD_DIM)


def own_lanes(pair, head):
    lane = lax.broadcasted_iota(jnp.int32, pair.shape, 1)
    mine = (lane < HEAD_DIM) if head % 2 == 0 else (lane >= HEAD_DIM)
    return jnp.where(mine, pair, jnp.zeros_like(pair))


def spare_lane(head):
    return HEAD_DIM if head % 2 == 0 else 0


def with_one(query, head):
    lane = lax.broadcasted_iota(jnp.int32, query.shape, 1)
    return jnp.where(lane == spare_lane(head), jnp.ones_like(query), query)


def with_mask(key_pair, head, length):
    lane = lax.broadcasted_iota(jnp.int32, key_pair.shape, 1)
    row = lax.broadcasted_iota(jnp.int32, key_pair.shape, 0)
    bias = jnp.where(row < length, 0.0, MASKED).astype(BF)
    return jnp.where(lane == spare_lane(head), bias, key_pair)


def part_spec(shape, layers, at):
    index = (at,) + (0,) * (len(shape) - 1)
    return pl.BlockSpec((layers,) + shape[1:], lambda *g: index, pipeline_mode=pl.Buffered(1))


def call(kernel, outs, args, scalars=(), scratch=(), flops=0, aliases=None, limit=61):
    in_specs = []
    for a in args:
        if not isinstance(a, tuple):
            in_specs.append(part_spec(a.shape, a.shape[0], 0))
        elif a[1] is None:
            in_specs.append(pl.BlockSpec(memory_space=pl.ANY))
        else:
            in_specs.append(part_spec(a[0].shape, None, a[1]))
    args = [a[0] if isinstance(a, tuple) else a for a in args]
    out_specs = []
    for out in outs:
        if out[-1] is None:
            out_specs.append(pl.BlockSpec(memory_space=pl.ANY))
        elif isinstance(out[-1], int):
            out_specs.append(part_spec(out[0], out[2], out[3]))
        else:
            out_specs.append(part_spec(out[0], out[0][0], 0))
    size = sum(a.size * a.dtype.itemsize for a in args)
    size += sum(math.prod(out[0]) * jnp.dtype(out[1]).itemsize for out in outs)
    return pl.pallas_call(
        kernel,
        grid_spec=pltpu.PrefetchScalarGridSpec(
            num_scalar_prefetch=len(scalars),
            grid=(1,),
            in_specs=in_specs,
            out_specs=out_specs,
            scratch_shapes=list(scratch),
        ),
        out_shape=[jax.ShapeDtypeStruct(out[0], out[1]) for out in outs],
        input_output_aliases=aliases or {},
        compiler_params=pltpu.CompilerParams(vmem_limit_bytes=limit * 1024 * 1024),
        cost_estimate=pl.CostEstimate(flops=flops, bytes_accessed=size, transcendentals=0),
        name=kernel.__name__,
    )(*scalars, *args)


def decoder_start(
    tok_ref, emb_ref, gain_ref, shift_ref, in_ref, in_b_ref, out_ref, out_b_ref, cross_ref,
    y1_ref, norm_c_ref, qkv_ref, ctx_t_ref, prob_ref, norm_d_ref, cross_q_ref,
):
    text = emb_ref.shape[0]
    width = emb_ref.shape[1]
    start = emb_ref[...].astype(F32) * math.sqrt(width)
    unit, _ = normalise(start)
    norm_c = (unit * gain_ref[2:3] + shift_ref[2:3]).astype(BF)
    norm_c_ref[...] = norm_c
    flat = nn(norm_c, in_ref[...])
    query = (flat[:, :width] + in_b_ref[1:2, :width]).astype(BF)
    key = flat[:, width : 2 * width].astype(BF)
    value = (flat[:, 2 * width :] + in_b_ref[1:2, width:]).astype(BF)
    qkv_ref[:, :width] = query
    qkv_ref[:, width : 2 * width] = key
    qkv_ref[:, 2 * width :] = value
    value_t = value.astype(F32).T.astype(BF)
    key_at = lax.broadcasted_iota(jnp.int32, (text, text), 0)
    query_at = lax.broadcasted_iota(jnp.int32, (text, text), 1)
    seen = jnp.logical_and(key_at <= query_at, key_at < tok_ref[0])
    scaled = query * jnp.asarray(HEAD_DIM**-0.5, BF)
    parts = []
    for head in range(HEADS):
        lanes = lanes_of(head)
        score = nt(key[:, lanes], own_lanes(scaled[:, lanes], head))
        score = jnp.where(seen, score, MASKED)
        weight = jnp.exp(score - jnp.max(score, axis=0, keepdims=True))
        prob = weight / jnp.sum(weight, axis=0, keepdims=True)
        prob_ref[head] = prob
        parts.append(nn(value_t[rows_of(head)], prob.astype(BF)))
    ctx_t = jnp.concatenate(parts, axis=0)
    ctx_t_ref[...] = ctx_t.astype(BF)
    y1 = start + nn(ctx_t.T.astype(BF), out_ref[...]) + out_b_ref[1:2]
    y1_ref[...] = y1
    unit, _ = normalise(y1)
    norm_d = (unit * gain_ref[3:4] + shift_ref[3:4]).astype(BF)
    norm_d_ref[...] = norm_d
    cross_q_ref[...] = (nn(norm_d, cross_ref[:, :width]) + in_b_ref[2:3, :width]).astype(BF)


def encoder_forward(
    len_ref, at_ref, x_ref, gain_ref, shift_ref, in_ref, in_b_ref, out_ref, out_b_ref,
    w1_ref, b1_ref, w2_ref, b2_ref, cin_ref,
    qkv_ref, ctx_t_ref, lse_ref, h1_ref, mem_ref, cross_ref,
    key_aug, value_t, act,
):
    rows, width = x_ref.shape
    unit, _ = normalise(x_ref[...].astype(F32))
    norm_a = (unit * gain_ref[0:1] + shift_ref[0:1]).astype(BF)
    qkv_ref[:, :width] = (nn(norm_a, in_ref[:, :width]) + in_b_ref[0:1, :width]).astype(BF)
    key = nn(norm_a, in_ref[:, width : 2 * width]).astype(BF)
    qkv_ref[:, width : 2 * width] = key
    value = (nn(norm_a, in_ref[:, 2 * width :]) + in_b_ref[0:1, width:]).astype(BF)
    qkv_ref[:, 2 * width :] = value
    value_t[...] = value.astype(F32).T.astype(BF)
    for head in range(HEADS):
        key_aug[head] = with_mask(key[:, lanes_of(head)], head, len_ref[at_ref[0]])
    for head in range(HEADS):
        query = qkv_ref[:, lanes_of(head)] * jnp.asarray(HEAD_DIM**-0.5, BF)
        query = with_one(own_lanes(query, head), head)
        score = nt(key_aug[head], query)
        highest = jnp.max(score, axis=0, keepdims=True)
        weight = jnp.exp(score - highest)
        total = jnp.sum(weight, axis=0, keepdims=True)
        context = nn(value_t[rows_of(head)], weight.astype(BF)) * (1.0 / total)
        ctx_t_ref[rows_of(head)] = context.astype(BF)
        lse_ref[head : head + 1] = highest + jnp.log(total)
    context = ctx_t_ref[...].astype(F32).T.astype(BF)
    h1 = x_ref[...].astype(F32) + nn(context, out_ref[...]) + out_b_ref[0:1]
    h1_ref[...] = h1
    unit, _ = normalise(h1)
    norm_b = (unit * gain_ref[1:2] + shift_ref[1:2]).astype(BF)

    hidden = nn(norm_b, w1_ref[...]) + b1_ref[0:1]
    act[...] = gelu_value(hidden).astype(BF)
    memory = (h1_ref[...] + nn(act[...], w2_ref[...]) + b2_ref[0:1]).astype(BF)
    mem_ref[...] = memory
    cross_ref[:, :width] = nn(memory, cin_ref[:, width : 2 * width]).astype(BF)
    cross_ref[:, width:] = (nn(memory, cin_ref[:, 2 * width :]) + in_b_ref[2:3, width:]).astype(BF)


def decoder_main(
    tok_ref, len_ref, at_ref, core_ref,
    y1_ref, norm_d_ref, cross_q_ref, cross_ref, mem_ref, cot_ref, gain_ref, shift_ref,
    in2_ref, out2_ref, out_b_ref, w1_ref, b1_ref, w2_ref, b2_ref,
    dec_ref, dmem_ref, early_ref, grad_ref, small_ref,
    probs,
):
    text, width = y1_ref.shape
    hidden_size = w1_ref.shape[1]
    slot = (core_ref[0], 1 - core_ref[0])
    small_ref[...] = jnp.zeros_like(small_ref)
    scaled = cross_q_ref[...] * jnp.asarray(HEAD_DIM**-0.5, BF)
    value_t = cross_ref[:, width:].astype(F32).T.astype(BF)
    parts = []
    for head in range(HEADS):
        lanes = lanes_of(head)
        key = with_mask(cross_ref[:, lanes], head, len_ref[at_ref[0]])
        score = nt(key, with_one(own_lanes(scaled[:, lanes], head), head))
        weight = jnp.exp(score - jnp.max(score, axis=0, keepdims=True))
        prob = weight * (1.0 / jnp.sum(weight, axis=0, keepdims=True))
        probs[head] = prob
        parts.append(nn(value_t[rows_of(head)], prob.astype(BF)))
    cross_t = jnp.concatenate(parts, axis=0)
    y2 = y1_ref[...] + nn(cross_t.T.astype(BF), out2_ref[...]) + out_b_ref[2:3]
    unit_e, scale_e = normalise(y2)
    norm_e = (unit_e * gain_ref[4:5] + shift_ref[4:5]).astype(BF)
    norm_e_t = norm_e.astype(F32).T.astype(BF)
    valid = lax.broadcasted_iota(jnp.int32, (text, 1), 0) < tok_ref[0]
    grad_low = jnp.where(valid, cot_ref[...], jnp.zeros_like(cot_ref))
    grad = grad_low.astype(F32)
    grad_low_t = grad.T.astype(BF)
    y3 = y2 + b2_ref[1:2]
    grad_norm = jnp.zeros((text, width), F32)
    chunk = 512
    for at in range(0, w1_ref.shape[1], chunk):
        part = slice(at, at + chunk)
        hidden = nn(norm_e, w1_ref[:, part]) + b1_ref[1:2, part]
        value, slope = gelu_both(hidden)
        active = value.astype(BF)
        y3 = y3 + nn(active, w2_ref[part])
        grad_hidden = (nt(grad_low, w2_ref[part]) * slope).astype(BF)
        bias = col_sum(grad_hidden)
        first = nn(norm_e_t, grad_hidden).astype(BF)
        for sub in range(0, chunk, width):
            row = (at + sub) // width
            small_ref[16 + row : 17 + row] = bias[:, sub : sub + width]
            early_ref[slot[0], width * row : width * row + width] = first[:, sub : sub + width]
        second = nn(grad_low_t, active).T.astype(BF)
        if at == 0:
            early_ref[slot[0], hidden_size:] = second
        else:
            early_ref[slot[1], at - chunk : at] = second
        grad_norm = grad_norm + nt(grad_hidden, w1_ref[:, part])
    dec_ref[...] = jnp.where(valid, y3, 0.0).astype(BF)
    small_ref[4:5] = col_sum(grad)
    grad_x, small_ref[0:1], small_ref[1:2] = norm_backward(grad_norm, unit_e, scale_e, gain_ref[4:5])
    grad = grad + grad_x
    grad_low = grad.astype(BF)
    small_ref[5:6] = col_sum(grad_low)
    base = hidden_size - chunk
    early_ref[slot[1], base + 3 * width :] = nn(cross_t.astype(BF), grad_low).astype(BF)
    grad_ctx = nt(grad_low, out2_ref[...]).astype(BF)
    key_t = cross_ref[:, :width].astype(F32).T.astype(BF)
    mem_t = mem_ref[...].astype(F32).T.astype(BF)
    dkeys = []
    dvalues = []
    dquery = []
    for pair in range(HEADS // 2):
        dkey = 0.0
        dvalue = 0.0
        for head in (2 * pair, 2 * pair + 1):
            lanes = lanes_of(head)
            own_grad = own_lanes(grad_ctx[:, lanes], head)
            prob = probs[head]
            dprob = nt(cross_ref[:, slice(width + lanes.start, width + lanes.stop)], own_grad)
            inner = jnp.sum(dprob * prob, axis=0, keepdims=True)
            dscore = (prob * (dprob - inner)).astype(BF)
            dvalue = dvalue + nn(prob.astype(BF), own_grad)
            dkey = dkey + nn(dscore, own_lanes(scaled[:, lanes], head))
            dquery.append(nn(key_t[rows_of(head)], dscore))
        dkeys.append(dkey.astype(BF))
        dvalues.append(dvalue.astype(BF))
    dq_t = jnp.concatenate(dquery, axis=0) * HEAD_DIM**-0.5
    dq = dq_t.T.astype(BF)
    dkv = jnp.concatenate(dkeys + dvalues, axis=1)
    small_ref[6:7] = col_sum(dq)
    small_ref[7:8] = col_sum(dkv[:, width:])
    norm_d = norm_d_ref[...]
    early_ref[slot[1], base : base + width] = nn(norm_d.astype(F32).T.astype(BF), dq).astype(BF)
    pairs = nn(mem_t, dkv).astype(BF)
    early_ref[slot[1], base + width : base + 2 * width] = pairs[:, :width]
    early_ref[slot[1], base + 2 * width : base + 3 * width] = pairs[:, width:]
    dmem_ref[...] = nt(dkv, in2_ref[:, width:]).astype(BF)
    unit, scale = normalise(y1_ref[...])
    grad_x, small_ref[8:9], small_ref[9:10] = norm_backward(
        nt(dq, in2_ref[:, :width]), unit, scale, gain_ref[3:4]
    )
    grad_ref[...] = grad + grad_x


def decoder_self_backward(
    emb_ref, norm_c_ref, qkv_ref, ctx_t_ref, prob_ref, grad_ref, small_ref, gain_ref, in1_ref, out1_ref,
    late_ref, swap_ref,
):
    text, width = emb_ref.shape
    grad = grad_ref[...]
    grad_low = grad.astype(BF)
    small_ref[10:11] = col_sum(grad_low)
    dout1 = nn(ctx_t_ref[...], grad_low).astype(BF)
    late_ref[3 * width :] = dout1[: width - SPILL]
    swap_ref[text + SMALL :] = dout1[width - SPILL :]
    grad_ctx = nt(grad_low, out1_ref[...]).astype(BF)
    key_t = qkv_ref[:, width : 2 * width].astype(F32).T.astype(BF)
    scaled = qkv_ref[:, :width] * jnp.asarray(HEAD_DIM**-0.5, BF)
    dkeys = []
    dvalues = []
    dquery = []
    for pair in range(HEADS // 2):
        dkey = 0.0
        dvalue = 0.0
        for head in (2 * pair, 2 * pair + 1):
            lanes = lanes_of(head)
            own_grad = own_lanes(grad_ctx[:, lanes], head)
            prob = prob_ref[head]
            dprob = nt(qkv_ref[:, slice(2 * width + lanes.start, 2 * width + lanes.stop)], own_grad)
            inner = jnp.sum(dprob * prob, axis=0, keepdims=True)
            dscore = (prob * (dprob - inner)).astype(BF)
            dvalue = dvalue + nn(prob.astype(BF), own_grad)
            dkey = dkey + nn(dscore, own_lanes(scaled[:, lanes], head))
            dquery.append(nn(key_t[rows_of(head)], dscore))
        dkeys.append(dkey.astype(BF))
        dvalues.append(dvalue.astype(BF))
    dq_t = jnp.concatenate(dquery, axis=0) * HEAD_DIM**-0.5
    dqkv = jnp.concatenate([dq_t.T.astype(BF)] + dkeys + dvalues, axis=1)
    small_ref[11:12] = col_sum(dqkv[:, :width])
    small_ref[12:13] = col_sum(dqkv[:, 2 * width :])
    din1 = nn(norm_c_ref[...].astype(F32).T.astype(BF), dqkv).astype(BF)
    for part in range(3):
        late_ref[width * part : width * part + width] = din1[:, width * part : width * part + width]
    unit, scale = normalise(emb_ref[...].astype(F32) * math.sqrt(width))
    grad_x, small_ref[13:14], small_ref[14:15] = norm_backward(
        nt(dqkv, in1_ref[...]), unit, scale, gain_ref[2:3]
    )
    swap_ref[:text] = ((grad + grad_x) * math.sqrt(width)).astype(BF)
    swap_ref[text : text + SMALL] = small_ref[...].astype(BF)


def forward_and_decoder(
    tok_ref, len_ref, at_ref, core_ref,
    x_ref, emb_ref, y1_ref, norm_c_ref, dec_qkv_ref, dec_ctx_t_ref, prob_ref, norm_d_ref, cross_q_ref,
    cot_ref, gain_ref, shift_ref, in_ref, in_b_ref, out_ref, out_b_ref, w1_ref, b1_ref, w2_ref, b2_ref,
    qkv_ref, ctx_t_ref, lse_ref, h1_ref, dec_ref, dmem_ref, late_ref, swap_ref, keep_ref, send_ref,
    key_aug, value_t, act, mem, cross, probs, grad, small, early, sems,
):
    in0, in1, in2 = (in_ref.at[i] for i in range(3))
    out0, out1, out2 = (out_ref.at[i] for i in range(3))
    encoder_forward(
        len_ref, at_ref, x_ref, gain_ref, shift_ref, in0, in_b_ref, out0, out_b_ref,
        w1_ref.at[0], b1_ref, w2_ref.at[0], b2_ref, in2,
        qkv_ref, ctx_t_ref, lse_ref, h1_ref, mem, cross,
        key_aug, value_t, act,
    )
    decoder_main(
        tok_ref, len_ref, at_ref, core_ref,
        y1_ref, norm_d_ref, cross_q_ref, cross, mem, cot_ref, gain_ref, shift_ref,
        in2, out2, out_b_ref, w1_ref.at[1], b1_ref, w2_ref.at[1], b2_ref,
        dec_ref, dmem_ref, early, grad, small,
        probs,
    )
    decoder_self_backward(
        emb_ref, norm_c_ref, dec_qkv_ref, dec_ctx_t_ref, prob_ref, grad, small, gain_ref, in1, out1,
        late_ref, swap_ref,
    )
    half = early.shape[1]
    hand_out(
        sems, (early.at[0], keep_ref), (early.at[1], send_ref.at[:half]), (swap_ref, send_ref.at[half:])
    )


def encoder_backward(
    len_ref, at_ref, core_ref,
    x_ref, h1_ref, dmem_ref, ctx_t_ref, qkv_ref, lse_ref, late_ref, gain_ref, shift_ref,
    in_ref, out_ref, w1_ref, b1_ref, w2_ref,
    dx_ref, keep_ref, send_ref,
    grad_hid, dh1, dctx, key_aug, key_t, dq_t, dqkv, small, feed, attn, sems,
):
    encoder_feed_backward(
        core_ref, h1_ref, dmem_ref, ctx_t_ref, gain_ref, shift_ref, w1_ref, b1_ref, w2_ref, out_ref, late_ref,
        dh1, dctx, feed, small,
        grad_hid,
    )
    encoder_attention_backward(
        len_ref, at_ref, core_ref, x_ref, qkv_ref, lse_ref, dctx, dh1, gain_ref, shift_ref, in_ref,
        dx_ref, attn,
        key_aug, key_t, dq_t, dqkv, small,
    )
    cut = feed.shape[1]
    hand_out(
        sems, (feed.at[0], keep_ref.at[:cut]), (attn.at[0], keep_ref.at[cut:]),
        (feed.at[1], send_ref.at[:cut]), (attn.at[1], send_ref.at[cut:]),
    )


def fetch(sems, *pairs):
    copies = [pltpu.make_async_copy(ref, held, sems.at[i]) for i, (ref, held) in enumerate(pairs)]
    for copy in copies:
        copy.start()
    return copies


def early_merge(
    core_ref, ids_ref, swap_ref, keep_ref, other_ref, out_ref, keep, other, swapped_ref, out, sems, out_sems
):
    core = core_ref[0]
    text = ids_ref.shape[1] // 2
    half = keep.shape[0]
    chunk = half // 4
    loads = fetch(sems, (other_ref.at[half:], swapped_ref), (keep_ref, keep), (other_ref.at[:half], other))
    loads[0].wait()
    grad = jnp.concatenate([swap_ref[:text], swapped_ref[:text]], axis=0)
    for at in range(0, half, chunk):
        row = lax.broadcasted_iota(jnp.int32, (chunk, 2 * text), 0) + (core * half + at)
        hot = jnp.where(row == ids_ref[...], 1.0, 0.0).astype(BF)
        out[half + at : half + at + chunk] = nn(hot, grad).astype(BF)

    @pl.when(core == 1)
    def _():
        rest = swap_ref[text:].astype(F32) + swapped_ref[text:].astype(F32)
        out[2 * half - rest.shape[0] :] = rest.astype(BF)

    table = pltpu.make_async_copy(out.at[half:], out_ref.at[half:], out_sems.at[0])
    table.start()
    for load in loads[1:]:
        load.wait()
    out[:half] = (keep[...].astype(F32) + other[...].astype(F32)).astype(BF)
    sums = pltpu.make_async_copy(out.at[:half], out_ref.at[:half], out_sems.at[1])
    sums.start()
    table.wait()
    sums.wait()


def late_merge(keep_ref, other_ref, early_ref, out_ref, keep, other, early, out, sems, out_sems):
    count, size, width = out.shape
    size = size - early.shape[1]
    loads = fetch(sems, (early_ref, early), (keep_ref, keep), (other_ref, other))
    loads[0].wait()
    own = jnp.sum(early[...].astype(F32), axis=0).astype(BF)
    for load in loads[1:]:
        load.wait()
    stores = []
    part = count // 4
    for step in range(4):
        rows = slice(step * part * size, (step + 1) * part * size)
        places = slice(step * part, step * part + part)
        late = (keep[rows].astype(F32) + other[rows].astype(F32)).astype(BF)
        out[places, :size] = late.reshape(part, size, width)
        for place in range(step * part, step * part + part):
            out[place, size:] = own
        stores.append(pltpu.make_async_copy(out.at[places], out_ref.at[places], out_sems.at[step]))
        stores[-1].start()
    for store in stores:
        store.wait()


def late_spread(parts_ref, out_ref, parts, out, sems, out_sems):
    size = out.shape[1]
    half = out.shape[0] // 2
    ends = (slice(0, half), slice(half, 2 * half))
    loads = fetch(sems, *[(parts_ref.at[end, :size], parts.at[end]) for end in ends])
    total = 0.0
    for load, end in zip(loads, ends):
        load.wait()
        total = total + jnp.sum(parts[end].astype(F32), axis=0)
    late = total.astype(BF)
    stores = []
    for step, end in enumerate(ends):
        for place in range(end.start, end.stop):
            out[place] = late
        stores.append(pltpu.make_async_copy(out.at[end], out_ref.at[end], out_sems.at[step]))
        stores[-1].start()
    for store in stores:
        store.wait()


def early_outputs(core_ref, rate_ref, mine_ref, other_ref, table_ref, in_ref, out_ref, w1_ref, w2_ref, rest_ref):
    rate = rate_ref[0]
    first = core_ref[0] == 0
    count, size, width = mine_ref.shape
    blocks = w1_ref.shape[1] // width
    half = in_ref.shape[0] * 2 + w2_ref.shape[0]
    skip = size - 2 * half // count

    def rows(core, part):
        at = slice(count // 2 * part, count // 2 * (part + 1))
        mine, other = mine_ref[at, skip:], other_ref[at, skip:]
        picked = jnp.where(first, mine, other) if core == 0 else jnp.where(first, other, mine)
        return picked.reshape(half, width)

    table_ref[:half] = rows(0, 1).astype(F32) * rate
    rest = rows(1, 1)
    table_ref[half:] = rest[: table_ref.shape[0] - half].astype(F32) * rate
    rest_ref[...] = rest[half - rest_ref.shape[0] :]
    grads = jnp.concatenate([rows(0, 0), rows(1, 0)], axis=0).astype(F32) * rate
    for block in range(blocks):
        w1_ref[:, width * block : width * block + width] = grads[width * block : width * block + width]
    w2_ref[...] = grads[width * blocks : 2 * width * blocks]
    base = 2 * width * blocks
    for part in range(3):
        in_ref[:, width * part : width * part + width] = grads[base + width * part : base + width * part + width]
    out_ref[...] = grads[base + 3 * width :]


def late_outputs(
    core_ref, rate_ref, mine_ref, other_ref, early_ref, in_in, out_in, w1_in, w2_in,
    in_ref, out_ref, w1_ref, w2_ref, gain_ref, shift_ref, in_b_ref, out_b_ref, b1_ref, b2_ref,
    mine, other, grad_in, grad_out, grad_w1, grad_w2, sems, out_sems,
):
    rate = rate_ref[0]
    first = core_ref[0] == 0
    width = mine.shape[1]
    hidden = grad_w2.shape[0]
    cut = (width - SPILL) // 2
    base = hidden + 2 * width
    ends = (slice(0, hidden), slice(hidden, mine.shape[0]))
    loads = fetch(sems, *[(ref.at[end], held.at[end]) for end in ends for ref, held in ((mine_ref, mine), (other_ref, other))])
    stores = []

    def rows(core, at, count):
        own, its = mine[at : at + count], other[at : at + count]
        picked = jnp.where(first, own, its) if core == 0 else jnp.where(first, its, own)
        return picked.astype(F32) * rate

    def hand(held, ref):
        stores.append(pltpu.make_async_copy(held, ref, out_sems.at[len(stores)]))
        stores[-1].start()

    loads[0].wait()
    loads[1].wait()
    for at in range(0, hidden, width):
        grad_w1[:, at : at + width] = rows(0, at, width)
    hand(grad_w1, w1_ref.at[0])
    grad_w2[...] = rows(1, 0, hidden)
    hand(grad_w2, w2_ref.at[0])
    loads[2].wait()
    loads[3].wait()
    grad_in[1, :, :width] = rows(0, hidden, width)
    grad_in[1, :, width : 2 * width] = rows(0, hidden + width, width)
    grad_in[1, :, 2 * width :] = rows(1, hidden, width)
    attn = jnp.concatenate(
        [rows(core, base + cut, mine.shape[0] - base - cut) for core in range(2)], axis=0
    )
    for part in range(3):
        grad_in[0, :, width * part : width * part + width] = attn[width * part : width * part + width]
    hand(grad_in, in_ref.at[0:2])
    grad_out[0] = rows(1, hidden + width, width)
    grad_out[1, :cut] = rows(0, base, cut)
    grad_out[1, cut : 2 * cut] = rows(1, base, cut)
    grad_out[1, 2 * cut :] = early_ref[SMALL:].astype(F32) * rate
    hand(grad_out, out_ref.at[0:2])
    enc = attn[3 * width : 3 * width + SMALL]
    dec = early_ref[:SMALL].astype(F32) * rate
    for row, (part, at) in enumerate(((enc, 0), (enc, 8), (dec, 13), (dec, 8), (dec, 0))):
        gain_ref[row : row + 1] = part[at : at + 1]
        shift_ref[row : row + 1] = part[at + 1 : at + 2]
    for row, (part, at, next_at) in enumerate(((enc, 2, 3), (dec, 11, 12), (dec, 6, 7))):
        in_b_ref[row : row + 1, :width] = part[at : at + 1]
        in_b_ref[row : row + 1, width:] = part[next_at : next_at + 1]
    for row, (part, at) in enumerate(((enc, 11), (dec, 10), (dec, 5))):
        out_b_ref[row : row + 1] = part[at : at + 1]
    for row, (part, at) in enumerate(((enc, 10), (dec, 4))):
        b2_ref[row : row + 1] = part[at : at + 1]
    for row, part in enumerate((enc, dec)):
        for block in range(hidden // width):
            b1_ref[row : row + 1, width * block : width * block + width] = part[16 + block : 17 + block]
    for store in stores:
        store.wait()


def frames_back(place_ref, own_ref, next_ref, second_ref, third_ref, out_ref):
    count = out_ref.shape[0]
    for shift, ref in enumerate((own_ref, next_ref, second_ref, third_ref)):
        out_ref[lax.rem(place_ref[0] + (count - shift), count)] = ref[...].astype(F32)


def encoder_feed_backward(
    core_ref, h1_ref, dmem_ref, ctx_t_ref, gain_ref, shift_ref, w1_ref, b1_ref, w2_ref, out_ref, late_ref,
    dh1_ref, dctx_ref, feed_ref, small_ref,
    grad_hid,
):
    width = h1_ref.shape[1]
    hidden_size = w1_ref.shape[1]
    slot = (core_ref[0], 1 - core_ref[0])
    cut = (width - SPILL) // 2
    feed_ref[slot[0], hidden_size : hidden_size + 2 * width] = late_ref[: 2 * width]
    feed_ref[slot[1], hidden_size : hidden_size + width] = late_ref[2 * width : 3 * width]
    feed_ref[slot[0], hidden_size + 2 * width :] = late_ref[3 * width : 3 * width + cut]
    feed_ref[slot[1], hidden_size + 2 * width :] = late_ref[3 * width + cut :]
    small_ref[...] = jnp.zeros_like(small_ref)
    unit, _ = normalise(h1_ref[...])
    norm_b = unit * gain_ref[1:2] + shift_ref[1:2]
    norm_b_t = norm_b.T.astype(BF)
    norm_b = norm_b.astype(BF)
    grad_low = dmem_ref[...]
    grad_low_t = grad_low.astype(F32).T.astype(BF)
    hidden = nn(norm_b, w1_ref[...]) + b1_ref[0:1]
    value, slope = gelu_both(hidden)
    grad_hidden = (nt(grad_low, w2_ref[...]) * slope).astype(BF)
    grad_hid[...] = grad_hidden
    bias = col_sum(grad_hidden)
    first = nn(norm_b_t, grad_hidden).astype(BF)
    for block in range(hidden_size // width):
        part = slice(width * block, width * block + width)
        small_ref[16 + block : 17 + block] = bias[:, part]
        feed_ref[slot[0], part] = first[:, part]
    feed_ref[slot[1], :hidden_size] = nn(grad_low_t, value.astype(BF)).T.astype(BF)
    grad = grad_low.astype(F32)
    small_ref[10:11] = col_sum(grad)
    unit, scale = normalise(h1_ref[...])
    grad_x, small_ref[8:9], small_ref[9:10] = norm_backward(
        nt(grad_hid[...], w1_ref[...]), unit, scale, gain_ref[1:2]
    )
    grad = grad + grad_x
    dh1_ref[...] = grad
    grad_low = grad.astype(BF)
    small_ref[11:12] = col_sum(grad_low)
    feed_ref[slot[1], hidden_size + width : hidden_size + 2 * width] = nn(ctx_t_ref[...], grad_low).astype(BF)
    dctx_ref[...] = nt(grad_low, out_ref[...]).astype(BF)


def encoder_attention_backward(
    len_ref, at_ref, core_ref, x_ref, qkv_ref, lse_ref, dctx_ref, dh1_ref, gain_ref, shift_ref, in_ref,
    dx_ref, attn_ref,
    key_aug, key_t, dq_t, dqkv, small_ref,
):
    rows, width = x_ref.shape
    for head in range(HEADS):
        lanes = lanes_of(head)
        key_aug[head] = with_mask(qkv_ref[:, slice(width + lanes.start, width + lanes.stop)], head, len_ref[at_ref[0]])
    key_t[...] = qkv_ref[:, width : 2 * width].astype(F32).T.astype(BF)
    for pair in range(HEADS // 2):
        dkey = 0.0
        dvalue = 0.0
        for head in (2 * pair, 2 * pair + 1):
            lanes = lanes_of(head)
            query = own_lanes(qkv_ref[:, lanes] * jnp.asarray(HEAD_DIM**-0.5, BF), head)
            score = nt(key_aug[head], with_one(query, head))
            prob = jnp.exp(score - lse_ref[head : head + 1])
            own_grad = own_lanes(dctx_ref[:, lanes], head)
            dprob = nt(qkv_ref[:, slice(2 * width + lanes.start, 2 * width + lanes.stop)], own_grad)
            inner = jnp.sum(dprob * prob, axis=0, keepdims=True)
            dscore = (prob * (dprob - inner)).astype(BF)
            dkey = dkey + nn(dscore, query)
            dvalue = dvalue + nn(prob.astype(BF), own_grad)
            dq_t[rows_of(head)] = nn(key_t[rows_of(head)], dscore)
        dqkv[:, slice(width + lanes.start, width + lanes.stop)] = dkey.astype(BF)
        dqkv[:, slice(2 * width + lanes.start, 2 * width + lanes.stop)] = dvalue.astype(BF)
    dqkv[:, :width] = (dq_t[...].T * HEAD_DIM**-0.5).astype(BF)
    small_ref[2:3] = col_sum(dqkv[:, :width])
    small_ref[3:4] = col_sum(dqkv[:, 2 * width :])
    unit, scale = normalise(x_ref[...].astype(F32))
    norm_a = unit * gain_ref[0:1] + shift_ref[0:1]
    din = nn(norm_a.T.astype(BF), dqkv[...]).astype(BF)
    blocks = [din[:, width * part : width * part + width] for part in range(3)]
    grad_x, small_ref[0:1], small_ref[1:2] = norm_backward(
        nt(dqkv[...], in_ref[...]), unit, scale, gain_ref[0:1]
    )
    dx_ref[...] = (dh1_ref[...] + grad_x).astype(BF)
    small = small_ref[...].astype(BF)
    packed = jnp.concatenate(blocks + [small, jnp.zeros_like(small)], axis=0)
    half = attn_ref.shape[1]
    attn_ref[core_ref[0]] = packed[:half]
    attn_ref[1 - core_ref[0]] = packed[half:]


def swap_cores(array):
    return lax.ppermute(array, "core", [(0, 1), (1, 0)])


def body(
    frames, utt_len, token_ids, tok_len, step, embed, norm_gain, norm_bias, attn_in, attn_in_bias,
    attn_out, attn_out_bias, ff_in, ff_in_bias, ff_out, ff_out_bias, cotangent,
):
    ring = ("frame", "pair")
    devices = lax.axis_size(ring)
    core = lax.axis_index("core")
    core_of = core[None]
    frame_at = lax.axis_index("frame")
    vocab, width = embed.shape
    hidden = ff_in.shape[2]
    frame_count = lax.axis_size("frame")
    local_len = frames.shape[2]
    rows = local_len * frame_count
    text = token_ids.shape[2]
    lengths = utt_len[0]
    frame_of = frame_at[None]
    my_tok = tok_len[0]
    arrived = lax.all_to_all(frames[0], "frame", split_axis=0, concat_axis=1, tiled=True)
    source = arrived.reshape(rows, width)
    ids = token_ids[0, 0]
    both_ids = jnp.concatenate([ids, swap_cores(ids)])[None]
    rows_in, both_ids = lax.optimization_barrier((embed[ids], both_ids))
    count_step = step[0].astype(F32)
    rate = jnp.minimum(lax.rsqrt(count_step), count_step * WARMUP ** (-1.5)) * WARMUP**0.5
    rate = rate[None]

    y1, norm_c, dec_qkv, dec_ctx_t, dec_prob, norm_d, cross_q = call(
        decoder_start,
        [
            ((text, width), F32), ((text, width), BF), ((text, 3 * width), BF), ((width, text), BF),
            ((HEADS, text, text), F32), ((text, width), BF), ((text, width), BF),
        ],
        [
            rows_in, norm_gain, norm_bias, (attn_in, 1), attn_in_bias, (attn_out, 1),
            attn_out_bias, (attn_in, 2),
        ],
        [my_tok],
        flops=2 * text * width * width * 5,
    )
    half = 2 * width + hidden
    swap_rows = text + SMALL + SPILL
    enc_qkv, enc_ctx_t, lse, h1, dec_out, dmem, self_grads, swap, early, early_send = call(
        forward_and_decoder,
        [
            ((rows, 3 * width), BF), ((width, rows), BF), ((8, rows), F32), ((rows, width), F32),
            ((text, width), BF), ((rows, width), BF), ((4 * width - SPILL, width), BF),
            ((swap_rows, width), BF), ((half, width), BF, None), ((half + swap_rows, width), BF, None),
        ],
        [
            source, rows_in, y1, norm_c, dec_qkv, dec_ctx_t, dec_prob, norm_d, cross_q, cotangent[0, 0],
            norm_gain, norm_bias, attn_in, attn_in_bias, attn_out, attn_out_bias, ff_in, ff_in_bias,
            ff_out, ff_out_bias,
        ],
        [my_tok, lengths, frame_of, core_of],
        [
            pltpu.VMEM((HEADS, rows, 128), BF), pltpu.VMEM((width, rows), BF),
            pltpu.VMEM((rows, hidden), BF), pltpu.VMEM((rows, width), BF), pltpu.VMEM((rows, 2 * width), BF),
            pltpu.VMEM((HEADS, rows, text), F32), pltpu.VMEM((text, width), F32),
            pltpu.VMEM((SMALL, width), F32), pltpu.VMEM((2, half, width), BF),
            pltpu.SemaphoreType.DMA((3,)),
        ],
        flops=2 * rows * width * (10 * width + 2 * rows + 2 * hidden)
        + 2 * text * width * (6 * hidden + 7 * rows + 26 * width),
    )
    (early_sum,) = call(
        early_merge,
        [((2 * half, width), BF, None)],
        [both_ids, swap, (early, None), (swap_cores(early_send), None)],
        [core_of],
        [
            pltpu.VMEM((half, width), BF), pltpu.VMEM((half, width), BF), pltpu.VMEM((swap_rows, width), BF),
            pltpu.VMEM((2 * half, width), BF),
            pltpu.SemaphoreType.DMA((3,)), pltpu.SemaphoreType.DMA((2,)),
        ],
        flops=4 * half * width * text,
    )
    early_sum, dmem = lax.optimization_barrier((early_sum, dmem))
    early_parts = lax.all_to_all(
        early_sum.reshape(devices, -1, width), ring, split_axis=0, concat_axis=0, tiled=True
    )
    early_own = jnp.sum(early_parts.astype(F32), axis=0).astype(BF)

    feed_half = (5 * width - SPILL) // 2 + hidden
    attn_half = 3 * width // 2 + SMALL
    late_half = feed_half + attn_half
    dx, late, late_send = call(
        encoder_backward,
        [((rows, width), BF), ((late_half, width), BF, None), ((late_half, width), BF, None)],
        [
            source, h1, dmem, enc_ctx_t, enc_qkv, lse, self_grads, norm_gain, norm_bias, (attn_in, 0),
            (attn_out, 0), (ff_in, 0), ff_in_bias, (ff_out, 0),
        ],
        [lengths, frame_of, core_of],
        [
            pltpu.VMEM((rows, hidden), BF), pltpu.VMEM((rows, width), F32), pltpu.VMEM((rows, width), BF),
            pltpu.VMEM((HEADS, rows, 128), BF), pltpu.VMEM((width, rows), BF),
            pltpu.VMEM((width, rows), F32), pltpu.VMEM((rows, 3 * width), BF),
            pltpu.VMEM((SMALL, width), F32), pltpu.VMEM((2, feed_half, width), BF),
            pltpu.VMEM((2, attn_half, width), BF), pltpu.SemaphoreType.DMA((4,)),
        ],
        flops=2 * rows * width * (5 * hidden + 5 * rows + 8 * width),
    )
    late_size = late_half // devices
    early_size = 2 * half // devices
    mixed_shape = (devices, late_size + early_size, width)
    (mixed,) = call(
        late_merge,
        [(mixed_shape, BF, None)],
        [(late, None), (swap_cores(late_send), None), (early_parts, None)],
        scratch=[
            pltpu.VMEM((late_half, width), BF), pltpu.VMEM((late_half, width), BF),
            pltpu.VMEM((devices, early_size, width), BF), pltpu.VMEM(mixed_shape, BF),
            pltpu.SemaphoreType.DMA((3,)), pltpu.SemaphoreType.DMA((4,)),
        ],
    )
    mixed = lax.all_to_all(mixed, ring, split_axis=0, concat_axis=0, tiled=True)
    chunks = dx.reshape(frame_count, local_len, width)
    moved = []
    for shift in range(frame_count):
        target = lax.rem(frame_at + shift, frame_count)
        chunk = lax.dynamic_index_in_dim(chunks, target, keepdims=False)
        if shift:
            chunk = lax.ppermute(chunk, "frame", [(i, (i + shift) % frame_count) for i in range(frame_count)])
        moved.append(chunk)
    mixed, moved = lax.optimization_barrier((mixed, moved))
    late_shape = (devices, late_size, width)
    (late_own,) = call(
        late_spread,
        [(late_shape, BF, None)],
        [(mixed, None)],
        scratch=[
            pltpu.VMEM(late_shape, BF), pltpu.VMEM(late_shape, BF),
            pltpu.SemaphoreType.DMA((2,)), pltpu.SemaphoreType.DMA((2,)),
        ],
    )
    early_other = swap_cores(mixed)
    (frames_grad,) = call(
        frames_back, [((frame_count, local_len, width), F32)], moved, [frame_of]
    )
    late_mine = lax.all_to_all(late_own, ring, split_axis=0, concat_axis=0, tiled=True)
    in_shape = (3, width, 3 * width)
    out_shape = (3, width, width)
    w1_shape = (2, width, hidden)
    w2_shape = (2, hidden, width)
    table_grad, in_grad, out_grad, w1_grad, w2_grad, early_rest = call(
        early_outputs,
        [
            ((vocab, width), F32), (in_shape, F32, None, 2), (out_shape, F32, None, 2),
            (w1_shape, F32, None, 1), (w2_shape, F32, None, 1), ((SMALL + SPILL, width), BF),
        ],
        [mixed, early_other],
        [core_of, rate],
    )
    late_mine, early_rest, frames_grad = lax.optimization_barrier((late_mine, early_rest, frames_grad))
    late_mine = late_mine.reshape(late_half, width)
    late_other = swap_cores(late_mine)

    in_grad, out_grad, w1_grad, w2_grad, gain_grad, shift_grad, in_b_grad, out_b_grad, b1_grad, b2_grad = call(
        late_outputs,
        [
            (in_shape, F32, None), (out_shape, F32, None), (w1_shape, F32, None), (w2_shape, F32, None),
            ((5, width), F32), ((5, width), F32), ((3, 2 * width), F32), ((3, width), F32),
            ((2, hidden), F32), ((2, width), F32),
        ],
        [
            (late_mine, None), (late_other, None), early_rest, (in_grad, None), (out_grad, None),
            (w1_grad, None), (w2_grad, None),
        ],
        [core_of, rate],
        [
            pltpu.VMEM((late_half, width), BF), pltpu.VMEM((late_half, width), BF),
            pltpu.VMEM((2,) + in_shape[1:], F32), pltpu.VMEM((2,) + out_shape[1:], F32),
            pltpu.VMEM(w1_shape[1:], F32), pltpu.VMEM(w2_shape[1:], F32),
            pltpu.SemaphoreType.DMA((4,)), pltpu.SemaphoreType.DMA((4,)),
        ],
        aliases={5: 0, 6: 1, 7: 2, 8: 3},
    )
    return (
        dec_out[None, None],
        frames_grad[None],
        table_grad,
        gain_grad,
        shift_grad,
        in_grad,
        in_b_grad,
        out_grad,
        out_b_grad,
        w1_grad,
        b1_grad,
        w2_grad,
        b2_grad,
    )


def solution(mesh):
    groups = ("pair", "core")
    frames, batch = mesh.devices.shape
    split = Mesh(mesh.devices.reshape(frames, batch // 2, 2), ("frame",) + groups)
    placed = (
        P(groups, None, "frame", None),
        P(groups, None),
        P(groups, "frame", None),
        P(groups, "frame"),
    ) + (P(),) * 12 + (P(groups, "frame", None, None),)
    results = (P(groups, "frame", None, None), P(groups, None, "frame", None)) + (P(),) * 11
    return jax.shard_map(body, mesh=split, in_specs=placed, out_specs=results, check_vma=False)
```

```python
import functools
import math

import jax
import jax.numpy as jnp
from jax import lax
from jax.experimental import pallas as pl
from jax.experimental.pallas import tpu as pltpu
from jax.sharding import Mesh, PartitionSpec as P

HEADS = 4
HEAD_DIM = 64
WARMUP = 25000
EPSILON = 1e-05
MASKED = -1e30
BF = jnp.bfloat16
F32 = jnp.float32
GELU_A = math.sqrt(2.0 / math.pi)
GELU_B = GELU_A * 0.044715
SMALL = 32
FEED_CHUNK = 1024
SPILL = 64


def nn(left, right):
    return lax.dot_general(left, right, (((1,), (0,)), ((), ())), preferred_element_type=F32)


def nt(left, right):
    return lax.dot_general(left, right, (((1,), (1,)), ((), ())), preferred_element_type=F32)


def hand_out(sems, *pairs):
    copies = [pltpu.make_async_copy(held, ref, sems.at[i]) for i, (held, ref) in enumerate(pairs)]
    for copy in copies:
        copy.start()
    for copy in copies:
        copy.wait()


def normalise(states):
    average = jnp.mean(states, axis=-1, keepdims=True)
    centred = states - average
    scale = lax.rsqrt(jnp.mean(centred * centred, axis=-1, keepdims=True) + EPSILON)
    return centred * scale, scale


def norm_backward(grad, unit, scale, gain):
    grad_unit = grad * gain
    mean_grad = jnp.mean(grad_unit, axis=-1, keepdims=True)
    mean_along = jnp.mean(grad_unit * unit, axis=-1, keepdims=True)
    grad_states = scale * (grad_unit - mean_grad - unit * mean_along)
    return grad_states, col_sum(grad * unit), col_sum(grad)


def col_sum(matrix):
    return jnp.sum(matrix.astype(F32), axis=0, keepdims=True)


def gelu_value(hidden):
    inner = hidden * (GELU_A + GELU_B * (hidden * hidden))
    return hidden * (0.5 + 0.5 * jnp.tanh(inner))


def gelu_both(hidden):
    square = hidden * hidden
    bent = jnp.tanh(hidden * (GELU_A + GELU_B * square))
    half = 0.5 + 0.5 * bent
    slope = half + (0.5 * hidden) * (1.0 - bent * bent) * (GELU_A + 3.0 * GELU_B * square)
    return hidden * half, slope


def lanes_of(head):
    return slice(128 * (head // 2), 128 * (head // 2) + 128)


def rows_of(head):
    return slice(HEAD_DIM * head, HEAD_DIM * head + HEAD_DIM)


def each_pair(step):
    def body(pair, carry):
        step(pl.multiple_of(pair * 2 * HEAD_DIM, 2 * HEAD_DIM), pair)
        return carry

    lax.fori_loop(0, HEADS // 2, body, 0)


def head_rows(at, odd):
    return pl.ds(pl.multiple_of(at + HEAD_DIM * odd, HEAD_DIM), HEAD_DIM)


def own_lanes(pair, head):
    lane = lax.broadcasted_iota(jnp.int32, pair.shape, 1)
    mine = (lane < HEAD_DIM) if head % 2 == 0 else (lane >= HEAD_DIM)
    return jnp.where(mine, pair, jnp.zeros_like(pair))


def spare_lane(head):
    return HEAD_DIM if head % 2 == 0 else 0


def with_one(query, head):
    lane = lax.broadcasted_iota(jnp.int32, query.shape, 1)
    return jnp.where(lane == spare_lane(head), jnp.ones_like(query), query)


def with_mask(key_pair, head, length):
    lane = lax.broadcasted_iota(jnp.int32, key_pair.shape, 1)
    row = lax.broadcasted_iota(jnp.int32, key_pair.shape, 0)
    bias = jnp.where(row < length, 0.0, MASKED).astype(BF)
    return jnp.where(lane == spare_lane(head), bias, key_pair)


def part_spec(shape, layers, at):
    index = (at,) + (0,) * (len(shape) - 1)
    return pl.BlockSpec((layers,) + shape[1:], lambda *g: index, pipeline_mode=pl.Buffered(1))


def call(kernel, outs, args, scalars=(), scratch=(), flops=0, aliases=None, limit=61):
    in_specs = []
    for a in args:
        if not isinstance(a, tuple):
            in_specs.append(part_spec(a.shape, a.shape[0], 0))
        elif a[1] is None or a[1] == "vmem":
            in_specs.append(pl.BlockSpec(memory_space=pl.ANY))
        else:
            in_specs.append(part_spec(a[0].shape, None, a[1]))
    spaces = {None: pltpu.HBM, "vmem": pltpu.VMEM}
    args = [a if isinstance(a, tuple) else (a, 0) for a in args]
    args = [a[0] if isinstance(a[1], int) else pltpu.with_memory_space_constraint(a[0], spaces[a[1]]) for a in args]
    out_specs = []
    for out in outs:
        if out[-1] is None:
            out_specs.append(pl.BlockSpec(memory_space=pltpu.HBM))
        elif isinstance(out[-1], int):
            out_specs.append(part_spec(out[0], out[2], out[3]))
        else:
            out_specs.append(part_spec(out[0], out[0][0], 0))
    size = sum(a.size * a.dtype.itemsize for a in args)
    size += sum(math.prod(out[0]) * jnp.dtype(out[1]).itemsize for out in outs)
    return pl.pallas_call(
        kernel,
        grid_spec=pltpu.PrefetchScalarGridSpec(
            num_scalar_prefetch=len(scalars),
            grid=(1,),
            in_specs=in_specs,
            out_specs=out_specs,
            scratch_shapes=list(scratch),
        ),
        out_shape=[
            (pltpu.HBM if out[-1] is None else jax.ShapeDtypeStruct)(out[0], out[1]) for out in outs
        ],
        input_output_aliases=aliases or {},
        compiler_params=pltpu.CompilerParams(vmem_limit_bytes=limit * 1024 * 1024),
        cost_estimate=pl.CostEstimate(flops=flops, bytes_accessed=size, transcendentals=0),
        name=kernel.__name__,
    )(*scalars, *args)


def decoder_start(
    tok_ref, emb_ref, gain_ref, shift_ref, in_ref, in_b_ref, out_ref, out_b_ref, cross_ref,
    y1_ref, norm_c_ref, qkv_ref, ctx_t_ref, prob_ref, norm_d_ref, cross_q_ref,
):
    text = emb_ref.shape[0]
    width = emb_ref.shape[1]
    start = emb_ref[...].astype(F32) * math.sqrt(width)
    unit, _ = normalise(start)
    norm_c = (unit * gain_ref[2:3] + shift_ref[2:3]).astype(BF)
    norm_c_ref[...] = norm_c
    flat = nn(norm_c, in_ref[...])
    query = (flat[:, :width] + in_b_ref[1:2, :width]).astype(BF)
    key = flat[:, width : 2 * width].astype(BF)
    value = (flat[:, 2 * width :] + in_b_ref[1:2, width:]).astype(BF)
    qkv_ref[:, :width] = query
    qkv_ref[:, width : 2 * width] = key
    qkv_ref[:, 2 * width :] = value
    value_t = value.astype(F32).T.astype(BF)
    key_at = lax.broadcasted_iota(jnp.int32, (text, text), 0)
    query_at = lax.broadcasted_iota(jnp.int32, (text, text), 1)
    seen = jnp.logical_and(key_at <= query_at, key_at < tok_ref[0])
    scaled = query * jnp.asarray(HEAD_DIM**-0.5, BF)
    parts = []
    for head in range(HEADS):
        lanes = lanes_of(head)
        score = nt(key[:, lanes], own_lanes(scaled[:, lanes], head))
        score = jnp.where(seen, score, MASKED)
        weight = jnp.exp(score - jnp.max(score, axis=0, keepdims=True))
        prob = weight / jnp.sum(weight, axis=0, keepdims=True)
        prob_ref[head] = prob
        parts.append(nn(value_t[rows_of(head)], prob.astype(BF)))
    ctx_t = jnp.concatenate(parts, axis=0)
    ctx_t_ref[...] = ctx_t.astype(BF)
    y1 = start + nn(ctx_t.T.astype(BF), out_ref[...]) + out_b_ref[1:2]
    y1_ref[...] = y1
    unit, _ = normalise(y1)
    norm_d = (unit * gain_ref[3:4] + shift_ref[3:4]).astype(BF)
    norm_d_ref[...] = norm_d
    cross_q_ref[...] = (nn(norm_d, cross_ref[:, :width]) + in_b_ref[2:3, :width]).astype(BF)


def encoder_forward(
    len_ref, at_ref, x_ref, gain_ref, shift_ref, in_ref, in_b_ref, out_ref, out_b_ref,
    w1_ref, b1_ref, w2_ref, b2_ref, cin_ref,
    qkv_ref, ctx_t_ref, lse_ref, h1_ref, mem_ref, cross_ref,
    value_t, act, between,
):
    rows, width = x_ref.shape
    unit, _ = normalise(x_ref[...].astype(F32))
    norm_a = (unit * gain_ref[0:1] + shift_ref[0:1]).astype(BF)
    qkv_ref[:, :width] = (nn(norm_a, in_ref[:, :width]) + in_b_ref[0:1, :width]).astype(BF)
    key = nn(norm_a, in_ref[:, width : 2 * width]).astype(BF)
    qkv_ref[:, width : 2 * width] = key
    value = (nn(norm_a, in_ref[:, 2 * width :]) + in_b_ref[0:1, width:]).astype(BF)
    qkv_ref[:, 2 * width :] = value
    value_t[...] = value.astype(F32).T.astype(BF)

    def attend(at, pair):
        keys = qkv_ref[:, pl.ds(width + at, 128)]
        queries = qkv_ref[:, pl.ds(at, 128)] * jnp.asarray(HEAD_DIM**-0.5, BF)
        for odd in range(2):
            query = with_one(own_lanes(queries, odd), odd)
            score = nt(with_mask(keys, odd, len_ref[at_ref[0]]), query)
            highest = jnp.max(score, axis=0, keepdims=True)
            weight = jnp.exp(score - highest)
            total = jnp.sum(weight, axis=0, keepdims=True)
            context = nn(value_t[head_rows(at, odd)], weight.astype(BF)) * (1.0 / total)
            ctx_t_ref[head_rows(at, odd)] = context.astype(BF)
            lse_ref[pl.ds(2 * pair + odd, 1)] = highest + jnp.log(total)

    each_pair(attend)
    context = ctx_t_ref[...].astype(F32).T.astype(BF)
    h1 = x_ref[...].astype(F32) + nn(context, out_ref[...]) + out_b_ref[0:1]
    h1_ref[...] = h1
    between()
    unit, _ = normalise(h1)
    norm_b = (unit * gain_ref[1:2] + shift_ref[1:2]).astype(BF)

    hidden = nn(norm_b, w1_ref[...]) + b1_ref[0:1]
    act[...] = gelu_value(hidden).astype(BF)
    memory = (h1_ref[...] + nn(act[...], w2_ref[...]) + b2_ref[0:1]).astype(BF)
    mem_ref[...] = memory
    cross_ref[:, :width] = nn(memory, cin_ref[:, width : 2 * width]).astype(BF)
    cross_ref[:, width:] = (nn(memory, cin_ref[:, 2 * width :]) + in_b_ref[2:3, width:]).astype(BF)


def decoder_main(
    tok_ref, len_ref, at_ref, core_ref,
    y1_ref, norm_d_ref, cross_q_ref, cross_ref, mem_ref, cot_ref, gain_ref, shift_ref,
    in2_ref, out2_ref, out_b_ref, w1_ref, b1_ref, w2_ref, b2_ref,
    dec_ref, dmem_ref, early_ref, grad_ref, small_ref,
    probs, turned, cross_t, dkv, dq_t,
):
    text, width = y1_ref.shape
    hidden_size = w1_ref.shape[1]
    slot = (core_ref[0], 1 - core_ref[0])
    small_ref[...] = jnp.zeros_like(small_ref)
    turned[...] = cross_ref[:, width:].astype(F32).T.astype(BF)

    def attend(at, pair):
        keys = cross_ref[:, pl.ds(at, 128)]
        queries = cross_q_ref[:, pl.ds(at, 128)] * jnp.asarray(HEAD_DIM**-0.5, BF)
        for odd in range(2):
            query = with_one(own_lanes(queries, odd), odd)
            score = nt(with_mask(keys, odd, len_ref[at_ref[0]]), query)
            weight = jnp.exp(score - jnp.max(score, axis=0, keepdims=True))
            prob = weight * (1.0 / jnp.sum(weight, axis=0, keepdims=True))
            probs[2 * pair + odd] = prob
            cross_t[head_rows(at, odd)] = nn(turned[head_rows(at, odd)], prob.astype(BF))

    each_pair(attend)
    context_t = cross_t[...]
    y2 = y1_ref[...] + nn(context_t.T.astype(BF), out2_ref[...]) + out_b_ref[2:3]
    unit_e, scale_e = normalise(y2)
    norm_e = (unit_e * gain_ref[4:5] + shift_ref[4:5]).astype(BF)
    norm_e_t = norm_e.astype(F32).T.astype(BF)
    valid = lax.broadcasted_iota(jnp.int32, (text, 1), 0) < tok_ref[0]
    grad_low = jnp.where(valid, cot_ref[...], jnp.zeros_like(cot_ref))
    grad = grad_low.astype(F32)
    grad_low_t = grad.T.astype(BF)
    chunk = 512

    def feed(index, sums):
        part = pl.ds(pl.multiple_of(index * chunk, chunk), chunk)
        hidden = nn(norm_e, w1_ref[:, part]) + b1_ref[1:2, part]
        value, slope = gelu_both(hidden)
        active = value.astype(BF)
        grad_hidden = (nt(grad_low, w2_ref[part]) * slope).astype(BF)
        bias = col_sum(grad_hidden)
        first = nn(norm_e_t, grad_hidden).astype(BF)
        for sub in range(chunk // width):
            row = index * (chunk // width) + sub
            small_ref[pl.ds(16 + row, 1)] = bias[:, width * sub : width * sub + width]
            at = pl.multiple_of(row * width, width)
            early_ref[slot[0], pl.ds(at, width)] = first[:, width * sub : width * sub + width]
        second = nn(grad_low_t, active).T.astype(BF)
        at = pl.multiple_of(jnp.where(index == 0, hidden_size, (index - 1) * chunk), chunk)
        early_ref[jnp.where(index == 0, slot[0], slot[1]), pl.ds(at, chunk)] = second
        return sums[0] + nn(active, w2_ref[part]), sums[1] + nt(grad_hidden, w1_ref[:, part])

    zeros = jnp.zeros((text, width), F32)
    feed_out, grad_norm = lax.fori_loop(0, hidden_size // chunk, feed, (zeros, zeros))
    y3 = y2 + b2_ref[1:2] + feed_out
    dec_ref[...] = jnp.where(valid, y3, 0.0).astype(BF)
    small_ref[4:5] = col_sum(grad)
    grad_x, small_ref[0:1], small_ref[1:2] = norm_backward(grad_norm, unit_e, scale_e, gain_ref[4:5])
    grad = grad + grad_x
    grad_low = grad.astype(BF)
    small_ref[5:6] = col_sum(grad_low)
    base = hidden_size - chunk
    early_ref[slot[1], base + 3 * width :] = nn(context_t.astype(BF), grad_low).astype(BF)
    grad_ctx = nt(grad_low, out2_ref[...]).astype(BF)
    turned[...] = cross_ref[:, :width].astype(F32).T.astype(BF)
    mem_t = mem_ref[...].astype(F32).T.astype(BF)
    grad_ref[...] = grad_ctx.astype(F32)

    def attend_backward(at, pair):
        queries = cross_q_ref[:, pl.ds(at, 128)] * jnp.asarray(HEAD_DIM**-0.5, BF)
        values = cross_ref[:, pl.ds(width + at, 128)]
        grads = grad_ref[:, pl.ds(at, 128)].astype(BF)
        dkey = 0.0
        dvalue = 0.0
        for odd in range(2):
            own_grad = own_lanes(grads, odd)
            prob = probs[2 * pair + odd]
            dprob = nt(values, own_grad)
            inner = jnp.sum(dprob * prob, axis=0, keepdims=True)
            dscore = (prob * (dprob - inner)).astype(BF)
            dvalue = dvalue + nn(prob.astype(BF), own_grad)
            dkey = dkey + nn(dscore, own_lanes(queries, odd))
            dq_t[head_rows(at, odd)] = nn(turned[head_rows(at, odd)], dscore)
        dkv[:, pl.ds(at, 128)] = dkey.astype(BF)
        dkv[:, pl.ds(width + at, 128)] = dvalue.astype(BF)

    each_pair(attend_backward)
    dq = (dq_t[...] * HEAD_DIM**-0.5).T.astype(BF)
    small_ref[6:7] = col_sum(dq)
    small_ref[7:8] = col_sum(dkv[:, width:])
    norm_d = norm_d_ref[...]
    early_ref[slot[1], base : base + width] = nn(norm_d.astype(F32).T.astype(BF), dq).astype(BF)
    pairs = nn(mem_t, dkv[...]).astype(BF)
    early_ref[slot[1], base + width : base + 2 * width] = pairs[:, :width]
    early_ref[slot[1], base + 2 * width : base + 3 * width] = pairs[:, width:]
    dmem_ref[...] = nt(dkv[...], in2_ref[:, width:]).astype(BF)
    unit, scale = normalise(y1_ref[...])
    grad_x, small_ref[8:9], small_ref[9:10] = norm_backward(
        nt(dq, in2_ref[:, :width]), unit, scale, gain_ref[3:4]
    )
    grad_ref[...] = grad + grad_x


def decoder_self_backward(
    emb_ref, norm_c_ref, qkv_ref, ctx_t_ref, prob_ref, grad_ref, small_ref, gain_ref, in1_ref, out1_ref,
    late_ref, swap_ref,
):
    text, width = emb_ref.shape
    grad = grad_ref[...]
    grad_low = grad.astype(BF)
    small_ref[10:11] = col_sum(grad_low)
    dout1 = nn(ctx_t_ref[...], grad_low).astype(BF)
    late_ref[3 * width :] = dout1[: width - SPILL]
    swap_ref[text + SMALL :] = dout1[width - SPILL :]
    grad_ctx = nt(grad_low, out1_ref[...]).astype(BF)
    key_t = qkv_ref[:, width : 2 * width].astype(F32).T.astype(BF)
    scaled = qkv_ref[:, :width] * jnp.asarray(HEAD_DIM**-0.5, BF)
    dkeys = []
    dvalues = []
    dquery = []
    for pair in range(HEADS // 2):
        dkey = 0.0
        dvalue = 0.0
        for head in (2 * pair, 2 * pair + 1):
            lanes = lanes_of(head)
            own_grad = own_lanes(grad_ctx[:, lanes], head)
            prob = prob_ref[head]
            dprob = nt(qkv_ref[:, slice(2 * width + lanes.start, 2 * width + lanes.stop)], own_grad)
            inner = jnp.sum(dprob * prob, axis=0, keepdims=True)
            dscore = (prob * (dprob - inner)).astype(BF)
            dvalue = dvalue + nn(prob.astype(BF), own_grad)
            dkey = dkey + nn(dscore, own_lanes(scaled[:, lanes], head))
            dquery.append(nn(key_t[rows_of(head)], dscore))
        dkeys.append(dkey.astype(BF))
        dvalues.append(dvalue.astype(BF))
    dq_t = jnp.concatenate(dquery, axis=0) * HEAD_DIM**-0.5
    dqkv = jnp.concatenate([dq_t.T.astype(BF)] + dkeys + dvalues, axis=1)
    small_ref[11:12] = col_sum(dqkv[:, :width])
    small_ref[12:13] = col_sum(dqkv[:, 2 * width :])
    din1 = nn(norm_c_ref[...].astype(F32).T.astype(BF), dqkv).astype(BF)
    for part in range(3):
        late_ref[width * part : width * part + width] = din1[:, width * part : width * part + width]
    unit, scale = normalise(emb_ref[...].astype(F32) * math.sqrt(width))
    grad_x, small_ref[13:14], small_ref[14:15] = norm_backward(
        nt(dqkv, in1_ref[...]), unit, scale, gain_ref[2:3]
    )
    swap_ref[:text] = ((grad + grad_x) * math.sqrt(width)).astype(BF)
    swap_ref[text : text + SMALL] = small_ref[...].astype(BF)


def forward_and_decoder(
    tok_ref, len_ref, at_ref, core_ref,
    x_ref, emb_ref, y1_ref, norm_c_ref, dec_qkv_ref, dec_ctx_t_ref, prob_ref, norm_d_ref, cross_q_ref,
    cot_ref, gain_ref, shift_ref, in_ref, in_b_ref, out_ref, out_b_ref, w1_from, b1_ref, w2_from, b2_ref,
    qkv_to, ctx_t_to, h1_to, lse_ref, dec_ref, dmem_ref, late_ref, swap_ref, keep_ref, send_ref,
    value_t, act, mem, cross, probs, cross_t, dkv, dq_t, grad, small, early, sems,
    w1_ref, w2_ref, qkv_ref, ctx_t_ref, h1_ref, load_sems, store_sems,
):
    loads = fetch(load_sems, (w1_from, w1_ref), (w2_from, w2_ref))
    stores = []

    def between():
        stores.extend(fetch(store_sems, (qkv_ref, qkv_to), (ctx_t_ref, ctx_t_to), (h1_ref, h1_to)))
        for load in loads:
            load.wait()

    in0, in1, in2 = (in_ref.at[i] for i in range(3))
    out0, out1, out2 = (out_ref.at[i] for i in range(3))
    encoder_forward(
        len_ref, at_ref, x_ref, gain_ref, shift_ref, in0, in_b_ref, out0, out_b_ref,
        w1_ref.at[0], b1_ref, w2_ref.at[0], b2_ref, in2,
        qkv_ref, ctx_t_ref, lse_ref, h1_ref, mem, cross,
        value_t, act, between,
    )
    decoder_main(
        tok_ref, len_ref, at_ref, core_ref,
        y1_ref, norm_d_ref, cross_q_ref, cross, mem, cot_ref, gain_ref, shift_ref,
        in2, out2, out_b_ref, w1_ref.at[1], b1_ref, w2_ref.at[1], b2_ref,
        dec_ref, dmem_ref, early, grad, small,
        probs, value_t, cross_t, dkv, dq_t,
    )
    decoder_self_backward(
        emb_ref, norm_c_ref, dec_qkv_ref, dec_ctx_t_ref, prob_ref, grad, small, gain_ref, in1, out1,
        late_ref, swap_ref,
    )
    half = early.shape[1]
    hand_out(
        sems, (early.at[0], keep_ref), (early.at[1], send_ref.at[:half]), (swap_ref, send_ref.at[half:])
    )
    for store in stores:
        store.wait()


def encoder_backward(
    len_ref, at_ref, core_ref,
    x_from, h1_ref, dmem_ref, ctx_t_ref, qkv_from, lse_ref, late_ref, gain_ref, shift_ref,
    in_from, out_ref, w1_ref, b1_ref, w2_ref,
    dx_ref, keep_ref, send_ref,
    grad_hid, dh1, dctx, key_t, dq_t, dqkv, small, feed, attn, sems,
    x_ref, qkv_ref, in_ref, load_sems, store_sems,
):
    loads = fetch(load_sems, (qkv_from, qkv_ref), (x_from, x_ref), (in_from.at[0], in_ref))
    encoder_feed_backward(
        core_ref, h1_ref, dmem_ref, ctx_t_ref, gain_ref, shift_ref, w1_ref, b1_ref, w2_ref, out_ref, late_ref,
        dh1, dctx, feed, small,
        grad_hid,
    )
    cut = feed.shape[1]
    stores = fetch(store_sems, (feed.at[0], keep_ref.at[:cut]), (feed.at[1], send_ref.at[:cut]))
    for load in loads:
        load.wait()
    encoder_attention_backward(
        len_ref, at_ref, core_ref, x_ref, qkv_ref, lse_ref, dctx, dh1, gain_ref, shift_ref, in_ref,
        dx_ref, attn,
        key_t, dq_t, dqkv, small,
    )
    hand_out(sems, (attn.at[0], keep_ref.at[cut:]), (attn.at[1], send_ref.at[cut:]))
    for store in stores:
        store.wait()


def fetch(sems, *pairs):
    copies = [pltpu.make_async_copy(ref, held, sems.at[i]) for i, (ref, held) in enumerate(pairs)]
    for copy in copies:
        copy.start()
    return copies


def early_merge(
    core_ref, ids_ref, swap_from, keep_ref, other_ref, out_ref, swap_ref, keep, other, swapped_ref, out, sems, out_sems
):
    core = core_ref[0]
    text = ids_ref.shape[1] // 2
    half = keep.shape[0]
    chunk = half // 4
    loads = fetch(
        sems, (swap_from, swap_ref), (other_ref.at[half:], swapped_ref), (keep_ref, keep),
        (other_ref.at[:half], other),
    )
    loads[0].wait()
    loads[1].wait()
    grad = jnp.concatenate([swap_ref[:text], swapped_ref[:text]], axis=0)
    for at in range(0, half, chunk):
        row = lax.broadcasted_iota(jnp.int32, (chunk, 2 * text), 0) + (core * half + at)
        hot = jnp.where(row == ids_ref[...], 1.0, 0.0).astype(BF)
        out[half + at : half + at + chunk] = nn(hot, grad).astype(BF)

    @pl.when(core == 1)
    def _():
        rest = swap_ref[text:].astype(F32) + swapped_ref[text:].astype(F32)
        out[2 * half - rest.shape[0] :] = rest.astype(BF)

    table = pltpu.make_async_copy(out.at[half:], out_ref.at[half:], out_sems.at[0])
    table.start()
    for load in loads[2:]:
        load.wait()
    out[:half] = (keep[...].astype(F32) + other[...].astype(F32)).astype(BF)
    sums = pltpu.make_async_copy(out.at[:half], out_ref.at[:half], out_sems.at[1])
    sums.start()
    table.wait()
    sums.wait()


def late_merge(keep_ref, other_ref, early_ref, out_ref, keep, other, early, out, sems, out_sems):
    count, size, width = out.shape
    size = size - early.shape[1]
    loads = fetch(sems, (early_ref, early), (keep_ref, keep), (other_ref, other))
    loads[0].wait()
    own = jnp.sum(early[...].astype(F32), axis=0).astype(BF)
    for load in loads[1:]:
        load.wait()
    stores = []
    part = count // 4
    for step in range(4):
        rows = slice(step * part * size, (step + 1) * part * size)
        places = slice(step * part, step * part + part)
        late = (keep[rows].astype(F32) + other[rows].astype(F32)).astype(BF)
        out[places, :size] = late.reshape(part, size, width)
        for place in range(step * part, step * part + part):
            out[place, size:] = own
        stores.append(pltpu.make_async_copy(out.at[places], out_ref.at[places], out_sems.at[step]))
        stores[-1].start()
    for store in stores:
        store.wait()


def late_spread(parts_ref, out_ref, parts, out, sems, out_sems):
    size = out.shape[1]
    half = out.shape[0] // 2
    ends = (slice(0, half), slice(half, 2 * half))
    loads = fetch(sems, *[(parts_ref.at[end, :size], parts.at[end]) for end in ends])
    total = 0.0
    for load, end in zip(loads, ends):
        load.wait()
        total = total + jnp.sum(parts[end].astype(F32), axis=0)
    late = total.astype(BF)
    stores = []
    for step, end in enumerate(ends):
        for place in range(end.start, end.stop):
            out[place] = late
        stores.append(pltpu.make_async_copy(out.at[end], out_ref.at[end], out_sems.at[step]))
        stores[-1].start()
    for store in stores:
        store.wait()


def early_outputs(core_ref, rate_ref, mine_ref, other_ref, table_ref, in_ref, out_ref, w1_ref, w2_ref, rest_ref):
    rate = rate_ref[0]
    first = core_ref[0] == 0
    count, size, width = mine_ref.shape
    blocks = w1_ref.shape[1] // width
    half = in_ref.shape[0] * 2 + w2_ref.shape[0]
    skip = size - 2 * half // count

    def rows(core, part):
        at = slice(count // 2 * part, count // 2 * (part + 1))
        mine, other = mine_ref[at, skip:], other_ref[at, skip:]
        picked = jnp.where(first, mine, other) if core == 0 else jnp.where(first, other, mine)
        return picked.reshape(half, width)

    table_ref[:half] = rows(0, 1).astype(F32) * rate
    rest = rows(1, 1)
    table_ref[half:] = rest[: table_ref.shape[0] - half].astype(F32) * rate
    rest_ref[...] = rest[half - rest_ref.shape[0] :]
    grads = jnp.concatenate([rows(0, 0), rows(1, 0)], axis=0).astype(F32) * rate
    for block in range(blocks):
        w1_ref[:, width * block : width * block + width] = grads[width * block : width * block + width]
    w2_ref[...] = grads[width * blocks : 2 * width * blocks]
    base = 2 * width * blocks
    for part in range(3):
        in_ref[:, width * part : width * part + width] = grads[base + width * part : base + width * part + width]
    out_ref[...] = grads[base + 3 * width :]


def late_outputs(
    half_ref, rate_ref, early_ref, rows_ref, in_in, out_in, w1_in, w2_in,
    in_ref, out_ref, w1_ref, w2_ref, rest_ref,
    rows, grads, sems, out_sems,
):
    size, width = rows.shape
    hidden = w2_ref.shape[1]
    cut = (width - SPILL) // 2
    base = hidden + 2 * width
    attn = base + cut
    over = size - attn - width
    (load,) = fetch(sems, (rows_ref, rows))
    load.wait()
    grads[:size] = rows[...].astype(F32) * rate_ref[0]
    grads[size:] = early_ref[SMALL:].astype(F32) * rate_ref[0]
    rest_ref[...] = rows[size - 2 * SMALL : size - SMALL]

    def block(at, rows=width):
        return grads.at[at : at + rows]

    def first():
        pairs = [(block(at), w1_ref.at[0, :, at : at + width]) for at in range(0, hidden, width)]
        pairs += [(block(hidden + at), in_ref.at[1, :, at : at + width]) for at in (0, width)]
        pairs.append((block(base, cut), out_ref.at[1, :cut]))
        pairs.append((block(attn), in_ref.at[0, :, :width]))
        pairs.append((block(attn + width, over), in_ref.at[0, :over, width : 2 * width]))
        return pairs

    def second():
        pairs = [(block(0, hidden), w2_ref.at[0])]
        pairs.append((block(hidden), in_ref.at[1, :, 2 * width :]))
        pairs.append((block(hidden + width), out_ref.at[0]))
        pairs.append((block(base, cut), out_ref.at[1, cut : 2 * cut]))
        pairs.append((block(size, SPILL), out_ref.at[1, 2 * cut :]))
        pairs.append((block(attn, width - over), in_ref.at[0, over:, width : 2 * width]))
        pairs.append((block(attn + width - over), in_ref.at[0, :, 2 * width :]))
        return pairs

    @pl.when(half_ref[0] == 0)
    def _():
        hand_out(out_sems, *first())

    @pl.when(half_ref[0] == 1)
    def _():
        hand_out(out_sems, *second())


def small_outputs(
    core_ref, rate_ref, mine_ref, other_ref, early_ref,
    gain_ref, shift_ref, in_b_ref, out_b_ref, b1_ref, b2_ref,
):
    width = mine_ref.shape[1]
    rate = rate_ref[0]
    enc = jnp.where(core_ref[0] == 1, mine_ref[...], other_ref[...]).astype(F32) * rate
    dec = early_ref[:SMALL].astype(F32) * rate
    for row, (part, at) in enumerate(((enc, 0), (enc, 8), (dec, 13), (dec, 8), (dec, 0))):
        gain_ref[row : row + 1] = part[at : at + 1]
        shift_ref[row : row + 1] = part[at + 1 : at + 2]
    for row, (part, at, next_at) in enumerate(((enc, 2, 3), (dec, 11, 12), (dec, 6, 7))):
        in_b_ref[row : row + 1, :width] = part[at : at + 1]
        in_b_ref[row : row + 1, width:] = part[next_at : next_at + 1]
    for row, (part, at) in enumerate(((enc, 11), (dec, 10), (dec, 5))):
        out_b_ref[row : row + 1] = part[at : at + 1]
    for row, (part, at) in enumerate(((enc, 10), (dec, 4))):
        b2_ref[row : row + 1] = part[at : at + 1]
    for row, part in enumerate((enc, dec)):
        for block in range(b1_ref.shape[1] // width):
            b1_ref[row : row + 1, width * block : width * block + width] = part[16 + block : 17 + block]


def frames_back(place_ref, own_ref, next_ref, second_ref, third_ref, out_ref):
    count = out_ref.shape[0]
    for shift, ref in enumerate((own_ref, next_ref, second_ref, third_ref)):
        out_ref[lax.rem(place_ref[0] + (count - shift), count)] = ref[...].astype(F32)


def encoder_feed_backward(
    core_ref, h1_ref, dmem_ref, ctx_t_ref, gain_ref, shift_ref, w1_ref, b1_ref, w2_ref, out_ref, late_ref,
    dh1_ref, dctx_ref, feed_ref, small_ref,
    grad_hid,
):
    width = h1_ref.shape[1]
    hidden_size = w1_ref.shape[1]
    slot = (core_ref[0], 1 - core_ref[0])
    cut = (width - SPILL) // 2
    feed_ref[slot[0], hidden_size : hidden_size + 2 * width] = late_ref[: 2 * width]
    feed_ref[slot[1], hidden_size : hidden_size + width] = late_ref[2 * width : 3 * width]
    feed_ref[slot[0], hidden_size + 2 * width :] = late_ref[3 * width : 3 * width + cut]
    feed_ref[slot[1], hidden_size + 2 * width :] = late_ref[3 * width + cut :]
    small_ref[...] = jnp.zeros_like(small_ref)
    unit, _ = normalise(h1_ref[...])
    norm_b = unit * gain_ref[1:2] + shift_ref[1:2]
    norm_b_t = norm_b.T.astype(BF)
    norm_b = norm_b.astype(BF)
    grad_low = dmem_ref[...]
    grad_low_t = grad_low.astype(F32).T.astype(BF)
    chunk = FEED_CHUNK

    def feed(index, carry):
        part = pl.ds(pl.multiple_of(index * chunk, chunk), chunk)
        hidden = nn(norm_b, w1_ref[:, part]) + b1_ref[0:1, part]
        value, slope = gelu_both(hidden)
        grad_hidden = (nt(grad_low, w2_ref[part]) * slope).astype(BF)
        grad_hid[:, part] = grad_hidden
        bias = col_sum(grad_hidden)
        first = nn(norm_b_t, grad_hidden).astype(BF)
        for sub in range(chunk // width):
            row = index * (chunk // width) + sub
            small_ref[pl.ds(16 + row, 1)] = bias[:, width * sub : width * sub + width]
            at = pl.multiple_of(row * width, width)
            feed_ref[slot[0], pl.ds(at, width)] = first[:, width * sub : width * sub + width]
        feed_ref[slot[1], part] = nn(grad_low_t, value.astype(BF)).T.astype(BF)
        return carry

    lax.fori_loop(0, hidden_size // chunk, feed, 0)
    grad = grad_low.astype(F32)
    small_ref[10:11] = col_sum(grad)
    unit, scale = normalise(h1_ref[...])
    grad_x, small_ref[8:9], small_ref[9:10] = norm_backward(
        nt(grad_hid[...], w1_ref[...]), unit, scale, gain_ref[1:2]
    )
    grad = grad + grad_x
    dh1_ref[...] = grad
    grad_low = grad.astype(BF)
    small_ref[11:12] = col_sum(grad_low)
    feed_ref[slot[1], hidden_size + width : hidden_size + 2 * width] = nn(ctx_t_ref[...], grad_low).astype(BF)
    dctx_ref[...] = nt(grad_low, out_ref[...]).astype(BF)


def encoder_attention_backward(
    len_ref, at_ref, core_ref, x_ref, qkv_ref, lse_ref, dctx_ref, dh1_ref, gain_ref, shift_ref, in_ref,
    dx_ref, attn_ref,
    key_t, dq_t, dqkv, small_ref,
):
    rows, width = x_ref.shape
    key_t[...] = qkv_ref[:, width : 2 * width].astype(F32).T.astype(BF)

    def attend_backward(at, pair):
        keys = qkv_ref[:, pl.ds(width + at, 128)]
        values = qkv_ref[:, pl.ds(2 * width + at, 128)]
        queries = qkv_ref[:, pl.ds(at, 128)] * jnp.asarray(HEAD_DIM**-0.5, BF)
        grads = dctx_ref[:, pl.ds(at, 128)]
        dkey = 0.0
        dvalue = 0.0
        for odd in range(2):
            query = own_lanes(queries, odd)
            score = nt(with_mask(keys, odd, len_ref[at_ref[0]]), with_one(query, odd))
            prob = jnp.exp(score - lse_ref[pl.ds(2 * pair + odd, 1)])
            own_grad = own_lanes(grads, odd)
            dprob = nt(values, own_grad)
            inner = jnp.sum(dprob * prob, axis=0, keepdims=True)
            dscore = (prob * (dprob - inner)).astype(BF)
            dkey = dkey + nn(dscore, query)
            dvalue = dvalue + nn(prob.astype(BF), own_grad)
            dq_t[head_rows(at, odd)] = nn(key_t[head_rows(at, odd)], dscore)
        dqkv[:, pl.ds(width + at, 128)] = dkey.astype(BF)
        dqkv[:, pl.ds(2 * width + at, 128)] = dvalue.astype(BF)

    each_pair(attend_backward)
    dqkv[:, :width] = (dq_t[...].T * HEAD_DIM**-0.5).astype(BF)
    small_ref[2:3] = col_sum(dqkv[:, :width])
    small_ref[3:4] = col_sum(dqkv[:, 2 * width :])
    unit, scale = normalise(x_ref[...].astype(F32))
    norm_a = unit * gain_ref[0:1] + shift_ref[0:1]
    din = nn(norm_a.T.astype(BF), dqkv[...]).astype(BF)
    blocks = [din[:, width * part : width * part + width] for part in range(3)]
    grad_x, small_ref[0:1], small_ref[1:2] = norm_backward(
        nt(dqkv[...], in_ref[...]), unit, scale, gain_ref[0:1]
    )
    dx_ref[...] = (dh1_ref[...] + grad_x).astype(BF)
    small = small_ref[...].astype(BF)
    packed = jnp.concatenate(blocks + [small, jnp.zeros_like(small)], axis=0)
    half = attn_ref.shape[1]
    attn_ref[core_ref[0]] = packed[:half]
    attn_ref[1 - core_ref[0]] = packed[half:]


def swap_cores(array):
    return lax.ppermute(array, "core", [(0, 1), (1, 0)])


def body(
    frames, utt_len, token_ids, tok_len, step, embed, norm_gain, norm_bias, attn_in, attn_in_bias,
    attn_out, attn_out_bias, ff_in, ff_in_bias, ff_out, ff_out_bias, cotangent,
):
    ring = ("frame", "pair")
    devices = lax.axis_size(ring)
    core = lax.axis_index("core")
    core_of = core[None]
    frame_at = lax.axis_index("frame")
    vocab, width = embed.shape
    hidden = ff_in.shape[2]
    frame_count = lax.axis_size("frame")
    local_len = frames.shape[2]
    rows = local_len * frame_count
    text = token_ids.shape[2]
    lengths = utt_len[0]
    frame_of = frame_at[None]
    my_tok = tok_len[0]
    arrived = lax.all_to_all(frames[0], "frame", split_axis=0, concat_axis=1, tiled=True)
    source = arrived.reshape(rows, width)
    ids = token_ids[0, 0]
    both_ids = jnp.concatenate([ids, swap_cores(ids)])[None]
    rows_in, both_ids = lax.optimization_barrier((embed[ids], both_ids))
    count_step = step[0].astype(F32)
    rate = jnp.minimum(lax.rsqrt(count_step), count_step * WARMUP ** (-1.5)) * WARMUP**0.5
    rate = rate[None]

    y1, norm_c, dec_qkv, dec_ctx_t, dec_prob, norm_d, cross_q = call(
        decoder_start,
        [
            ((text, width), F32), ((text, width), BF), ((text, 3 * width), BF), ((width, text), BF),
            ((HEADS, text, text), F32), ((text, width), BF), ((text, width), BF),
        ],
        [
            rows_in, norm_gain, norm_bias, (attn_in, 1), attn_in_bias, (attn_out, 1),
            attn_out_bias, (attn_in, 2),
        ],
        [my_tok],
        flops=2 * text * width * width * 5,
    )
    half = 2 * width + hidden
    swap_rows = text + SMALL + SPILL
    enc_qkv, enc_ctx_t, h1, lse, dec_out, dmem, self_grads, swap, early, early_send = call(
        forward_and_decoder,
        [
            ((rows, 3 * width), BF, None), ((width, rows), BF, None), ((rows, width), F32, None),
            ((8, rows), F32), ((text, width), BF), ((rows, width), BF), ((4 * width - SPILL, width), BF),
            ((swap_rows, width), BF), ((half, width), BF, None), ((half + swap_rows, width), BF, None),
        ],
        [
            source, rows_in, y1, norm_c, dec_qkv, dec_ctx_t, dec_prob, norm_d, cross_q, cotangent[0, 0],
            norm_gain, norm_bias, attn_in, attn_in_bias, attn_out, attn_out_bias, (ff_in, None), ff_in_bias,
            (ff_out, None), ff_out_bias,
        ],
        [my_tok, lengths, frame_of, core_of],
        [
            pltpu.VMEM((width, rows), BF), pltpu.VMEM((rows, hidden), BF), pltpu.VMEM((rows, width), BF),
            pltpu.VMEM((rows, 2 * width), BF), pltpu.VMEM((HEADS, rows, text), F32),
            pltpu.VMEM((width, text), F32), pltpu.VMEM((rows, 2 * width), BF),
            pltpu.VMEM((width, text), F32), pltpu.VMEM((text, width), F32),
            pltpu.VMEM((SMALL, width), F32), pltpu.VMEM((2, half, width), BF),
            pltpu.SemaphoreType.DMA((3,)),
            pltpu.VMEM(ff_in.shape, BF), pltpu.VMEM(ff_out.shape, BF), pltpu.VMEM((rows, 3 * width), BF),
            pltpu.VMEM((width, rows), BF), pltpu.VMEM((rows, width), F32),
            pltpu.SemaphoreType.DMA((2,)), pltpu.SemaphoreType.DMA((3,)),
        ],
        flops=2 * rows * width * (10 * width + 2 * rows + 2 * hidden)
        + 2 * text * width * (6 * hidden + 7 * rows + 26 * width),
    )
    (early_sum,) = call(
        early_merge,
        [((2 * half, width), BF, None)],
        [both_ids, (swap, None), (early, None), (swap_cores(early_send), "vmem")],
        [core_of],
        [
            pltpu.VMEM((swap_rows, width), BF), pltpu.VMEM((half, width), BF), pltpu.VMEM((half, width), BF),
            pltpu.VMEM((swap_rows, width), BF), pltpu.VMEM((2 * half, width), BF),
            pltpu.SemaphoreType.DMA((4,)), pltpu.SemaphoreType.DMA((2,)),
        ],
        flops=4 * half * width * text,
        limit=20,
    )
    early_sum, dmem = lax.optimization_barrier((early_sum, dmem))
    early_parts = lax.all_to_all(
        early_sum.reshape(devices, -1, width), ring, split_axis=0, concat_axis=0, tiled=True
    )
    early_own = jnp.sum(early_parts.astype(F32), axis=0).astype(BF)

    feed_half = (5 * width - SPILL) // 2 + hidden
    attn_half = 3 * width // 2 + SMALL
    late_half = feed_half + attn_half
    dx, late, late_send = call(
        encoder_backward,
        [((rows, width), BF), ((late_half, width), BF, None), ((late_half, width), BF, None)],
        [
            (source, None), h1, dmem, enc_ctx_t, (enc_qkv, None), lse, self_grads, norm_gain, norm_bias,
            (attn_in, None), (attn_out, 0), (ff_in, 0), ff_in_bias, (ff_out, 0),
        ],
        [lengths, frame_of, core_of],
        [
            pltpu.VMEM((rows, hidden), BF), pltpu.VMEM((rows, width), F32), pltpu.VMEM((rows, width), BF),
            pltpu.VMEM((width, rows), BF), pltpu.VMEM((width, rows), F32), pltpu.VMEM((rows, 3 * width), BF),
            pltpu.VMEM((SMALL, width), F32), pltpu.VMEM((2, feed_half, width), BF),
            pltpu.VMEM((2, attn_half, width), BF), pltpu.SemaphoreType.DMA((2,)),
            pltpu.VMEM((rows, width), BF), pltpu.VMEM((rows, 3 * width), BF), pltpu.VMEM((width, 3 * width), BF),
            pltpu.SemaphoreType.DMA((3,)), pltpu.SemaphoreType.DMA((2,)),
        ],
        flops=2 * rows * width * (5 * hidden + 5 * rows + 8 * width),
    )
    late_size = late_half // devices
    early_size = 2 * half // devices
    mixed_shape = (devices, late_size + early_size, width)
    (mixed,) = call(
        late_merge,
        [(mixed_shape, BF, None)],
        [(late, None), (swap_cores(late_send), None), (early_parts, None)],
        scratch=[
            pltpu.VMEM((late_half, width), BF), pltpu.VMEM((late_half, width), BF),
            pltpu.VMEM((devices, early_size, width), BF), pltpu.VMEM(mixed_shape, BF),
            pltpu.SemaphoreType.DMA((3,)), pltpu.SemaphoreType.DMA((4,)),
        ],
        limit=24,
    )
    mixed = lax.all_to_all(mixed, ring, split_axis=0, concat_axis=0, tiled=True)
    chunks = dx.reshape(frame_count, local_len, width)
    moved = []
    for shift in range(frame_count):
        target = lax.rem(frame_at + shift, frame_count)
        chunk = lax.dynamic_index_in_dim(chunks, target, keepdims=False)
        if shift:
            chunk = lax.ppermute(chunk, "frame", [(i, (i + shift) % frame_count) for i in range(frame_count)])
        moved.append(chunk)
    mixed, moved = lax.optimization_barrier((mixed, moved))
    late_shape = (devices, late_size, width)
    (late_own,) = call(
        late_spread,
        [(late_shape, BF, None)],
        [(mixed, None)],
        scratch=[
            pltpu.VMEM(late_shape, BF), pltpu.VMEM(late_shape, BF),
            pltpu.SemaphoreType.DMA((2,)), pltpu.SemaphoreType.DMA((2,)),
        ],
    )
    early_other = swap_cores(mixed)
    (frames_grad,) = call(
        frames_back, [((frame_count, local_len, width), F32)], moved, [frame_of], limit=16
    )
    late_mine = lax.all_to_all(late_own, ring, split_axis=0, concat_axis=0, tiled=True)
    in_shape = (3, width, 3 * width)
    out_shape = (3, width, width)
    w1_shape = (2, width, hidden)
    w2_shape = (2, hidden, width)
    table_grad, in_grad, out_grad, w1_grad, w2_grad, early_rest = call(
        early_outputs,
        [
            ((vocab, width), F32), (in_shape, F32, None, 2), (out_shape, F32, None, 2),
            (w1_shape, F32, None, 1), (w2_shape, F32, None, 1), ((SMALL + SPILL, width), BF),
        ],
        [mixed, early_other],
        [core_of, rate],
        limit=40,
    )
    late_mine, early_rest, frames_grad = lax.optimization_barrier((late_mine, early_rest, frames_grad))
    late_mine = late_mine.reshape(late_half, width)
    late_other = swap_cores(late_mine)
    results = (in_grad, out_grad, w1_grad, w2_grad)
    rests = []
    for rows_of_half, which in ((late_mine, core_of), (late_other, 1 - core_of)):
        *results, rest = call(
            late_outputs,
            [
                (in_shape, F32, None), (out_shape, F32, None), (w1_shape, F32, None),
                (w2_shape, F32, None), ((SMALL, width), BF),
            ],
            [early_rest, (rows_of_half, "vmem")] + [(result, None) for result in results],
            [which, rate],
            [
                pltpu.VMEM((late_half, width), BF), pltpu.VMEM((late_half + SPILL, width), F32),
                pltpu.SemaphoreType.DMA((1,)), pltpu.SemaphoreType.DMA((16,)),
            ],
            aliases={4: 0, 5: 1, 6: 2, 7: 3},
            limit=16,
        )
        rests.append(rest)
    in_grad, out_grad, w1_grad, w2_grad = results
    gain_grad, shift_grad, in_b_grad, out_b_grad, b1_grad, b2_grad = call(
        small_outputs,
        [
            ((5, width), F32), ((5, width), F32), ((3, 2 * width), F32), ((3, width), F32),
            ((2, hidden), F32), ((2, width), F32),
        ],
        rests + [early_rest],
        [core_of, rate],
        limit=32,
    )
    return (
        dec_out[None, None],
        frames_grad[None],
        table_grad,
        gain_grad,
        shift_grad,
        in_grad,
        in_b_grad,
        out_grad,
        out_b_grad,
        w1_grad,
        b1_grad,
        w2_grad,
        b2_grad,
    )


def solution(mesh):
    groups = ("pair", "core")
    frames, batch = mesh.devices.shape
    split = Mesh(mesh.devices.reshape(frames, batch // 2, 2), ("frame",) + groups)
    placed = (
        P(groups, None, "frame", None),
        P(groups, None),
        P(groups, "frame", None),
        P(groups, "frame"),
    ) + (P(),) * 12 + (P(groups, "frame", None, None),)
    results = (P(groups, "frame", None, None), P(groups, None, "frame", None)) + (P(),) * 11
    return jax.shard_map(body, mesh=split, in_specs=placed, out_specs=results, check_vma=False)
```

```python
import functools
import math

import jax
import jax.numpy as jnp
from jax import lax
from jax.experimental import pallas as pl
from jax.experimental.pallas import tpu as pltpu
from jax.sharding import Mesh, PartitionSpec as P

HEADS = 4
HEAD_DIM = 64
WARMUP = 25000
EPSILON = 1e-05
MASKED = -1e30
BF = jnp.bfloat16
F32 = jnp.float32
GELU_A = math.sqrt(2.0 / math.pi)
GELU_B = GELU_A * 0.044715
SMALL = 32
FEED_CHUNK = 512
SPILL = 64


def nn(left, right):
    return lax.dot_general(left, right, (((1,), (0,)), ((), ())), preferred_element_type=F32)


def nt(left, right):
    return lax.dot_general(left, right, (((1,), (1,)), ((), ())), preferred_element_type=F32)


def hand_out(sems, *pairs):
    copies = [pltpu.make_async_copy(held, ref, sems.at[i]) for i, (held, ref) in enumerate(pairs)]
    for copy in copies:
        copy.start()
    for copy in copies:
        copy.wait()


def normalise(states):
    average = jnp.mean(states, axis=-1, keepdims=True)
    centred = states - average
    scale = lax.rsqrt(jnp.mean(centred * centred, axis=-1, keepdims=True) + EPSILON)
    return centred * scale, scale


def norm_backward(grad, unit, scale, gain):
    grad_unit = grad * gain
    mean_grad = jnp.mean(grad_unit, axis=-1, keepdims=True)
    mean_along = jnp.mean(grad_unit * unit, axis=-1, keepdims=True)
    grad_states = scale * (grad_unit - mean_grad - unit * mean_along)
    return grad_states, col_sum(grad * unit), col_sum(grad)


def col_sum(matrix):
    return jnp.sum(matrix.astype(F32), axis=0, keepdims=True)


def gelu_value(hidden):
    inner = hidden * (GELU_A + GELU_B * (hidden * hidden))
    return hidden * (0.5 + 0.5 * jnp.tanh(inner))


def gelu_both(hidden):
    square = hidden * hidden
    bent = jnp.tanh(hidden * (GELU_A + GELU_B * square))
    half = 0.5 + 0.5 * bent
    slope = half + (0.5 * hidden) * (1.0 - bent * bent) * (GELU_A + 3.0 * GELU_B * square)
    return hidden * half, slope


def lanes_of(head):
    return slice(128 * (head // 2), 128 * (head // 2) + 128)


def rows_of(head):
    return slice(HEAD_DIM * head, HEAD_DIM * head + HEAD_DIM)


def each_pair(step):
    def body(pair, carry):
        step(pl.multiple_of(pair * 2 * HEAD_DIM, 2 * HEAD_DIM), pair)
        return carry

    lax.fori_loop(0, HEADS // 2, body, 0)


def head_rows(at, odd):
    return pl.ds(pl.multiple_of(at + HEAD_DIM * odd, HEAD_DIM), HEAD_DIM)


def own_lanes(pair, head):
    lane = lax.broadcasted_iota(jnp.int32, pair.shape, 1)
    mine = (lane < HEAD_DIM) if head % 2 == 0 else (lane >= HEAD_DIM)
    return jnp.where(mine, pair, jnp.zeros_like(pair))


def spare_lane(head):
    return HEAD_DIM if head % 2 == 0 else 0


def with_one(query, head):
    lane = lax.broadcasted_iota(jnp.int32, query.shape, 1)
    return jnp.where(lane == spare_lane(head), jnp.ones_like(query), query)


def with_mask(key_pair, head, length):
    lane = lax.broadcasted_iota(jnp.int32, key_pair.shape, 1)
    row = lax.broadcasted_iota(jnp.int32, key_pair.shape, 0)
    bias = jnp.where(row < length, 0.0, MASKED).astype(BF)
    return jnp.where(lane == spare_lane(head), bias, key_pair)


def part_spec(shape, layers, at):
    index = (at,) + (0,) * (len(shape) - 1)
    return pl.BlockSpec((layers,) + shape[1:], lambda *g: index, pipeline_mode=pl.Buffered(1))


def call(kernel, outs, args, scalars=(), scratch=(), flops=0, aliases=None, limit=61):
    in_specs = []
    for a in args:
        if not isinstance(a, tuple):
            in_specs.append(part_spec(a.shape, a.shape[0], 0))
        elif a[1] is None or a[1] == "vmem":
            in_specs.append(pl.BlockSpec(memory_space=pl.ANY))
        else:
            in_specs.append(part_spec(a[0].shape, None, a[1]))
    spaces = {None: pltpu.HBM, "vmem": pltpu.VMEM}
    args = [a if isinstance(a, tuple) else (a, 0) for a in args]
    args = [a[0] if isinstance(a[1], int) else pltpu.with_memory_space_constraint(a[0], spaces[a[1]]) for a in args]
    out_specs = []
    for out in outs:
        if out[-1] is None:
            out_specs.append(pl.BlockSpec(memory_space=pltpu.HBM))
        elif isinstance(out[-1], int):
            out_specs.append(part_spec(out[0], out[2], out[3]))
        else:
            out_specs.append(part_spec(out[0], out[0][0], 0))
    size = sum(a.size * a.dtype.itemsize for a in args)
    size += sum(math.prod(out[0]) * jnp.dtype(out[1]).itemsize for out in outs)
    return pl.pallas_call(
        kernel,
        grid_spec=pltpu.PrefetchScalarGridSpec(
            num_scalar_prefetch=len(scalars),
            grid=(1,),
            in_specs=in_specs,
            out_specs=out_specs,
            scratch_shapes=list(scratch),
        ),
        out_shape=[
            (pltpu.HBM if out[-1] is None else jax.ShapeDtypeStruct)(out[0], out[1]) for out in outs
        ],
        input_output_aliases=aliases or {},
        compiler_params=pltpu.CompilerParams(vmem_limit_bytes=limit * 1024 * 1024),
        cost_estimate=pl.CostEstimate(flops=flops, bytes_accessed=size, transcendentals=0),
        name=kernel.__name__,
    )(*scalars, *args)


def decoder_start(
    tok_ref, emb_ref, gain_ref, shift_ref, in_ref, in_b_ref, out_ref, out_b_ref, cross_ref,
    y1_ref, norm_c_ref, qkv_ref, ctx_t_ref, prob_ref, norm_d_ref, cross_q_ref,
):
    text = emb_ref.shape[0]
    width = emb_ref.shape[1]
    start = emb_ref[...].astype(F32) * math.sqrt(width)
    unit, _ = normalise(start)
    norm_c = (unit * gain_ref[2:3] + shift_ref[2:3]).astype(BF)
    norm_c_ref[...] = norm_c
    flat = nn(norm_c, in_ref[...])
    query = (flat[:, :width] + in_b_ref[1:2, :width]).astype(BF)
    key = flat[:, width : 2 * width].astype(BF)
    value = (flat[:, 2 * width :] + in_b_ref[1:2, width:]).astype(BF)
    qkv_ref[:, :width] = query
    qkv_ref[:, width : 2 * width] = key
    qkv_ref[:, 2 * width :] = value
    value_t = value.astype(F32).T.astype(BF)
    key_at = lax.broadcasted_iota(jnp.int32, (text, text), 0)
    query_at = lax.broadcasted_iota(jnp.int32, (text, text), 1)
    seen = jnp.logical_and(key_at <= query_at, key_at < tok_ref[0])
    scaled = query * jnp.asarray(HEAD_DIM**-0.5, BF)
    parts = []
    for head in range(HEADS):
        lanes = lanes_of(head)
        score = nt(key[:, lanes], own_lanes(scaled[:, lanes], head))
        score = jnp.where(seen, score, MASKED)
        weight = jnp.exp(score - jnp.max(score, axis=0, keepdims=True))
        prob = weight / jnp.sum(weight, axis=0, keepdims=True)
        prob_ref[head] = prob
        parts.append(nn(value_t[rows_of(head)], prob.astype(BF)))
    ctx_t = jnp.concatenate(parts, axis=0)
    ctx_t_ref[...] = ctx_t.astype(BF)
    y1 = start + nn(ctx_t.T.astype(BF), out_ref[...]) + out_b_ref[1:2]
    y1_ref[...] = y1
    unit, _ = normalise(y1)
    norm_d = (unit * gain_ref[3:4] + shift_ref[3:4]).astype(BF)
    norm_d_ref[...] = norm_d
    cross_q_ref[...] = (nn(norm_d, cross_ref[:, :width]) + in_b_ref[2:3, :width]).astype(BF)


def encoder_forward(
    len_ref, at_ref, x_ref, gain_ref, shift_ref, in_ref, in_b_ref, out_ref, out_b_ref,
    w1_ref, b1_ref, w2_ref, b2_ref, cin_ref,
    qkv_ref, ctx_t_ref, lse_ref, h1_ref, mem_ref, cross_ref,
    value_t, act, between,
):
    rows, width = x_ref.shape
    unit, _ = normalise(x_ref[...].astype(F32))
    norm_a = (unit * gain_ref[0:1] + shift_ref[0:1]).astype(BF)
    qkv_ref[:, :width] = (nn(norm_a, in_ref[:, :width]) + in_b_ref[0:1, :width]).astype(BF)
    key = nn(norm_a, in_ref[:, width : 2 * width]).astype(BF)
    qkv_ref[:, width : 2 * width] = key
    value = (nn(norm_a, in_ref[:, 2 * width :]) + in_b_ref[0:1, width:]).astype(BF)
    qkv_ref[:, 2 * width :] = value
    value_t[...] = value.astype(F32).T.astype(BF)

    def attend(at, pair):
        keys = qkv_ref[:, pl.ds(width + at, 128)]
        queries = qkv_ref[:, pl.ds(at, 128)] * jnp.asarray(HEAD_DIM**-0.5, BF)
        for odd in range(2):
            query = with_one(own_lanes(queries, odd), odd)
            score = nt(with_mask(keys, odd, len_ref[at_ref[0]]), query)
            highest = jnp.max(score, axis=0, keepdims=True)
            weight = jnp.exp(score - highest)
            total = jnp.sum(weight, axis=0, keepdims=True)
            context = nn(value_t[head_rows(at, odd)], weight.astype(BF)) * (1.0 / total)
            ctx_t_ref[head_rows(at, odd)] = context.astype(BF)
            lse_ref[pl.ds(2 * pair + odd, 1)] = highest + jnp.log(total)

    each_pair(attend)
    between()
    context = ctx_t_ref[...].astype(F32).T.astype(BF)
    h1 = x_ref[...].astype(F32) + nn(context, out_ref[...]) + out_b_ref[0:1]
    h1_ref[...] = h1
    unit, _ = normalise(h1)
    norm_b = (unit * gain_ref[1:2] + shift_ref[1:2]).astype(BF)

    hidden = nn(norm_b, w1_ref[...]) + b1_ref[0:1]
    act[...] = gelu_value(hidden).astype(BF)
    memory = (h1_ref[...] + nn(act[...], w2_ref[...]) + b2_ref[0:1]).astype(BF)
    mem_ref[...] = memory
    cross_ref[:, :width] = nn(memory, cin_ref[:, width : 2 * width]).astype(BF)
    cross_ref[:, width:] = (nn(memory, cin_ref[:, 2 * width :]) + in_b_ref[2:3, width:]).astype(BF)


def decoder_main(
    tok_ref, len_ref, at_ref, core_ref,
    y1_ref, norm_d_ref, cross_q_ref, cross_ref, mem_ref, cot_ref, gain_ref, shift_ref,
    in2_ref, out2_ref, out_b_ref, w1_ref, b1_ref, w2_ref, b2_ref,
    dec_ref, dmem_ref, early_ref, grad_ref, small_ref,
    probs, turned, cross_t, dkv, dq_t, fed,
):
    text, width = y1_ref.shape
    hidden_size = w1_ref.shape[1]
    slot = (core_ref[0], 1 - core_ref[0])
    small_ref[...] = jnp.zeros_like(small_ref)
    turned[...] = cross_ref[:, width:].astype(F32).T.astype(BF)

    def attend(at, pair):
        keys = cross_ref[:, pl.ds(at, 128)]
        queries = cross_q_ref[:, pl.ds(at, 128)] * jnp.asarray(HEAD_DIM**-0.5, BF)
        for odd in range(2):
            query = with_one(own_lanes(queries, odd), odd)
            score = nt(with_mask(keys, odd, len_ref[at_ref[0]]), query)
            weight = jnp.exp(score - jnp.max(score, axis=0, keepdims=True))
            prob = weight * (1.0 / jnp.sum(weight, axis=0, keepdims=True))
            probs[2 * pair + odd] = prob
            cross_t[head_rows(at, odd)] = nn(turned[head_rows(at, odd)], prob.astype(BF))

    each_pair(attend)
    context_t = cross_t[...]
    y2 = y1_ref[...] + nn(context_t.T.astype(BF), out2_ref[...]) + out_b_ref[2:3]
    unit_e, scale_e = normalise(y2)
    norm_e = (unit_e * gain_ref[4:5] + shift_ref[4:5]).astype(BF)
    norm_e_t = norm_e.astype(F32).T.astype(BF)
    valid = lax.broadcasted_iota(jnp.int32, (text, 1), 0) < tok_ref[0]
    grad_low = jnp.where(valid, cot_ref[...], jnp.zeros_like(cot_ref))
    grad = grad_low.astype(F32)
    grad_low_t = grad.T.astype(BF)
    chunk = 512

    def feed(index, sums):
        part = pl.ds(pl.multiple_of(index * chunk, chunk), chunk)
        hidden = nn(norm_e, w1_ref[:, part]) + b1_ref[1:2, part]
        value, slope = gelu_both(hidden)
        active = value.astype(BF)
        grad_hidden = (nt(grad_low, w2_ref[part]) * slope).astype(BF)
        bias = col_sum(grad_hidden)
        first = nn(norm_e_t, grad_hidden).astype(BF)
        for sub in range(chunk // width):
            row = index * (chunk // width) + sub
            small_ref[pl.ds(16 + row, 1)] = bias[:, width * sub : width * sub + width]
            at = pl.multiple_of(row * width, width)
            early_ref[slot[0], pl.ds(at, width)] = first[:, width * sub : width * sub + width]
        second = nn(grad_low_t, active).T.astype(BF)
        at = pl.multiple_of(jnp.where(index == 0, hidden_size, (index - 1) * chunk), chunk)
        early_ref[jnp.where(index == 0, slot[0], slot[1]), pl.ds(at, chunk)] = second
        return sums[0] + nn(active, w2_ref[part]), sums[1] + nt(grad_hidden, w1_ref[:, part])

    zeros = jnp.zeros((text, width), F32)
    feed_out, grad_norm = lax.fori_loop(0, hidden_size // chunk, feed, (zeros, zeros))
    fed()
    y3 = y2 + b2_ref[1:2] + feed_out
    dec_ref[...] = jnp.where(valid, y3, 0.0).astype(BF)
    small_ref[4:5] = col_sum(grad)
    grad_x, small_ref[0:1], small_ref[1:2] = norm_backward(grad_norm, unit_e, scale_e, gain_ref[4:5])
    grad = grad + grad_x
    grad_low = grad.astype(BF)
    small_ref[5:6] = col_sum(grad_low)
    base = hidden_size - chunk
    early_ref[slot[1], base + 3 * width :] = nn(context_t.astype(BF), grad_low).astype(BF)
    grad_ctx = nt(grad_low, out2_ref[...]).astype(BF)
    turned[...] = cross_ref[:, :width].astype(F32).T.astype(BF)
    mem_t = mem_ref[...].astype(F32).T.astype(BF)
    grad_ref[...] = grad_ctx.astype(F32)

    def attend_backward(at, pair):
        queries = cross_q_ref[:, pl.ds(at, 128)] * jnp.asarray(HEAD_DIM**-0.5, BF)
        values = cross_ref[:, pl.ds(width + at, 128)]
        grads = grad_ref[:, pl.ds(at, 128)].astype(BF)
        dkey = 0.0
        dvalue = 0.0
        for odd in range(2):
            own_grad = own_lanes(grads, odd)
            prob = probs[2 * pair + odd]
            dprob = nt(values, own_grad)
            inner = jnp.sum(dprob * prob, axis=0, keepdims=True)
            dscore = (prob * (dprob - inner)).astype(BF)
            dvalue = dvalue + nn(prob.astype(BF), own_grad)
            dkey = dkey + nn(dscore, own_lanes(queries, odd))
            dq_t[head_rows(at, odd)] = nn(turned[head_rows(at, odd)], dscore)
        dkv[:, pl.ds(at, 128)] = dkey.astype(BF)
        dkv[:, pl.ds(width + at, 128)] = dvalue.astype(BF)

    each_pair(attend_backward)
    dq = (dq_t[...] * HEAD_DIM**-0.5).T.astype(BF)
    small_ref[6:7] = col_sum(dq)
    small_ref[7:8] = col_sum(dkv[:, width:])
    norm_d = norm_d_ref[...]
    early_ref[slot[1], base : base + width] = nn(norm_d.astype(F32).T.astype(BF), dq).astype(BF)
    pairs = nn(mem_t, dkv[...]).astype(BF)
    early_ref[slot[1], base + width : base + 2 * width] = pairs[:, :width]
    early_ref[slot[1], base + 2 * width : base + 3 * width] = pairs[:, width:]
    dmem_ref[...] = nt(dkv[...], in2_ref[:, width:]).astype(BF)
    unit, scale = normalise(y1_ref[...])
    grad_x, small_ref[8:9], small_ref[9:10] = norm_backward(
        nt(dq, in2_ref[:, :width]), unit, scale, gain_ref[3:4]
    )
    grad_ref[...] = grad + grad_x


def decoder_self_backward(
    emb_ref, norm_c_ref, qkv_ref, ctx_t_ref, prob_ref, grad_ref, small_ref, gain_ref, in1_ref, out1_ref,
    late_ref, swap_ref,
):
    text, width = emb_ref.shape
    grad = grad_ref[...]
    grad_low = grad.astype(BF)
    small_ref[10:11] = col_sum(grad_low)
    dout1 = nn(ctx_t_ref[...], grad_low).astype(BF)
    late_ref[3 * width :] = dout1[: width - SPILL]
    swap_ref[text + SMALL :] = dout1[width - SPILL :]
    grad_ctx = nt(grad_low, out1_ref[...]).astype(BF)
    key_t = qkv_ref[:, width : 2 * width].astype(F32).T.astype(BF)
    scaled = qkv_ref[:, :width] * jnp.asarray(HEAD_DIM**-0.5, BF)
    dkeys = []
    dvalues = []
    dquery = []
    for pair in range(HEADS // 2):
        dkey = 0.0
        dvalue = 0.0
        for head in (2 * pair, 2 * pair + 1):
            lanes = lanes_of(head)
            own_grad = own_lanes(grad_ctx[:, lanes], head)
            prob = prob_ref[head]
            dprob = nt(qkv_ref[:, slice(2 * width + lanes.start, 2 * width + lanes.stop)], own_grad)
            inner = jnp.sum(dprob * prob, axis=0, keepdims=True)
            dscore = (prob * (dprob - inner)).astype(BF)
            dvalue = dvalue + nn(prob.astype(BF), own_grad)
            dkey = dkey + nn(dscore, own_lanes(scaled[:, lanes], head))
            dquery.append(nn(key_t[rows_of(head)], dscore))
        dkeys.append(dkey.astype(BF))
        dvalues.append(dvalue.astype(BF))
    dq_t = jnp.concatenate(dquery, axis=0) * HEAD_DIM**-0.5
    dqkv = jnp.concatenate([dq_t.T.astype(BF)] + dkeys + dvalues, axis=1)
    small_ref[11:12] = col_sum(dqkv[:, :width])
    small_ref[12:13] = col_sum(dqkv[:, 2 * width :])
    din1 = nn(norm_c_ref[...].astype(F32).T.astype(BF), dqkv).astype(BF)
    for part in range(3):
        late_ref[width * part : width * part + width] = din1[:, width * part : width * part + width]
    unit, scale = normalise(emb_ref[...].astype(F32) * math.sqrt(width))
    grad_x, small_ref[13:14], small_ref[14:15] = norm_backward(
        nt(dqkv, in1_ref[...]), unit, scale, gain_ref[2:3]
    )
    swap_ref[:text] = ((grad + grad_x) * math.sqrt(width)).astype(BF)
    swap_ref[text : text + SMALL] = small_ref[...].astype(BF)


def forward_and_decoder(
    tok_ref, len_ref, at_ref, core_ref,
    x_ref, in0, gain_ref, shift_ref, in_b_ref, out_b_ref, b1_ref, b2_ref,
    in_from, out_from, w1_from, w2_from,
    emb_from, y1_from, norm_c_from, dec_qkv_from, dec_ctx_t_from, prob_from, norm_d_from, cross_q_from, cot_from,
    qkv_to, ctx_t_to, h1_to, lse_ref, dec_ref, dmem_to, late_ref, swap_ref, keep_ref, send_ref,
    value_t, act, mem, cross, probs, cross_t, dkv, dq_t, grad, small, early,
    qkv_ref, ctx_t_ref, h1_ref, dmem_ref,
    in_ref, out_ref, w1_ref, w2_ref,
    emb_ref, y1_ref, norm_c_ref, dec_qkv_ref, dec_ctx_t_ref, prob_ref, norm_d_ref, cross_q_ref, cot_ref,
    load_sems, store_sems,
):
    loads = fetch(
        load_sems, (out_from, out_ref), (w1_from, w1_ref), (w2_from, w2_ref), (in_from.at[1:], in_ref),
        (emb_from, emb_ref), (y1_from, y1_ref), (norm_c_from, norm_c_ref), (dec_qkv_from, dec_qkv_ref),
        (dec_ctx_t_from, dec_ctx_t_ref), (prob_from, prob_ref), (norm_d_from, norm_d_ref),
        (cross_q_from, cross_q_ref), (cot_from, cot_ref),
    )
    stores = []

    def send(*pairs):
        for held, ref in pairs:
            stores.append(pltpu.make_async_copy(held, ref, store_sems.at[len(stores)]))
            stores[-1].start()

    def arrived():
        for load in loads:
            load.wait()
        send((qkv_ref, qkv_to), (ctx_t_ref, ctx_t_to))

    in1, in2 = in_ref.at[0], in_ref.at[1]
    out0, out1, out2 = (out_ref.at[i] for i in range(3))
    encoder_forward(
        len_ref, at_ref, x_ref, gain_ref, shift_ref, in0, in_b_ref, out0, out_b_ref,
        w1_ref.at[0], b1_ref, w2_ref.at[0], b2_ref, in2,
        qkv_ref, ctx_t_ref, lse_ref, h1_ref, mem, cross,
        value_t, act, arrived,
    )
    half = early.shape[1]
    full = half - 4 * x_ref.shape[1]
    places = (keep_ref, send_ref)

    def fed():
        send((h1_ref, h1_to), *[(early.at[i, :full], places[i].at[:full]) for i in range(2)])

    decoder_main(
        tok_ref, len_ref, at_ref, core_ref,
        y1_ref, norm_d_ref, cross_q_ref, cross, mem, cot_ref, gain_ref, shift_ref,
        in2, out2, out_b_ref, w1_ref.at[1], b1_ref, w2_ref.at[1], b2_ref,
        dec_ref, dmem_ref, early, grad, small,
        probs, value_t, cross_t, dkv, dq_t, fed,
    )
    send((dmem_ref, dmem_to), *[(early.at[i, full:], places[i].at[full:half]) for i in range(2)])
    decoder_self_backward(
        emb_ref, norm_c_ref, dec_qkv_ref, dec_ctx_t_ref, prob_ref, grad, small, gain_ref, in1, out1,
        late_ref, swap_ref,
    )
    send((swap_ref, send_ref.at[half:]))
    for store in stores:
        store.wait()


def encoder_backward(
    len_ref, at_ref, core_ref,
    h1_ref, dmem_ref, lse_ref, gain_ref, shift_ref, w1_ref, b1_ref, w2_ref,
    x_from, ctx_t_from, qkv_from, late_from, in_from, out_from,
    dx_ref, keep_ref, send_ref,
    grad_hid, dh1, dctx, key_t, dq_t, dqkv, small, feed, attn,
    x_ref, ctx_t_ref, qkv_ref, late_ref, in_ref, out_ref, load_sems, store_sems,
):
    loads = fetch(
        load_sems, (ctx_t_from, ctx_t_ref), (late_from, late_ref), (out_from.at[0], out_ref),
        (qkv_from, qkv_ref), (x_from, x_ref), (in_from.at[0], in_ref),
    )
    hidden = w1_ref.shape[1]
    places = (keep_ref, send_ref)
    stores = []

    def send(*pairs):
        for held, ref in pairs:
            stores.append(pltpu.make_async_copy(held, ref, store_sems.at[len(stores)]))
            stores[-1].start()

    def fed():
        for load in loads:
            load.wait()
        send(*[(feed.at[i, :hidden], places[i].at[:hidden]) for i in range(2)])

    encoder_feed_backward(
        core_ref, h1_ref, dmem_ref, ctx_t_ref, gain_ref, shift_ref, w1_ref, b1_ref, w2_ref, out_ref, late_ref,
        dh1, dctx, feed, small,
        grad_hid, fed,
    )
    cut = feed.shape[1]
    encoder_attention_backward(
        len_ref, at_ref, core_ref, x_ref, qkv_ref, lse_ref, dctx, dh1, gain_ref, shift_ref, in_ref,
        dx_ref, attn,
        key_t, dq_t, dqkv, small,
    )
    send(*[(feed.at[i, hidden:], places[i].at[hidden:cut]) for i in range(2)])
    send(*[(attn.at[i], places[i].at[cut:]) for i in range(2)])
    for store in stores:
        store.wait()


def fetch(sems, *pairs):
    copies = [pltpu.make_async_copy(ref, held, sems.at[i]) for i, (ref, held) in enumerate(pairs)]
    for copy in copies:
        copy.start()
    return copies


def early_merge(
    core_ref, ids_ref, swap_from, keep_ref, other_ref, out_ref, swap_ref, keep, other, swapped_ref, out, sems, out_sems
):
    core = core_ref[0]
    text = ids_ref.shape[1] // 2
    half = keep.shape[0]
    chunk = half // 4
    loads = fetch(
        sems, (swap_from, swap_ref), (other_ref.at[half:], swapped_ref), (keep_ref, keep),
        (other_ref.at[:half], other),
    )
    loads[0].wait()
    loads[1].wait()
    grad = jnp.concatenate([swap_ref[:text], swapped_ref[:text]], axis=0)
    for at in range(0, half, chunk):
        row = lax.broadcasted_iota(jnp.int32, (chunk, 2 * text), 0) + (core * half + at)
        hot = jnp.where(row == ids_ref[...], 1.0, 0.0).astype(BF)
        out[half + at : half + at + chunk] = nn(hot, grad).astype(BF)

    @pl.when(core == 1)
    def _():
        rest = swap_ref[text:].astype(F32) + swapped_ref[text:].astype(F32)
        out[2 * half - rest.shape[0] :] = rest.astype(BF)

    table = pltpu.make_async_copy(out.at[half:], out_ref.at[half:], out_sems.at[0])
    table.start()
    for load in loads[2:]:
        load.wait()
    out[:half] = (keep[...].astype(F32) + other[...].astype(F32)).astype(BF)
    sums = pltpu.make_async_copy(out.at[:half], out_ref.at[:half], out_sems.at[1])
    sums.start()
    table.wait()
    sums.wait()


def late_merge(keep_ref, other_ref, early_ref, out_ref, keep, other, early, out, sems, out_sems):
    count, size, width = out.shape
    size = size - early.shape[1]
    loads = fetch(sems, (early_ref, early), (keep_ref, keep), (other_ref, other))
    loads[0].wait()
    own = jnp.sum(early[...].astype(F32), axis=0).astype(BF)
    for load in loads[1:]:
        load.wait()
    stores = []
    part = count // 4
    for step in range(4):
        rows = slice(step * part * size, (step + 1) * part * size)
        places = slice(step * part, step * part + part)
        late = (keep[rows].astype(F32) + other[rows].astype(F32)).astype(BF)
        out[places, :size] = late.reshape(part, size, width)
        for place in range(step * part, step * part + part):
            out[place, size:] = own
        stores.append(pltpu.make_async_copy(out.at[places], out_ref.at[places], out_sems.at[step]))
        stores[-1].start()
    for store in stores:
        store.wait()


def late_spread(parts_ref, out_ref, parts, out, sems, out_sems):
    size = out.shape[1]
    half = out.shape[0] // 2
    ends = (slice(0, half), slice(half, 2 * half))
    loads = fetch(sems, *[(parts_ref.at[end, :size], parts.at[end]) for end in ends])
    total = 0.0
    for load, end in zip(loads, ends):
        load.wait()
        total = total + jnp.sum(parts[end].astype(F32), axis=0)
    late = total.astype(BF)
    stores = []
    for step, end in enumerate(ends):
        for place in range(end.start, end.stop):
            out[place] = late
        stores.append(pltpu.make_async_copy(out.at[end], out_ref.at[end], out_sems.at[step]))
        stores[-1].start()
    for store in stores:
        store.wait()


def early_outputs(
    core_ref, rate_ref, mine_ref, other_ref,
    table_ref, in_ref, out_ref, w1_ref, w2_ref, rest_ref,
    grads, table, sems,
):
    rate = rate_ref[0]
    first = core_ref[0] == 0
    count, size, width = mine_ref.shape
    hidden = w2_ref.shape[1]
    half = grads.shape[0] // 2
    each = 2 * half // count
    skip = size - each

    def chunk(index, carry):
        at = pl.multiple_of(index * each, each)
        for part, held in ((0, grads), (count // 2, table)):
            mine, other = mine_ref[part + index, skip:], other_ref[part + index, skip:]
            held[pl.ds(at, each)] = jnp.where(first, mine, other).astype(F32) * rate
            held[pl.ds(half + at, each)] = jnp.where(first, other, mine).astype(F32) * rate
        return carry

    lax.fori_loop(0, count // 2, chunk, 0)
    tail = mine_ref[count - 2 :, skip:].reshape(2 * each, width)
    other_tail = other_ref[count - 2 :, skip:].reshape(2 * each, width)
    rest_ref[...] = jnp.where(first, other_tail, tail)[2 * each - rest_ref.shape[0] :]
    base = 2 * hidden
    pairs = [(table.at[: table_ref.shape[0]], table_ref), (grads.at[hidden:base], w2_ref.at[1])]
    pairs += [(grads.at[at : at + width], w1_ref.at[1, :, at : at + width]) for at in range(0, hidden, width)]
    pairs += [
        (grads.at[base + at : base + at + width], in_ref.at[2, :, at : at + width])
        for at in range(0, 3 * width, width)
    ]
    pairs.append((grads.at[base + 3 * width :], out_ref.at[2]))
    hand_out(sems, *pairs)


def late_outputs(
    half_ref, rate_ref, early_ref, rows_ref, in_in, out_in, w1_in, w2_in,
    in_ref, out_ref, w1_ref, w2_ref, rest_ref,
    rows, grads, sems, out_sems,
):
    size, width = rows.shape
    hidden = w2_ref.shape[1]
    cut = (width - SPILL) // 2
    base = hidden + 2 * width
    attn = base + cut
    over = size - attn - width
    (load,) = fetch(sems, (rows_ref, rows))
    load.wait()

    def scale(index, carry):
        part = pl.ds(pl.multiple_of(index * width, width), width)
        grads[part] = rows[part].astype(F32) * rate_ref[0]
        return carry

    lax.fori_loop(0, size // width, scale, 0)
    grads[size:] = early_ref[SMALL:].astype(F32) * rate_ref[0]
    rest_ref[...] = rows[size - 2 * SMALL : size - SMALL]

    def block(at, rows=width):
        return grads.at[at : at + rows]

    def first():
        pairs = [(block(at), w1_ref.at[0, :, at : at + width]) for at in range(0, hidden, width)]
        pairs += [(block(hidden + at), in_ref.at[1, :, at : at + width]) for at in (0, width)]
        pairs.append((block(base, cut), out_ref.at[1, :cut]))
        pairs.append((block(attn), in_ref.at[0, :, :width]))
        pairs.append((block(attn + width, over), in_ref.at[0, :over, width : 2 * width]))
        return pairs

    def second():
        pairs = [(block(0, hidden), w2_ref.at[0])]
        pairs.append((block(hidden), in_ref.at[1, :, 2 * width :]))
        pairs.append((block(hidden + width), out_ref.at[0]))
        pairs.append((block(base, cut), out_ref.at[1, cut : 2 * cut]))
        pairs.append((block(size, SPILL), out_ref.at[1, 2 * cut :]))
        pairs.append((block(attn, width - over), in_ref.at[0, over:, width : 2 * width]))
        pairs.append((block(attn + width - over), in_ref.at[0, :, 2 * width :]))
        return pairs

    @pl.when(half_ref[0] == 0)
    def _():
        hand_out(out_sems, *first())

    @pl.when(half_ref[0] == 1)
    def _():
        hand_out(out_sems, *second())


def small_outputs(
    core_ref, rate_ref, mine_ref, other_ref, early_ref,
    gain_ref, shift_ref, in_b_ref, out_b_ref, b1_ref, b2_ref,
):
    width = mine_ref.shape[1]
    rate = rate_ref[0]
    enc = jnp.where(core_ref[0] == 1, mine_ref[...], other_ref[...]).astype(F32) * rate
    dec = early_ref[:SMALL].astype(F32) * rate
    for row, (part, at) in enumerate(((enc, 0), (enc, 8), (dec, 13), (dec, 8), (dec, 0))):
        gain_ref[row : row + 1] = part[at : at + 1]
        shift_ref[row : row + 1] = part[at + 1 : at + 2]
    for row, (part, at, next_at) in enumerate(((enc, 2, 3), (dec, 11, 12), (dec, 6, 7))):
        in_b_ref[row : row + 1, :width] = part[at : at + 1]
        in_b_ref[row : row + 1, width:] = part[next_at : next_at + 1]
    for row, (part, at) in enumerate(((enc, 11), (dec, 10), (dec, 5))):
        out_b_ref[row : row + 1] = part[at : at + 1]
    for row, (part, at) in enumerate(((enc, 10), (dec, 4))):
        b2_ref[row : row + 1] = part[at : at + 1]
    for row, part in enumerate((enc, dec)):
        for block in range(b1_ref.shape[1] // width):
            b1_ref[row : row + 1, width * block : width * block + width] = part[16 + block : 17 + block]


def frames_back(place_ref, own_ref, next_ref, second_ref, third_ref, out_ref):
    count = out_ref.shape[0]
    for shift, ref in enumerate((own_ref, next_ref, second_ref, third_ref)):
        out_ref[lax.rem(place_ref[0] + (count - shift), count)] = ref[...].astype(F32)


def encoder_feed_backward(
    core_ref, h1_ref, dmem_ref, ctx_t_ref, gain_ref, shift_ref, w1_ref, b1_ref, w2_ref, out_ref, late_ref,
    dh1_ref, dctx_ref, feed_ref, small_ref,
    grad_hid, fed,
):
    width = h1_ref.shape[1]
    hidden_size = w1_ref.shape[1]
    slot = (core_ref[0], 1 - core_ref[0])
    cut = (width - SPILL) // 2
    small_ref[...] = jnp.zeros_like(small_ref)
    unit, _ = normalise(h1_ref[...])
    norm_b = unit * gain_ref[1:2] + shift_ref[1:2]
    norm_b_t = norm_b.T.astype(BF)
    norm_b = norm_b.astype(BF)
    grad_low = dmem_ref[...]
    grad_low_t = grad_low.astype(F32).T.astype(BF)
    chunk = FEED_CHUNK

    def feed(index, carry):
        part = pl.ds(pl.multiple_of(index * chunk, chunk), chunk)
        hidden = nn(norm_b, w1_ref[:, part]) + b1_ref[0:1, part]
        value, slope = gelu_both(hidden)
        grad_hidden = (nt(grad_low, w2_ref[part]) * slope).astype(BF)
        grad_hid[:, part] = grad_hidden
        bias = col_sum(grad_hidden)
        first = nn(norm_b_t, grad_hidden).astype(BF)
        for sub in range(chunk // width):
            row = index * (chunk // width) + sub
            small_ref[pl.ds(16 + row, 1)] = bias[:, width * sub : width * sub + width]
            at = pl.multiple_of(row * width, width)
            feed_ref[slot[0], pl.ds(at, width)] = first[:, width * sub : width * sub + width]
        feed_ref[slot[1], part] = nn(grad_low_t, value.astype(BF)).T.astype(BF)
        return carry

    lax.fori_loop(0, hidden_size // chunk, feed, 0)
    fed()
    feed_ref[slot[0], hidden_size : hidden_size + 2 * width] = late_ref[: 2 * width]
    feed_ref[slot[1], hidden_size : hidden_size + width] = late_ref[2 * width : 3 * width]
    feed_ref[slot[0], hidden_size + 2 * width :] = late_ref[3 * width : 3 * width + cut]
    feed_ref[slot[1], hidden_size + 2 * width :] = late_ref[3 * width + cut :]
    grad = grad_low.astype(F32)
    small_ref[10:11] = col_sum(grad)
    unit, scale = normalise(h1_ref[...])
    grad_x, small_ref[8:9], small_ref[9:10] = norm_backward(
        nt(grad_hid[...], w1_ref[...]), unit, scale, gain_ref[1:2]
    )
    grad = grad + grad_x
    dh1_ref[...] = grad
    grad_low = grad.astype(BF)
    small_ref[11:12] = col_sum(grad_low)
    feed_ref[slot[1], hidden_size + width : hidden_size + 2 * width] = nn(ctx_t_ref[...], grad_low).astype(BF)
    dctx_ref[...] = nt(grad_low, out_ref[...]).astype(BF)


def encoder_attention_backward(
    len_ref, at_ref, core_ref, x_ref, qkv_ref, lse_ref, dctx_ref, dh1_ref, gain_ref, shift_ref, in_ref,
    dx_ref, attn_ref,
    key_t, dq_t, dqkv, small_ref,
):
    rows, width = x_ref.shape
    key_t[...] = qkv_ref[:, width : 2 * width].astype(F32).T.astype(BF)

    def attend_backward(at, pair):
        keys = qkv_ref[:, pl.ds(width + at, 128)]
        values = qkv_ref[:, pl.ds(2 * width + at, 128)]
        queries = qkv_ref[:, pl.ds(at, 128)] * jnp.asarray(HEAD_DIM**-0.5, BF)
        grads = dctx_ref[:, pl.ds(at, 128)]
        dkey = 0.0
        dvalue = 0.0
        for odd in range(2):
            query = own_lanes(queries, odd)
            score = nt(with_mask(keys, odd, len_ref[at_ref[0]]), with_one(query, odd))
            prob = jnp.exp(score - lse_ref[pl.ds(2 * pair + odd, 1)])
            own_grad = own_lanes(grads, odd)
            dprob = nt(values, own_grad)
            inner = jnp.sum(dprob * prob, axis=0, keepdims=True)
            dscore = (prob * (dprob - inner)).astype(BF)
            dkey = dkey + nn(dscore, query)
            dvalue = dvalue + nn(prob.astype(BF), own_grad)
            dq_t[head_rows(at, odd)] = nn(key_t[head_rows(at, odd)], dscore)
        dqkv[:, pl.ds(width + at, 128)] = dkey.astype(BF)
        dqkv[:, pl.ds(2 * width + at, 128)] = dvalue.astype(BF)

    each_pair(attend_backward)
    dqkv[:, :width] = (dq_t[...].T * HEAD_DIM**-0.5).astype(BF)
    small_ref[2:3] = col_sum(dqkv[:, :width])
    small_ref[3:4] = col_sum(dqkv[:, 2 * width :])
    unit, scale = normalise(x_ref[...].astype(F32))
    norm_a = unit * gain_ref[0:1] + shift_ref[0:1]
    din = nn(norm_a.T.astype(BF), dqkv[...]).astype(BF)
    blocks = [din[:, width * part : width * part + width] for part in range(3)]
    grad_x, small_ref[0:1], small_ref[1:2] = norm_backward(
        nt(dqkv[...], in_ref[...]), unit, scale, gain_ref[0:1]
    )
    dx_ref[...] = (dh1_ref[...] + grad_x).astype(BF)
    small = small_ref[...].astype(BF)
    packed = jnp.concatenate(blocks + [small, jnp.zeros_like(small)], axis=0)
    half = attn_ref.shape[1]
    attn_ref[core_ref[0]] = packed[:half]
    attn_ref[1 - core_ref[0]] = packed[half:]


def swap_cores(array):
    return lax.ppermute(array, "core", [(0, 1), (1, 0)])


def body(
    frames, utt_len, token_ids, tok_len, step, embed, norm_gain, norm_bias, attn_in, attn_in_bias,
    attn_out, attn_out_bias, ff_in, ff_in_bias, ff_out, ff_out_bias, cotangent,
):
    ring = ("frame", "pair")
    devices = lax.axis_size(ring)
    core = lax.axis_index("core")
    core_of = core[None]
    frame_at = lax.axis_index("frame")
    vocab, width = embed.shape
    hidden = ff_in.shape[2]
    frame_count = lax.axis_size("frame")
    local_len = frames.shape[2]
    rows = local_len * frame_count
    text = token_ids.shape[2]
    lengths = utt_len[0]
    frame_of = frame_at[None]
    my_tok = tok_len[0]
    arrived = lax.all_to_all(frames[0], "frame", split_axis=0, concat_axis=1, tiled=True)
    source = arrived.reshape(rows, width)
    ids = token_ids[0, 0]
    both_ids = jnp.concatenate([ids, swap_cores(ids)])[None]
    rows_in, both_ids = lax.optimization_barrier((embed[ids], both_ids))
    count_step = step[0].astype(F32)
    rate = jnp.minimum(lax.rsqrt(count_step), count_step * WARMUP ** (-1.5)) * WARMUP**0.5
    rate = rate[None]

    y1, norm_c, dec_qkv, dec_ctx_t, dec_prob, norm_d, cross_q = call(
        decoder_start,
        [
            ((text, width), F32), ((text, width), BF), ((text, 3 * width), BF), ((width, text), BF),
            ((HEADS, text, text), F32), ((text, width), BF), ((text, width), BF),
        ],
        [
            rows_in, norm_gain, norm_bias, (attn_in, 1), attn_in_bias, (attn_out, 1),
            attn_out_bias, (attn_in, 2),
        ],
        [my_tok],
        flops=2 * text * width * width * 5,
    )
    half = 2 * width + hidden
    swap_rows = text + SMALL + SPILL
    decoder_args = [rows_in, y1, norm_c, dec_qkv, dec_ctx_t, dec_prob, norm_d, cross_q, cotangent[0, 0]]
    enc_qkv, enc_ctx_t, h1, lse, dec_out, dmem, self_grads, swap, early, early_send = call(
        forward_and_decoder,
        [
            ((rows, 3 * width), BF, None), ((width, rows), BF, None), ((rows, width), F32, None),
            ((8, rows), F32), ((text, width), BF), ((rows, width), BF, None), ((4 * width - SPILL, width), BF),
            ((swap_rows, width), BF), ((half, width), BF, None), ((half + swap_rows, width), BF, None),
        ],
        [
            source, (attn_in, 0), norm_gain, norm_bias, attn_in_bias, attn_out_bias, ff_in_bias, ff_out_bias,
            (attn_in, None), (attn_out, None), (ff_in, None), (ff_out, None),
        ]
        + [(arg, None) for arg in decoder_args],
        [my_tok, lengths, frame_of, core_of],
        [
            pltpu.VMEM((width, rows), BF), pltpu.VMEM((rows, hidden), BF), pltpu.VMEM((rows, width), BF),
            pltpu.VMEM((rows, 2 * width), BF), pltpu.VMEM((HEADS, rows, text), F32),
            pltpu.VMEM((width, text), F32), pltpu.VMEM((rows, 2 * width), BF),
            pltpu.VMEM((width, text), F32), pltpu.VMEM((text, width), F32),
            pltpu.VMEM((SMALL, width), F32), pltpu.VMEM((2, half, width), BF),
            pltpu.VMEM((rows, 3 * width), BF), pltpu.VMEM((width, rows), BF), pltpu.VMEM((rows, width), F32),
            pltpu.VMEM((rows, width), BF),
            pltpu.VMEM((2,) + attn_in.shape[1:], BF), pltpu.VMEM(attn_out.shape, BF),
            pltpu.VMEM(ff_in.shape, BF), pltpu.VMEM(ff_out.shape, BF),
        ]
        + [pltpu.VMEM(arg.shape, arg.dtype) for arg in decoder_args]
        + [pltpu.SemaphoreType.DMA((13,)), pltpu.SemaphoreType.DMA((9,))],
        flops=2 * rows * width * (10 * width + 2 * rows + 2 * hidden)
        + 2 * text * width * (6 * hidden + 7 * rows + 26 * width),
    )
    (early_sum,) = call(
        early_merge,
        [((2 * half, width), BF, None)],
        [both_ids, (swap, None), (early, None), (swap_cores(early_send), "vmem")],
        [core_of],
        [
            pltpu.VMEM((swap_rows, width), BF), pltpu.VMEM((half, width), BF), pltpu.VMEM((half, width), BF),
            pltpu.VMEM((swap_rows, width), BF), pltpu.VMEM((2 * half, width), BF),
            pltpu.SemaphoreType.DMA((4,)), pltpu.SemaphoreType.DMA((2,)),
        ],
        flops=4 * half * width * text,
        limit=20,
    )
    early_sum, dmem = lax.optimization_barrier((early_sum, dmem))
    early_parts = lax.all_to_all(
        early_sum.reshape(devices, -1, width), ring, split_axis=0, concat_axis=0, tiled=True
    )
    early_own = jnp.sum(early_parts.astype(F32), axis=0).astype(BF)

    feed_half = (5 * width - SPILL) // 2 + hidden
    attn_half = 3 * width // 2 + SMALL
    late_half = feed_half + attn_half
    dx, late, late_send = call(
        encoder_backward,
        [((rows, width), BF), ((late_half, width), BF, None), ((late_half, width), BF, None)],
        [
            h1, dmem, lse, norm_gain, norm_bias, (ff_in, 0), ff_in_bias, (ff_out, 0), (source, None),
            (enc_ctx_t, None), (enc_qkv, None), (self_grads, None), (attn_in, None), (attn_out, None),
        ],
        [lengths, frame_of, core_of],
        [
            pltpu.VMEM((rows, hidden), BF), pltpu.VMEM((rows, width), F32), pltpu.VMEM((rows, width), BF),
            pltpu.VMEM((width, rows), BF), pltpu.VMEM((width, rows), F32), pltpu.VMEM((rows, 3 * width), BF),
            pltpu.VMEM((SMALL, width), F32), pltpu.VMEM((2, feed_half, width), BF),
            pltpu.VMEM((2, attn_half, width), BF),
            pltpu.VMEM((rows, width), BF), pltpu.VMEM((width, rows), BF), pltpu.VMEM((rows, 3 * width), BF),
            pltpu.VMEM(self_grads.shape, BF), pltpu.VMEM((width, 3 * width), BF), pltpu.VMEM((width, width), BF),
            pltpu.SemaphoreType.DMA((6,)), pltpu.SemaphoreType.DMA((6,)),
        ],
        flops=2 * rows * width * (5 * hidden + 5 * rows + 8 * width),
    )
    late_size = late_half // devices
    early_size = 2 * half // devices
    mixed_shape = (devices, late_size + early_size, width)
    (mixed,) = call(
        late_merge,
        [(mixed_shape, BF, None)],
        [(late, None), (swap_cores(late_send), None), (early_parts, None)],
        scratch=[
            pltpu.VMEM((late_half, width), BF), pltpu.VMEM((late_half, width), BF),
            pltpu.VMEM((devices, early_size, width), BF), pltpu.VMEM(mixed_shape, BF),
            pltpu.SemaphoreType.DMA((3,)), pltpu.SemaphoreType.DMA((4,)),
        ],
        limit=24,
    )
    mixed = lax.all_to_all(mixed, ring, split_axis=0, concat_axis=0, tiled=True)
    chunks = dx.reshape(frame_count, local_len, width)
    moved = []
    for shift in range(frame_count):
        target = lax.rem(frame_at + shift, frame_count)
        chunk = lax.dynamic_index_in_dim(chunks, target, keepdims=False)
        if shift:
            chunk = lax.ppermute(chunk, "frame", [(i, (i + shift) % frame_count) for i in range(frame_count)])
        moved.append(chunk)
    mixed, moved = lax.optimization_barrier((mixed, moved))
    late_shape = (devices, late_size, width)
    (late_own,) = call(
        late_spread,
        [(late_shape, BF, None)],
        [(mixed, None)],
        scratch=[
            pltpu.VMEM(late_shape, BF), pltpu.VMEM(late_shape, BF),
            pltpu.SemaphoreType.DMA((2,)), pltpu.SemaphoreType.DMA((2,)),
        ],
    )
    early_other = swap_cores(mixed)
    (frames_grad,) = call(
        frames_back, [((frame_count, local_len, width), F32)], moved, [frame_of], limit=16
    )
    late_mine = lax.all_to_all(late_own, ring, split_axis=0, concat_axis=0, tiled=True)
    in_shape = (3, width, 3 * width)
    out_shape = (3, width, width)
    w1_shape = (2, width, hidden)
    w2_shape = (2, hidden, width)
    table_grad, in_grad, out_grad, w1_grad, w2_grad, early_rest = call(
        early_outputs,
        [
            ((vocab, width), F32, None), (in_shape, F32, None), (out_shape, F32, None),
            (w1_shape, F32, None), (w2_shape, F32, None), ((SMALL + SPILL, width), BF),
        ],
        [mixed, early_other],
        [core_of, rate],
        [
            pltpu.VMEM((2 * half, width), F32), pltpu.VMEM((2 * half, width), F32),
            pltpu.SemaphoreType.DMA((14,)),
        ],
        limit=40,
    )
    late_mine, early_rest, frames_grad = lax.optimization_barrier((late_mine, early_rest, frames_grad))
    late_mine = late_mine.reshape(late_half, width)
    late_other = swap_cores(late_mine)
    results = (in_grad, out_grad, w1_grad, w2_grad)
    rests = []
    for rows_of_half, which in ((late_mine, core_of), (late_other, 1 - core_of)):
        *results, rest = call(
            late_outputs,
            [
                (in_shape, F32, None), (out_shape, F32, None), (w1_shape, F32, None),
                (w2_shape, F32, None), ((SMALL, width), BF),
            ],
            [early_rest, (rows_of_half, "vmem")] + [(result, None) for result in results],
            [which, rate],
            [
                pltpu.VMEM((late_half, width), BF), pltpu.VMEM((late_half + SPILL, width), F32),
                pltpu.SemaphoreType.DMA((1,)), pltpu.SemaphoreType.DMA((16,)),
            ],
            aliases={4: 0, 5: 1, 6: 2, 7: 3},
            limit=16,
        )
        rests.append(rest)
    in_grad, out_grad, w1_grad, w2_grad = results
    gain_grad, shift_grad, in_b_grad, out_b_grad, b1_grad, b2_grad = call(
        small_outputs,
        [
            ((5, width), F32), ((5, width), F32), ((3, 2 * width), F32), ((3, width), F32),
            ((2, hidden), F32), ((2, width), F32),
        ],
        rests + [early_rest],
        [core_of, rate],
        limit=32,
    )
    return (
        dec_out[None, None],
        frames_grad[None],
        table_grad,
        gain_grad,
        shift_grad,
        in_grad,
        in_b_grad,
        out_grad,
        out_b_grad,
        w1_grad,
        b1_grad,
        w2_grad,
        b2_grad,
    )


def solution(mesh):
    groups = ("pair", "core")
    frames, batch = mesh.devices.shape
    split = Mesh(mesh.devices.reshape(frames, batch // 2, 2), ("frame",) + groups)
    placed = (
        P(groups, None, "frame", None),
        P(groups, None),
        P(groups, "frame", None),
        P(groups, "frame"),
    ) + (P(),) * 12 + (P(groups, "frame", None, None),)
    results = (P(groups, "frame", None, None), P(groups, None, "frame", None)) + (P(),) * 11
    return jax.shard_map(body, mesh=split, in_specs=placed, out_specs=results, check_vma=False)
```

```python
import functools
import math

import jax
import jax.numpy as jnp
from jax import lax
from jax.experimental import pallas as pl
from jax.experimental.pallas import tpu as pltpu
from jax.sharding import Mesh, PartitionSpec as P

HEADS = 4
HEAD_DIM = 64
WARMUP = 25000
EPSILON = 1e-05
MASKED = -1e30
BF = jnp.bfloat16
F32 = jnp.float32
GELU_A = math.sqrt(2.0 / math.pi)
GELU_B = GELU_A * 0.044715
SMALL = 32
FEED_CHUNK = 512
SPILL = 64


def nn(left, right):
    return lax.dot_general(left, right, (((1,), (0,)), ((), ())), preferred_element_type=F32)


def nt(left, right):
    return lax.dot_general(left, right, (((1,), (1,)), ((), ())), preferred_element_type=F32)


def hand_out(sems, *pairs):
    copies = [pltpu.make_async_copy(held, ref, sems.at[i]) for i, (held, ref) in enumerate(pairs)]
    for copy in copies:
        copy.start()
    for copy in copies:
        copy.wait()


def normalise(states):
    average = jnp.mean(states, axis=-1, keepdims=True)
    centred = states - average
    scale = lax.rsqrt(jnp.mean(centred * centred, axis=-1, keepdims=True) + EPSILON)
    return centred * scale, scale


def norm_backward(grad, unit, scale, gain):
    grad_unit = grad * gain
    mean_grad = jnp.mean(grad_unit, axis=-1, keepdims=True)
    mean_along = jnp.mean(grad_unit * unit, axis=-1, keepdims=True)
    grad_states = scale * (grad_unit - mean_grad - unit * mean_along)
    return grad_states, col_sum(grad * unit), col_sum(grad)


def col_sum(matrix):
    return jnp.sum(matrix.astype(F32), axis=0, keepdims=True)


def gelu_value(hidden):
    inner = hidden * (GELU_A + GELU_B * (hidden * hidden))
    return hidden * (0.5 + 0.5 * jnp.tanh(inner))


def gelu_both(hidden):
    square = hidden * hidden
    bent = jnp.tanh(hidden * (GELU_A + GELU_B * square))
    half = 0.5 + 0.5 * bent
    slope = half + (0.5 * hidden) * (1.0 - bent * bent) * (GELU_A + 3.0 * GELU_B * square)
    return hidden * half, slope


def lanes_of(head):
    return slice(128 * (head // 2), 128 * (head // 2) + 128)


def rows_of(head):
    return slice(HEAD_DIM * head, HEAD_DIM * head + HEAD_DIM)


def each_pair(step):
    def body(pair, carry):
        step(pl.multiple_of(pair * 2 * HEAD_DIM, 2 * HEAD_DIM), pair)
        return carry

    lax.fori_loop(0, HEADS // 2, body, 0)


def head_rows(at, odd):
    return pl.ds(pl.multiple_of(at + HEAD_DIM * odd, HEAD_DIM), HEAD_DIM)


def own_lanes(pair, head):
    lane = lax.broadcasted_iota(jnp.int32, pair.shape, 1)
    mine = (lane < HEAD_DIM) if head % 2 == 0 else (lane >= HEAD_DIM)
    return jnp.where(mine, pair, jnp.zeros_like(pair))


def both_heads(pair):
    return jnp.concatenate([own_lanes(pair, 0), own_lanes(pair, 1)], axis=0)


def spare_lane(head):
    return HEAD_DIM if head % 2 == 0 else 0


def with_one(query, head):
    lane = lax.broadcasted_iota(jnp.int32, query.shape, 1)
    return jnp.where(lane == spare_lane(head), jnp.ones_like(query), query)


def with_mask(key_pair, head, length):
    lane = lax.broadcasted_iota(jnp.int32, key_pair.shape, 1)
    row = lax.broadcasted_iota(jnp.int32, key_pair.shape, 0)
    bias = jnp.where(row < length, 0.0, MASKED).astype(BF)
    return jnp.where(lane == spare_lane(head), bias, key_pair)


def part_spec(shape, layers, at):
    index = (at,) + (0,) * (len(shape) - 1)
    return pl.BlockSpec((layers,) + shape[1:], lambda *g: index, pipeline_mode=pl.Buffered(1))


def call(kernel, outs, args, scalars=(), scratch=(), flops=0, aliases=None, limit=61):
    in_specs = []
    for a in args:
        if not isinstance(a, tuple):
            in_specs.append(part_spec(a.shape, a.shape[0], 0))
        elif a[1] is None or a[1] == "vmem":
            in_specs.append(pl.BlockSpec(memory_space=pl.ANY))
        else:
            in_specs.append(part_spec(a[0].shape, None, a[1]))
    spaces = {None: pltpu.HBM, "vmem": pltpu.VMEM}
    args = [a if isinstance(a, tuple) else (a, 0) for a in args]
    args = [a[0] if isinstance(a[1], int) else pltpu.with_memory_space_constraint(a[0], spaces[a[1]]) for a in args]
    out_specs = []
    for out in outs:
        if out[-1] is None:
            out_specs.append(pl.BlockSpec(memory_space=pltpu.HBM))
        elif isinstance(out[-1], int):
            out_specs.append(part_spec(out[0], out[2], out[3]))
        else:
            out_specs.append(part_spec(out[0], out[0][0], 0))
    size = sum(a.size * a.dtype.itemsize for a in args)
    size += sum(math.prod(out[0]) * jnp.dtype(out[1]).itemsize for out in outs)
    return pl.pallas_call(
        kernel,
        grid_spec=pltpu.PrefetchScalarGridSpec(
            num_scalar_prefetch=len(scalars),
            grid=(1,),
            in_specs=in_specs,
            out_specs=out_specs,
            scratch_shapes=list(scratch),
        ),
        out_shape=[
            (pltpu.HBM if out[-1] is None else jax.ShapeDtypeStruct)(out[0], out[1]) for out in outs
        ],
        input_output_aliases=aliases or {},
        compiler_params=pltpu.CompilerParams(vmem_limit_bytes=limit * 1024 * 1024),
        cost_estimate=pl.CostEstimate(flops=flops, bytes_accessed=size, transcendentals=0),
        name=kernel.__name__,
    )(*scalars, *args)


def decoder_start(
    tok_ref, emb_ref, gain_ref, shift_ref, in_ref, in_b_ref, out_ref, out_b_ref, cross_ref,
    y1_ref, norm_c_ref, qkv_ref, ctx_t_ref, prob_ref, norm_d_ref, cross_q_ref,
):
    text = emb_ref.shape[0]
    width = emb_ref.shape[1]
    start = emb_ref[...].astype(F32) * math.sqrt(width)
    unit, _ = normalise(start)
    norm_c = (unit * gain_ref[2:3] + shift_ref[2:3]).astype(BF)
    norm_c_ref[...] = norm_c
    flat = nn(norm_c, in_ref[...])
    query = (flat[:, :width] + in_b_ref[1:2, :width]).astype(BF)
    key = flat[:, width : 2 * width].astype(BF)
    value = (flat[:, 2 * width :] + in_b_ref[1:2, width:]).astype(BF)
    qkv_ref[:, :width] = query
    qkv_ref[:, width : 2 * width] = key
    qkv_ref[:, 2 * width :] = value
    value_t = value.astype(F32).T.astype(BF)
    key_at = lax.broadcasted_iota(jnp.int32, (text, text), 0)
    query_at = lax.broadcasted_iota(jnp.int32, (text, text), 1)
    seen = jnp.logical_and(key_at <= query_at, key_at < tok_ref[0])
    scaled = query * jnp.asarray(HEAD_DIM**-0.5, BF)
    parts = []
    for head in range(HEADS):
        lanes = lanes_of(head)
        score = nt(key[:, lanes], own_lanes(scaled[:, lanes], head))
        score = jnp.where(seen, score, MASKED)
        weight = jnp.exp(score - jnp.max(score, axis=0, keepdims=True))
        prob = weight / jnp.sum(weight, axis=0, keepdims=True)
        prob_ref[head] = prob
        parts.append(nn(value_t[rows_of(head)], prob.astype(BF)))
    ctx_t = jnp.concatenate(parts, axis=0)
    ctx_t_ref[...] = ctx_t.astype(BF)
    y1 = start + nn(ctx_t.T.astype(BF), out_ref[...]) + out_b_ref[1:2]
    y1_ref[...] = y1
    unit, _ = normalise(y1)
    norm_d = (unit * gain_ref[3:4] + shift_ref[3:4]).astype(BF)
    norm_d_ref[...] = norm_d
    cross_q_ref[...] = (nn(norm_d, cross_ref[:, :width]) + in_b_ref[2:3, :width]).astype(BF)


def encoder_forward(
    len_ref, at_ref, x_ref, gain_ref, shift_ref, in_ref, in_b_ref, out_ref, out_b_ref,
    w1_ref, b1_ref, w2_ref, b2_ref, cin_ref,
    qkv_ref, ctx_t_ref, lse_ref, h1_ref, mem_ref, cross_ref,
    value_t, act, between,
):
    rows, width = x_ref.shape
    unit, _ = normalise(x_ref[...].astype(F32))
    norm_a = (unit * gain_ref[0:1] + shift_ref[0:1]).astype(BF)
    qkv_ref[:, :width] = (nn(norm_a, in_ref[:, :width]) + in_b_ref[0:1, :width]).astype(BF)
    key = nn(norm_a, in_ref[:, width : 2 * width]).astype(BF)
    qkv_ref[:, width : 2 * width] = key
    value = (nn(norm_a, in_ref[:, 2 * width :]) + in_b_ref[0:1, width:]).astype(BF)
    qkv_ref[:, 2 * width :] = value
    value_t[...] = value.astype(F32).T.astype(BF)

    def attend(at, pair):
        keys = qkv_ref[:, pl.ds(width + at, 128)]
        queries = qkv_ref[:, pl.ds(at, 128)] * jnp.asarray(HEAD_DIM**-0.5, BF)
        for odd in range(2):
            query = with_one(own_lanes(queries, odd), odd)
            score = nt(with_mask(keys, odd, len_ref[at_ref[0]]), query)
            highest = jnp.max(score, axis=0, keepdims=True)
            weight = jnp.exp(score - highest)
            total = jnp.sum(weight, axis=0, keepdims=True)
            context = nn(value_t[head_rows(at, odd)], weight.astype(BF)) * (1.0 / total)
            ctx_t_ref[head_rows(at, odd)] = context.astype(BF)
            lse_ref[pl.ds(2 * pair + odd, 1)] = highest + jnp.log(total)

    each_pair(attend)
    between()
    context = ctx_t_ref[...].astype(F32).T.astype(BF)
    h1 = x_ref[...].astype(F32) + nn(context, out_ref[...]) + out_b_ref[0:1]
    h1_ref[...] = h1
    unit, _ = normalise(h1)
    norm_b = (unit * gain_ref[1:2] + shift_ref[1:2]).astype(BF)

    hidden = nn(norm_b, w1_ref[...]) + b1_ref[0:1]
    act[...] = gelu_value(hidden).astype(BF)
    memory = (h1_ref[...] + nn(act[...], w2_ref[...]) + b2_ref[0:1]).astype(BF)
    mem_ref[...] = memory
    cross_ref[:, :width] = nn(memory, cin_ref[:, width : 2 * width]).astype(BF)
    cross_ref[:, width:] = (nn(memory, cin_ref[:, 2 * width :]) + in_b_ref[2:3, width:]).astype(BF)


def decoder_main(
    tok_ref, len_ref, at_ref, core_ref,
    y1_ref, norm_d_ref, cross_q_ref, cross_ref, mem_ref, cot_ref, gain_ref, shift_ref,
    in2_ref, out2_ref, out_b_ref, w1_ref, b1_ref, w2_ref, b2_ref,
    dec_ref, dmem_ref, early_ref, grad_ref, small_ref,
    probs, turned, cross_t, dkv, dq_t, fed,
):
    text, width = y1_ref.shape
    hidden_size = w1_ref.shape[1]
    slot = (core_ref[0], 1 - core_ref[0])
    small_ref[...] = jnp.zeros_like(small_ref)
    turned[...] = cross_ref[:, width:].astype(F32).T.astype(BF)

    def attend(at, pair):
        queries = both_heads(cross_q_ref[:, pl.ds(at, 128)] * jnp.asarray(HEAD_DIM**-0.5, BF))
        score = nt(cross_ref[:, pl.ds(at, 128)], queries)
        frame = lax.broadcasted_iota(jnp.int32, score.shape, 0)
        score = jnp.where(frame < len_ref[at_ref[0]], score, MASKED)
        weight = jnp.exp(score - jnp.max(score, axis=0, keepdims=True))
        prob = weight * (1.0 / jnp.sum(weight, axis=0, keepdims=True))
        probs[pair] = prob
        full = nn(turned[pl.ds(at, 128)], prob.astype(BF))
        for odd in range(2):
            cross_t[head_rows(at, odd)] = full[HEAD_DIM * odd : HEAD_DIM * odd + HEAD_DIM, text * odd : text * odd + text]

    each_pair(attend)
    context_t = cross_t[...]
    y2 = y1_ref[...] + nn(context_t.T.astype(BF), out2_ref[...]) + out_b_ref[2:3]
    unit_e, scale_e = normalise(y2)
    norm_e = (unit_e * gain_ref[4:5] + shift_ref[4:5]).astype(BF)
    norm_e_t = norm_e.astype(F32).T.astype(BF)
    valid = lax.broadcasted_iota(jnp.int32, (text, 1), 0) < tok_ref[0]
    grad_low = jnp.where(valid, cot_ref[...], jnp.zeros_like(cot_ref))
    grad = grad_low.astype(F32)
    grad_low_t = grad.T.astype(BF)
    chunk = 512

    def feed(index, sums):
        part = pl.ds(pl.multiple_of(index * chunk, chunk), chunk)
        hidden = nn(norm_e, w1_ref[:, part]) + b1_ref[1:2, part]
        value, slope = gelu_both(hidden)
        active = value.astype(BF)
        grad_hidden = (nt(grad_low, w2_ref[part]) * slope).astype(BF)
        bias = col_sum(grad_hidden)
        first = nn(norm_e_t, grad_hidden).astype(BF)
        for sub in range(chunk // width):
            row = index * (chunk // width) + sub
            small_ref[pl.ds(16 + row, 1)] = bias[:, width * sub : width * sub + width]
            at = pl.multiple_of(row * width, width)
            early_ref[slot[0], pl.ds(at, width)] = first[:, width * sub : width * sub + width]
        second = nn(grad_low_t, active).T.astype(BF)
        at = pl.multiple_of(jnp.where(index == 0, hidden_size, (index - 1) * chunk), chunk)
        early_ref[jnp.where(index == 0, slot[0], slot[1]), pl.ds(at, chunk)] = second
        return sums[0] + nn(active, w2_ref[part]), sums[1] + nt(grad_hidden, w1_ref[:, part])

    zeros = jnp.zeros((text, width), F32)
    feed_out, grad_norm = lax.fori_loop(0, hidden_size // chunk, feed, (zeros, zeros))
    fed()
    y3 = y2 + b2_ref[1:2] + feed_out
    dec_ref[...] = jnp.where(valid, y3, 0.0).astype(BF)
    small_ref[4:5] = col_sum(grad)
    grad_x, small_ref[0:1], small_ref[1:2] = norm_backward(grad_norm, unit_e, scale_e, gain_ref[4:5])
    grad = grad + grad_x
    grad_low = grad.astype(BF)
    small_ref[5:6] = col_sum(grad_low)
    base = hidden_size - chunk
    early_ref[slot[1], base + 3 * width :] = nn(context_t.astype(BF), grad_low).astype(BF)
    grad_ctx = nt(grad_low, out2_ref[...]).astype(BF)
    turned[...] = cross_ref[:, :width].astype(F32).T.astype(BF)
    mem_t = mem_ref[...].astype(F32).T.astype(BF)
    grad_ref[...] = grad_ctx.astype(F32)

    def attend_backward(at, pair):
        queries = both_heads(cross_q_ref[:, pl.ds(at, 128)] * jnp.asarray(HEAD_DIM**-0.5, BF))
        grads = both_heads(grad_ref[:, pl.ds(at, 128)].astype(BF))
        prob = probs[pair]
        dprob = nt(cross_ref[:, pl.ds(width + at, 128)], grads)
        inner = jnp.sum(dprob * prob, axis=0, keepdims=True)
        dscore = (prob * (dprob - inner)).astype(BF)
        dkv[:, pl.ds(at, 128)] = nn(dscore, queries).astype(BF)
        dkv[:, pl.ds(width + at, 128)] = nn(prob.astype(BF), grads).astype(BF)
        full = nn(turned[pl.ds(at, 128)], dscore)
        for odd in range(2):
            dq_t[head_rows(at, odd)] = full[HEAD_DIM * odd : HEAD_DIM * odd + HEAD_DIM, text * odd : text * odd + text]

    each_pair(attend_backward)
    dq = (dq_t[...] * HEAD_DIM**-0.5).T.astype(BF)
    small_ref[6:7] = col_sum(dq)
    small_ref[7:8] = col_sum(dkv[:, width:])
    norm_d = norm_d_ref[...]
    early_ref[slot[1], base : base + width] = nn(norm_d.astype(F32).T.astype(BF), dq).astype(BF)
    pairs = nn(mem_t, dkv[...]).astype(BF)
    early_ref[slot[1], base + width : base + 2 * width] = pairs[:, :width]
    early_ref[slot[1], base + 2 * width : base + 3 * width] = pairs[:, width:]
    dmem_ref[...] = nt(dkv[...], in2_ref[:, width:]).astype(BF)
    unit, scale = normalise(y1_ref[...])
    grad_x, small_ref[8:9], small_ref[9:10] = norm_backward(
        nt(dq, in2_ref[:, :width]), unit, scale, gain_ref[3:4]
    )
    grad_ref[...] = grad + grad_x


def decoder_self_backward(
    emb_ref, norm_c_ref, qkv_ref, ctx_t_ref, prob_ref, grad_ref, small_ref, gain_ref, in1_ref, out1_ref,
    late_ref, swap_ref,
):
    text, width = emb_ref.shape
    grad = grad_ref[...]
    grad_low = grad.astype(BF)
    small_ref[10:11] = col_sum(grad_low)
    dout1 = nn(ctx_t_ref[...], grad_low).astype(BF)
    late_ref[3 * width :] = dout1[: width - SPILL]
    swap_ref[text + SMALL :] = dout1[width - SPILL :]
    grad_ctx = nt(grad_low, out1_ref[...]).astype(BF)
    key_t = qkv_ref[:, width : 2 * width].astype(F32).T.astype(BF)
    scaled = qkv_ref[:, :width] * jnp.asarray(HEAD_DIM**-0.5, BF)
    dkeys = []
    dvalues = []
    dquery = []
    for pair in range(HEADS // 2):
        dkey = 0.0
        dvalue = 0.0
        for head in (2 * pair, 2 * pair + 1):
            lanes = lanes_of(head)
            own_grad = own_lanes(grad_ctx[:, lanes], head)
            prob = prob_ref[head]
            dprob = nt(qkv_ref[:, slice(2 * width + lanes.start, 2 * width + lanes.stop)], own_grad)
            inner = jnp.sum(dprob * prob, axis=0, keepdims=True)
            dscore = (prob * (dprob - inner)).astype(BF)
            dvalue = dvalue + nn(prob.astype(BF), own_grad)
            dkey = dkey + nn(dscore, own_lanes(scaled[:, lanes], head))
            dquery.append(nn(key_t[rows_of(head)], dscore))
        dkeys.append(dkey.astype(BF))
        dvalues.append(dvalue.astype(BF))
    dq_t = jnp.concatenate(dquery, axis=0) * HEAD_DIM**-0.5
    dqkv = jnp.concatenate([dq_t.T.astype(BF)] + dkeys + dvalues, axis=1)
    small_ref[11:12] = col_sum(dqkv[:, :width])
    small_ref[12:13] = col_sum(dqkv[:, 2 * width :])
    din1 = nn(norm_c_ref[...].astype(F32).T.astype(BF), dqkv).astype(BF)
    for part in range(3):
        late_ref[width * part : width * part + width] = din1[:, width * part : width * part + width]
    unit, scale = normalise(emb_ref[...].astype(F32) * math.sqrt(width))
    grad_x, small_ref[13:14], small_ref[14:15] = norm_backward(
        nt(dqkv, in1_ref[...]), unit, scale, gain_ref[2:3]
    )
    swap_ref[:text] = ((grad + grad_x) * math.sqrt(width)).astype(BF)
    swap_ref[text : text + SMALL] = small_ref[...].astype(BF)


def forward_and_decoder(
    tok_ref, len_ref, at_ref, core_ref,
    x_ref, in0, gain_ref, shift_ref, in_b_ref, out_b_ref, b1_ref, b2_ref,
    in_from, out_from, w1_from, w2_from,
    emb_from, y1_from, norm_c_from, dec_qkv_from, dec_ctx_t_from, prob_from, norm_d_from, cross_q_from, cot_from,
    qkv_to, ctx_t_to, h1_to, lse_ref, dec_ref, dmem_to, late_ref, swap_ref, keep_ref, send_ref,
    value_t, act, mem, cross, probs, cross_t, dkv, dq_t, grad, small, early,
    qkv_ref, ctx_t_ref, h1_ref, dmem_ref,
    in_ref, out_ref, w1_ref, w2_ref,
    emb_ref, y1_ref, norm_c_ref, dec_qkv_ref, dec_ctx_t_ref, prob_ref, norm_d_ref, cross_q_ref, cot_ref,
    load_sems, store_sems,
):
    loads = fetch(
        load_sems, (out_from, out_ref), (w1_from, w1_ref), (w2_from, w2_ref), (in_from.at[1:], in_ref),
        (emb_from, emb_ref), (y1_from, y1_ref), (norm_c_from, norm_c_ref), (dec_qkv_from, dec_qkv_ref),
        (dec_ctx_t_from, dec_ctx_t_ref), (prob_from, prob_ref), (norm_d_from, norm_d_ref),
        (cross_q_from, cross_q_ref), (cot_from, cot_ref),
    )
    stores = []

    def send(*pairs):
        for held, ref in pairs:
            stores.append(pltpu.make_async_copy(held, ref, store_sems.at[len(stores)]))
            stores[-1].start()

    def arrived():
        for load in loads:
            load.wait()
        send((qkv_ref, qkv_to), (ctx_t_ref, ctx_t_to))

    in1, in2 = in_ref.at[0], in_ref.at[1]
    out0, out1, out2 = (out_ref.at[i] for i in range(3))
    encoder_forward(
        len_ref, at_ref, x_ref, gain_ref, shift_ref, in0, in_b_ref, out0, out_b_ref,
        w1_ref.at[0], b1_ref, w2_ref.at[0], b2_ref, in2,
        qkv_ref, ctx_t_ref, lse_ref, h1_ref, mem, cross,
        value_t, act, arrived,
    )
    half = early.shape[1]
    full = half - 4 * x_ref.shape[1]
    places = (keep_ref, send_ref)

    def fed():
        send((h1_ref, h1_to), *[(early.at[i, :full], places[i].at[:full]) for i in range(2)])

    decoder_main(
        tok_ref, len_ref, at_ref, core_ref,
        y1_ref, norm_d_ref, cross_q_ref, cross, mem, cot_ref, gain_ref, shift_ref,
        in2, out2, out_b_ref, w1_ref.at[1], b1_ref, w2_ref.at[1], b2_ref,
        dec_ref, dmem_ref, early, grad, small,
        probs, value_t, cross_t, dkv, dq_t, fed,
    )
    send((dmem_ref, dmem_to), *[(early.at[i, full:], places[i].at[full:half]) for i in range(2)])
    decoder_self_backward(
        emb_ref, norm_c_ref, dec_qkv_ref, dec_ctx_t_ref, prob_ref, grad, small, gain_ref, in1, out1,
        late_ref, swap_ref,
    )
    send((swap_ref, send_ref.at[half:]))
    for store in stores:
        store.wait()


def encoder_backward(
    len_ref, at_ref, core_ref,
    h1_ref, dmem_ref, lse_ref, gain_ref, shift_ref, w1_ref, b1_ref, w2_ref,
    x_from, ctx_t_from, qkv_from, late_from, in_from, out_from,
    dx_ref, keep_ref, send_ref,
    grad_hid, dh1, dctx, key_t, dq_t, dqkv, small, feed, attn,
    x_ref, ctx_t_ref, qkv_ref, late_ref, in_ref, out_ref, load_sems, store_sems,
):
    loads = fetch(
        load_sems, (ctx_t_from, ctx_t_ref), (late_from, late_ref), (out_from.at[0], out_ref),
        (qkv_from, qkv_ref), (x_from, x_ref), (in_from.at[0], in_ref),
    )
    hidden = w1_ref.shape[1]
    places = (keep_ref, send_ref)
    stores = []

    def send(*pairs):
        for held, ref in pairs:
            stores.append(pltpu.make_async_copy(held, ref, store_sems.at[len(stores)]))
            stores[-1].start()

    def fed():
        for load in loads:
            load.wait()
        send(*[(feed.at[i, :hidden], places[i].at[:hidden]) for i in range(2)])

    encoder_feed_backward(
        core_ref, h1_ref, dmem_ref, ctx_t_ref, gain_ref, shift_ref, w1_ref, b1_ref, w2_ref, out_ref, late_ref,
        dh1, dctx, feed, small,
        grad_hid, fed,
    )
    cut = feed.shape[1]
    encoder_attention_backward(
        len_ref, at_ref, core_ref, x_ref, qkv_ref, lse_ref, dctx, dh1, gain_ref, shift_ref, in_ref,
        dx_ref, attn,
        key_t, dq_t, dqkv, small,
    )
    send(*[(feed.at[i, hidden:], places[i].at[hidden:cut]) for i in range(2)])
    send(*[(attn.at[i], places[i].at[cut:]) for i in range(2)])
    for store in stores:
        store.wait()


def fetch(sems, *pairs):
    copies = [pltpu.make_async_copy(ref, held, sems.at[i]) for i, (ref, held) in enumerate(pairs)]
    for copy in copies:
        copy.start()
    return copies


def early_merge(
    core_ref, ids_ref, swap_from, keep_ref, other_ref, out_ref, swap_ref, keep, other, swapped_ref, out, sems, out_sems
):
    core = core_ref[0]
    text = ids_ref.shape[1] // 2
    half = keep.shape[0]
    chunk = half // 4
    loads = fetch(
        sems, (swap_from, swap_ref), (other_ref.at[half:], swapped_ref), (keep_ref, keep),
        (other_ref.at[:half], other),
    )
    loads[0].wait()
    loads[1].wait()
    grad = jnp.concatenate([swap_ref[:text], swapped_ref[:text]], axis=0)
    for at in range(0, half, chunk):
        row = lax.broadcasted_iota(jnp.int32, (chunk, 2 * text), 0) + (core * half + at)
        hot = jnp.where(row == ids_ref[...], 1.0, 0.0).astype(BF)
        out[half + at : half + at + chunk] = nn(hot, grad).astype(BF)

    @pl.when(core == 1)
    def _():
        rest = swap_ref[text:].astype(F32) + swapped_ref[text:].astype(F32)
        out[2 * half - rest.shape[0] :] = rest.astype(BF)

    table = pltpu.make_async_copy(out.at[half:], out_ref.at[half:], out_sems.at[0])
    table.start()
    for load in loads[2:]:
        load.wait()
    out[:half] = (keep[...].astype(F32) + other[...].astype(F32)).astype(BF)
    sums = pltpu.make_async_copy(out.at[:half], out_ref.at[:half], out_sems.at[1])
    sums.start()
    table.wait()
    sums.wait()


def late_merge(keep_ref, other_ref, early_ref, out_ref, keep, other, early, out, sems, out_sems):
    count, size, width = out.shape
    size = size - early.shape[1]
    loads = fetch(sems, (early_ref, early), (keep_ref, keep), (other_ref, other))
    loads[0].wait()
    own = jnp.sum(early[...].astype(F32), axis=0).astype(BF)
    for load in loads[1:]:
        load.wait()
    stores = []
    part = count // 4
    for step in range(4):
        rows = slice(step * part * size, (step + 1) * part * size)
        places = slice(step * part, step * part + part)
        late = (keep[rows].astype(F32) + other[rows].astype(F32)).astype(BF)
        out[places, :size] = late.reshape(part, size, width)
        for place in range(step * part, step * part + part):
            out[place, size:] = own
        stores.append(pltpu.make_async_copy(out.at[places], out_ref.at[places], out_sems.at[step]))
        stores[-1].start()
    for store in stores:
        store.wait()


def late_spread(parts_ref, out_ref, parts, out, sems, out_sems):
    size = out.shape[1]
    half = out.shape[0] // 2
    ends = (slice(0, half), slice(half, 2 * half))
    loads = fetch(sems, *[(parts_ref.at[end, :size], parts.at[end]) for end in ends])
    total = 0.0
    for load, end in zip(loads, ends):
        load.wait()
        total = total + jnp.sum(parts[end].astype(F32), axis=0)
    late = total.astype(BF)
    stores = []
    for step, end in enumerate(ends):
        for place in range(end.start, end.stop):
            out[place] = late
        stores.append(pltpu.make_async_copy(out.at[end], out_ref.at[end], out_sems.at[step]))
        stores[-1].start()
    for store in stores:
        store.wait()


def early_outputs(
    core_ref, rate_ref, mine_ref, other_ref,
    table_ref, in_ref, out_ref, w1_ref, w2_ref, rest_ref,
    grads, table, sems,
):
    rate = rate_ref[0]
    first = core_ref[0] == 0
    count, size, width = mine_ref.shape
    hidden = w2_ref.shape[1]
    half = grads.shape[0] // 2
    each = 2 * half // count
    skip = size - each

    def chunk(index, carry):
        at = pl.multiple_of(index * each, each)
        for part, held in ((0, grads), (count // 2, table)):
            mine, other = mine_ref[part + index, skip:], other_ref[part + index, skip:]
            held[pl.ds(at, each)] = jnp.where(first, mine, other).astype(F32) * rate
            held[pl.ds(half + at, each)] = jnp.where(first, other, mine).astype(F32) * rate
        return carry

    lax.fori_loop(0, count // 2, chunk, 0)
    tail = mine_ref[count - 2 :, skip:].reshape(2 * each, width)
    other_tail = other_ref[count - 2 :, skip:].reshape(2 * each, width)
    rest_ref[...] = jnp.where(first, other_tail, tail)[2 * each - rest_ref.shape[0] :]
    base = 2 * hidden
    pairs = [(table.at[: table_ref.shape[0]], table_ref), (grads.at[hidden:base], w2_ref.at[1])]
    pairs += [(grads.at[at : at + width], w1_ref.at[1, :, at : at + width]) for at in range(0, hidden, width)]
    pairs += [
        (grads.at[base + at : base + at + width], in_ref.at[2, :, at : at + width])
        for at in range(0, 3 * width, width)
    ]
    pairs.append((grads.at[base + 3 * width :], out_ref.at[2]))
    hand_out(sems, *pairs)


def late_outputs(
    half_ref, rate_ref, early_ref, rows_ref, in_in, out_in, w1_in, w2_in,
    in_ref, out_ref, w1_ref, w2_ref, rest_ref,
    rows, grads, sems, out_sems,
):
    size, width = rows.shape
    hidden = w2_ref.shape[1]
    cut = (width - SPILL) // 2
    base = hidden + 2 * width
    attn = base + cut
    over = size - attn - width
    (load,) = fetch(sems, (rows_ref, rows))
    load.wait()

    def scale(index, carry):
        part = pl.ds(pl.multiple_of(index * width, width), width)
        grads[part] = rows[part].astype(F32) * rate_ref[0]
        return carry

    lax.fori_loop(0, size // width, scale, 0)
    grads[size:] = early_ref[SMALL:].astype(F32) * rate_ref[0]
    rest_ref[...] = rows[size - 2 * SMALL : size - SMALL]

    def block(at, rows=width):
        return grads.at[at : at + rows]

    def first():
        pairs = [(block(at), w1_ref.at[0, :, at : at + width]) for at in range(0, hidden, width)]
        pairs += [(block(hidden + at), in_ref.at[1, :, at : at + width]) for at in (0, width)]
        pairs.append((block(base, cut), out_ref.at[1, :cut]))
        pairs.append((block(attn), in_ref.at[0, :, :width]))
        pairs.append((block(attn + width, over), in_ref.at[0, :over, width : 2 * width]))
        return pairs

    def second():
        pairs = [(block(0, hidden), w2_ref.at[0])]
        pairs.append((block(hidden), in_ref.at[1, :, 2 * width :]))
        pairs.append((block(hidden + width), out_ref.at[0]))
        pairs.append((block(base, cut), out_ref.at[1, cut : 2 * cut]))
        pairs.append((block(size, SPILL), out_ref.at[1, 2 * cut :]))
        pairs.append((block(attn, width - over), in_ref.at[0, over:, width : 2 * width]))
        pairs.append((block(attn + width - over), in_ref.at[0, :, 2 * width :]))
        return pairs

    @pl.when(half_ref[0] == 0)
    def _():
        hand_out(out_sems, *first())

    @pl.when(half_ref[0] == 1)
    def _():
        hand_out(out_sems, *second())


def small_outputs(
    core_ref, rate_ref, mine_ref, other_ref, early_ref,
    gain_ref, shift_ref, in_b_ref, out_b_ref, b1_ref, b2_ref,
):
    width = mine_ref.shape[1]
    rate = rate_ref[0]
    enc = jnp.where(core_ref[0] == 1, mine_ref[...], other_ref[...]).astype(F32) * rate
    dec = early_ref[:SMALL].astype(F32) * rate
    for row, (part, at) in enumerate(((enc, 0), (enc, 8), (dec, 13), (dec, 8), (dec, 0))):
        gain_ref[row : row + 1] = part[at : at + 1]
        shift_ref[row : row + 1] = part[at + 1 : at + 2]
    for row, (part, at, next_at) in enumerate(((enc, 2, 3), (dec, 11, 12), (dec, 6, 7))):
        in_b_ref[row : row + 1, :width] = part[at : at + 1]
        in_b_ref[row : row + 1, width:] = part[next_at : next_at + 1]
    for row, (part, at) in enumerate(((enc, 11), (dec, 10), (dec, 5))):
        out_b_ref[row : row + 1] = part[at : at + 1]
    for row, (part, at) in enumerate(((enc, 10), (dec, 4))):
        b2_ref[row : row + 1] = part[at : at + 1]
    for row, part in enumerate((enc, dec)):
        for block in range(b1_ref.shape[1] // width):
            b1_ref[row : row + 1, width * block : width * block + width] = part[16 + block : 17 + block]


def frames_back(place_ref, own_ref, next_ref, second_ref, third_ref, out_ref):
    count = out_ref.shape[0]
    for shift, ref in enumerate((own_ref, next_ref, second_ref, third_ref)):
        out_ref[lax.rem(place_ref[0] + (count - shift), count)] = ref[...].astype(F32)


def encoder_feed_backward(
    core_ref, h1_ref, dmem_ref, ctx_t_ref, gain_ref, shift_ref, w1_ref, b1_ref, w2_ref, out_ref, late_ref,
    dh1_ref, dctx_ref, feed_ref, small_ref,
    grad_hid, fed,
):
    width = h1_ref.shape[1]
    hidden_size = w1_ref.shape[1]
    slot = (core_ref[0], 1 - core_ref[0])
    cut = (width - SPILL) // 2
    small_ref[...] = jnp.zeros_like(small_ref)
    unit, _ = normalise(h1_ref[...])
    norm_b = unit * gain_ref[1:2] + shift_ref[1:2]
    norm_b_t = norm_b.T.astype(BF)
    norm_b = norm_b.astype(BF)
    grad_low = dmem_ref[...]
    grad_low_t = grad_low.astype(F32).T.astype(BF)
    chunk = FEED_CHUNK

    def feed(index, carry):
        part = pl.ds(pl.multiple_of(index * chunk, chunk), chunk)
        hidden = nn(norm_b, w1_ref[:, part]) + b1_ref[0:1, part]
        value, slope = gelu_both(hidden)
        grad_hidden = (nt(grad_low, w2_ref[part]) * slope).astype(BF)
        grad_hid[:, part] = grad_hidden
        bias = col_sum(grad_hidden)
        first = nn(norm_b_t, grad_hidden).astype(BF)
        for sub in range(chunk // width):
            row = index * (chunk // width) + sub
            small_ref[pl.ds(16 + row, 1)] = bias[:, width * sub : width * sub + width]
            at = pl.multiple_of(row * width, width)
            feed_ref[slot[0], pl.ds(at, width)] = first[:, width * sub : width * sub + width]
        feed_ref[slot[1], part] = nn(grad_low_t, value.astype(BF)).T.astype(BF)
        return carry

    lax.fori_loop(0, hidden_size // chunk, feed, 0)
    fed()
    feed_ref[slot[0], hidden_size : hidden_size + 2 * width] = late_ref[: 2 * width]
    feed_ref[slot[1], hidden_size : hidden_size + width] = late_ref[2 * width : 3 * width]
    feed_ref[slot[0], hidden_size + 2 * width :] = late_ref[3 * width : 3 * width + cut]
    feed_ref[slot[1], hidden_size + 2 * width :] = late_ref[3 * width + cut :]
    grad = grad_low.astype(F32)
    small_ref[10:11] = col_sum(grad)
    unit, scale = normalise(h1_ref[...])
    grad_x, small_ref[8:9], small_ref[9:10] = norm_backward(
        nt(grad_hid[...], w1_ref[...]), unit, scale, gain_ref[1:2]
    )
    grad = grad + grad_x
    dh1_ref[...] = grad
    grad_low = grad.astype(BF)
    small_ref[11:12] = col_sum(grad_low)
    feed_ref[slot[1], hidden_size + width : hidden_size + 2 * width] = nn(ctx_t_ref[...], grad_low).astype(BF)
    dctx_ref[...] = nt(grad_low, out_ref[...]).astype(BF)


def encoder_attention_backward(
    len_ref, at_ref, core_ref, x_ref, qkv_ref, lse_ref, dctx_ref, dh1_ref, gain_ref, shift_ref, in_ref,
    dx_ref, attn_ref,
    key_t, dq_t, dqkv, small_ref,
):
    rows, width = x_ref.shape
    key_t[...] = qkv_ref[:, width : 2 * width].astype(F32).T.astype(BF)

    def attend_backward(at, pair):
        keys = qkv_ref[:, pl.ds(width + at, 128)]
        values = qkv_ref[:, pl.ds(2 * width + at, 128)]
        queries = qkv_ref[:, pl.ds(at, 128)] * jnp.asarray(HEAD_DIM**-0.5, BF)
        grads = dctx_ref[:, pl.ds(at, 128)]
        dkey = 0.0
        dvalue = 0.0
        for odd in range(2):
            query = own_lanes(queries, odd)
            score = nt(with_mask(keys, odd, len_ref[at_ref[0]]), with_one(query, odd))
            prob = jnp.exp(score - lse_ref[pl.ds(2 * pair + odd, 1)])
            own_grad = own_lanes(grads, odd)
            dprob = nt(values, own_grad)
            inner = jnp.sum(dprob * prob, axis=0, keepdims=True)
            dscore = (prob * (dprob - inner)).astype(BF)
            dkey = dkey + nn(dscore, query)
            dvalue = dvalue + nn(prob.astype(BF), own_grad)
            dq_t[head_rows(at, odd)] = nn(key_t[head_rows(at, odd)], dscore)
        dqkv[:, pl.ds(width + at, 128)] = dkey.astype(BF)
        dqkv[:, pl.ds(2 * width + at, 128)] = dvalue.astype(BF)

    each_pair(attend_backward)
    dqkv[:, :width] = (dq_t[...].T * HEAD_DIM**-0.5).astype(BF)
    small_ref[2:3] = col_sum(dqkv[:, :width])
    small_ref[3:4] = col_sum(dqkv[:, 2 * width :])
    unit, scale = normalise(x_ref[...].astype(F32))
    norm_a = unit * gain_ref[0:1] + shift_ref[0:1]
    din = nn(norm_a.T.astype(BF), dqkv[...]).astype(BF)
    blocks = [din[:, width * part : width * part + width] for part in range(3)]
    grad_x, small_ref[0:1], small_ref[1:2] = norm_backward(
        nt(dqkv[...], in_ref[...]), unit, scale, gain_ref[0:1]
    )
    dx_ref[...] = (dh1_ref[...] + grad_x).astype(BF)
    small = small_ref[...].astype(BF)
    packed = jnp.concatenate(blocks + [small, jnp.zeros_like(small)], axis=0)
    half = attn_ref.shape[1]
    attn_ref[core_ref[0]] = packed[:half]
    attn_ref[1 - core_ref[0]] = packed[half:]


def swap_cores(array):
    return lax.ppermute(array, "core", [(0, 1), (1, 0)])


def body(
    frames, utt_len, token_ids, tok_len, step, embed, norm_gain, norm_bias, attn_in, attn_in_bias,
    attn_out, attn_out_bias, ff_in, ff_in_bias, ff_out, ff_out_bias, cotangent,
):
    ring = ("frame", "pair")
    devices = lax.axis_size(ring)
    core = lax.axis_index("core")
    core_of = core[None]
    frame_at = lax.axis_index("frame")
    vocab, width = embed.shape
    hidden = ff_in.shape[2]
    frame_count = lax.axis_size("frame")
    local_len = frames.shape[2]
    rows = local_len * frame_count
    text = token_ids.shape[2]
    lengths = utt_len[0]
    frame_of = frame_at[None]
    my_tok = tok_len[0]
    arrived = lax.all_to_all(frames[0], "frame", split_axis=0, concat_axis=1, tiled=True)
    source = arrived.reshape(rows, width)
    ids = token_ids[0, 0]
    both_ids = jnp.concatenate([ids, swap_cores(ids)])[None]
    rows_in, both_ids = lax.optimization_barrier((embed[ids], both_ids))
    count_step = step[0].astype(F32)
    rate = jnp.minimum(lax.rsqrt(count_step), count_step * WARMUP ** (-1.5)) * WARMUP**0.5
    rate = rate[None]

    y1, norm_c, dec_qkv, dec_ctx_t, dec_prob, norm_d, cross_q = call(
        decoder_start,
        [
            ((text, width), F32), ((text, width), BF), ((text, 3 * width), BF), ((width, text), BF),
            ((HEADS, text, text), F32), ((text, width), BF), ((text, width), BF),
        ],
        [
            rows_in, norm_gain, norm_bias, (attn_in, 1), attn_in_bias, (attn_out, 1),
            attn_out_bias, (attn_in, 2),
        ],
        [my_tok],
        flops=2 * text * width * width * 5,
    )
    half = 2 * width + hidden
    swap_rows = text + SMALL + SPILL
    decoder_args = [rows_in, y1, norm_c, dec_qkv, dec_ctx_t, dec_prob, norm_d, cross_q, cotangent[0, 0]]
    enc_qkv, enc_ctx_t, h1, lse, dec_out, dmem, self_grads, swap, early, early_send = call(
        forward_and_decoder,
        [
            ((rows, 3 * width), BF, None), ((width, rows), BF, None), ((rows, width), F32, None),
            ((8, rows), F32), ((text, width), BF), ((rows, width), BF, None), ((4 * width - SPILL, width), BF),
            ((swap_rows, width), BF), ((half, width), BF, None), ((half + swap_rows, width), BF, None),
        ],
        [
            source, (attn_in, 0), norm_gain, norm_bias, attn_in_bias, attn_out_bias, ff_in_bias, ff_out_bias,
            (attn_in, None), (attn_out, None), (ff_in, None), (ff_out, None),
        ]
        + [(arg, None) for arg in decoder_args],
        [my_tok, lengths, frame_of, core_of],
        [
            pltpu.VMEM((width, rows), BF), pltpu.VMEM((rows, hidden), BF), pltpu.VMEM((rows, width), BF),
            pltpu.VMEM((rows, 2 * width), BF), pltpu.VMEM((HEADS // 2, rows, 2 * text), F32),
            pltpu.VMEM((width, text), F32), pltpu.VMEM((rows, 2 * width), BF),
            pltpu.VMEM((width, text), F32), pltpu.VMEM((text, width), F32),
            pltpu.VMEM((SMALL, width), F32), pltpu.VMEM((2, half, width), BF),
            pltpu.VMEM((rows, 3 * width), BF), pltpu.VMEM((width, rows), BF), pltpu.VMEM((rows, width), F32),
            pltpu.VMEM((rows, width), BF),
            pltpu.VMEM((2,) + attn_in.shape[1:], BF), pltpu.VMEM(attn_out.shape, BF),
            pltpu.VMEM(ff_in.shape, BF), pltpu.VMEM(ff_out.shape, BF),
        ]
        + [pltpu.VMEM(arg.shape, arg.dtype) for arg in decoder_args]
        + [pltpu.SemaphoreType.DMA((13,)), pltpu.SemaphoreType.DMA((9,))],
        flops=2 * rows * width * (10 * width + 2 * rows + 2 * hidden)
        + 2 * text * width * (6 * hidden + 7 * rows + 26 * width),
    )
    (early_sum,) = call(
        early_merge,
        [((2 * half, width), BF, None)],
        [both_ids, (swap, None), (early, None), (swap_cores(early_send), "vmem")],
        [core_of],
        [
            pltpu.VMEM((swap_rows, width), BF), pltpu.VMEM((half, width), BF), pltpu.VMEM((half, width), BF),
            pltpu.VMEM((swap_rows, width), BF), pltpu.VMEM((2 * half, width), BF),
            pltpu.SemaphoreType.DMA((4,)), pltpu.SemaphoreType.DMA((2,)),
        ],
        flops=4 * half * width * text,
        limit=20,
    )
    early_sum, dmem = lax.optimization_barrier((early_sum, dmem))
    early_parts = lax.all_to_all(
        early_sum.reshape(devices, -1, width), ring, split_axis=0, concat_axis=0, tiled=True
    )
    early_own = jnp.sum(early_parts.astype(F32), axis=0).astype(BF)

    feed_half = (5 * width - SPILL) // 2 + hidden
    attn_half = 3 * width // 2 + SMALL
    late_half = feed_half + attn_half
    dx, late, late_send = call(
        encoder_backward,
        [((rows, width), BF), ((late_half, width), BF, None), ((late_half, width), BF, None)],
        [
            h1, dmem, lse, norm_gain, norm_bias, (ff_in, 0), ff_in_bias, (ff_out, 0), (source, None),
            (enc_ctx_t, None), (enc_qkv, None), (self_grads, None), (attn_in, None), (attn_out, None),
        ],
        [lengths, frame_of, core_of],
        [
            pltpu.VMEM((rows, hidden), BF), pltpu.VMEM((rows, width), F32), pltpu.VMEM((rows, width), BF),
            pltpu.VMEM((width, rows), BF), pltpu.VMEM((width, rows), F32), pltpu.VMEM((rows, 3 * width), BF),
            pltpu.VMEM((SMALL, width), F32), pltpu.VMEM((2, feed_half, width), BF),
            pltpu.VMEM((2, attn_half, width), BF),
            pltpu.VMEM((rows, width), BF), pltpu.VMEM((width, rows), BF), pltpu.VMEM((rows, 3 * width), BF),
            pltpu.VMEM(self_grads.shape, BF), pltpu.VMEM((width, 3 * width), BF), pltpu.VMEM((width, width), BF),
            pltpu.SemaphoreType.DMA((6,)), pltpu.SemaphoreType.DMA((6,)),
        ],
        flops=2 * rows * width * (5 * hidden + 5 * rows + 8 * width),
    )
    late_size = late_half // devices
    early_size = 2 * half // devices
    mixed_shape = (devices, late_size + early_size, width)
    (mixed,) = call(
        late_merge,
        [(mixed_shape, BF, None)],
        [(late, None), (swap_cores(late_send), None), (early_parts, None)],
        scratch=[
            pltpu.VMEM((late_half, width), BF), pltpu.VMEM((late_half, width), BF),
            pltpu.VMEM((devices, early_size, width), BF), pltpu.VMEM(mixed_shape, BF),
            pltpu.SemaphoreType.DMA((3,)), pltpu.SemaphoreType.DMA((4,)),
        ],
        limit=24,
    )
    mixed = lax.all_to_all(mixed, ring, split_axis=0, concat_axis=0, tiled=True)
    chunks = dx.reshape(frame_count, local_len, width)
    moved = []
    for shift in range(frame_count):
        target = lax.rem(frame_at + shift, frame_count)
        chunk = lax.dynamic_index_in_dim(chunks, target, keepdims=False)
        if shift:
            chunk = lax.ppermute(chunk, "frame", [(i, (i + shift) % frame_count) for i in range(frame_count)])
        moved.append(chunk)
    mixed, moved = lax.optimization_barrier((mixed, moved))
    late_shape = (devices, late_size, width)
    (late_own,) = call(
        late_spread,
        [(late_shape, BF, None)],
        [(mixed, None)],
        scratch=[
            pltpu.VMEM(late_shape, BF), pltpu.VMEM(late_shape, BF),
            pltpu.SemaphoreType.DMA((2,)), pltpu.SemaphoreType.DMA((2,)),
        ],
    )
    early_other = swap_cores(mixed)
    (frames_grad,) = call(
        frames_back, [((frame_count, local_len, width), F32)], moved, [frame_of], limit=16
    )
    late_mine = lax.all_to_all(late_own, ring, split_axis=0, concat_axis=0, tiled=True)
    in_shape = (3, width, 3 * width)
    out_shape = (3, width, width)
    w1_shape = (2, width, hidden)
    w2_shape = (2, hidden, width)
    table_grad, in_grad, out_grad, w1_grad, w2_grad, early_rest = call(
        early_outputs,
        [
            ((vocab, width), F32, None), (in_shape, F32, None), (out_shape, F32, None),
            (w1_shape, F32, None), (w2_shape, F32, None), ((SMALL + SPILL, width), BF),
        ],
        [mixed, early_other],
        [core_of, rate],
        [
            pltpu.VMEM((2 * half, width), F32), pltpu.VMEM((2 * half, width), F32),
            pltpu.SemaphoreType.DMA((14,)),
        ],
        limit=40,
    )
    late_mine, early_rest, frames_grad = lax.optimization_barrier((late_mine, early_rest, frames_grad))
    late_mine = late_mine.reshape(late_half, width)
    late_other = swap_cores(late_mine)
    results = (in_grad, out_grad, w1_grad, w2_grad)
    rests = []
    for rows_of_half, which in ((late_mine, core_of), (late_other, 1 - core_of)):
        *results, rest = call(
            late_outputs,
            [
                (in_shape, F32, None), (out_shape, F32, None), (w1_shape, F32, None),
                (w2_shape, F32, None), ((SMALL, width), BF),
            ],
            [early_rest, (rows_of_half, "vmem")] + [(result, None) for result in results],
            [which, rate],
            [
                pltpu.VMEM((late_half, width), BF), pltpu.VMEM((late_half + SPILL, width), F32),
                pltpu.SemaphoreType.DMA((1,)), pltpu.SemaphoreType.DMA((16,)),
            ],
            aliases={4: 0, 5: 1, 6: 2, 7: 3},
            limit=16,
        )
        rests.append(rest)
    in_grad, out_grad, w1_grad, w2_grad = results
    gain_grad, shift_grad, in_b_grad, out_b_grad, b1_grad, b2_grad = call(
        small_outputs,
        [
            ((5, width), F32), ((5, width), F32), ((3, 2 * width), F32), ((3, width), F32),
            ((2, hidden), F32), ((2, width), F32),
        ],
        rests + [early_rest],
        [core_of, rate],
        limit=32,
    )
    return (
        dec_out[None, None],
        frames_grad[None],
        table_grad,
        gain_grad,
        shift_grad,
        in_grad,
        in_b_grad,
        out_grad,
        out_b_grad,
        w1_grad,
        b1_grad,
        w2_grad,
        b2_grad,
    )


def solution(mesh):
    groups = ("pair", "core")
    frames, batch = mesh.devices.shape
    split = Mesh(mesh.devices.reshape(frames, batch // 2, 2), ("frame",) + groups)
    placed = (
        P(groups, None, "frame", None),
        P(groups, None),
        P(groups, "frame", None),
        P(groups, "frame"),
    ) + (P(),) * 12 + (P(groups, "frame", None, None),)
    results = (P(groups, "frame", None, None), P(groups, None, "frame", None)) + (P(),) * 11
    return jax.shard_map(body, mesh=split, in_specs=placed, out_specs=results, check_vma=False)
```

```python
import functools
import math

import jax
import jax.numpy as jnp
from jax import lax
from jax.experimental import pallas as pl
from jax.experimental.pallas import tpu as pltpu
from jax.sharding import Mesh, PartitionSpec as P

HEADS = 4
HEAD_DIM = 64
WARMUP = 25000
EPSILON = 1e-05
MASKED = -1e30
BF = jnp.bfloat16
F32 = jnp.float32
GELU_A = math.sqrt(2.0 / math.pi)
GELU_B = GELU_A * 0.044715
SMALL = 32
FEED_CHUNK = 512
SPILL = 64


def nn(left, right):
    return lax.dot_general(left, right, (((1,), (0,)), ((), ())), preferred_element_type=F32)


def nt(left, right):
    return lax.dot_general(left, right, (((1,), (1,)), ((), ())), preferred_element_type=F32)


def hand_out(sems, *pairs):
    copies = [pltpu.make_async_copy(held, ref, sems.at[i]) for i, (held, ref) in enumerate(pairs)]
    for copy in copies:
        copy.start()
    for copy in copies:
        copy.wait()


def normalise(states):
    average = jnp.mean(states, axis=-1, keepdims=True)
    centred = states - average
    scale = lax.rsqrt(jnp.mean(centred * centred, axis=-1, keepdims=True) + EPSILON)
    return centred * scale, scale


def norm_backward(grad, unit, scale, gain):
    grad_unit = grad * gain
    mean_grad = jnp.mean(grad_unit, axis=-1, keepdims=True)
    mean_along = jnp.mean(grad_unit * unit, axis=-1, keepdims=True)
    grad_states = scale * (grad_unit - mean_grad - unit * mean_along)
    return grad_states, col_sum(grad * unit), col_sum(grad)


def col_sum(matrix):
    return jnp.sum(matrix.astype(F32), axis=0, keepdims=True)


def gelu_value(hidden):
    inner = hidden * (GELU_A + GELU_B * (hidden * hidden))
    return hidden * (0.5 + 0.5 * jnp.tanh(inner))


def gelu_both(hidden):
    square = hidden * hidden
    bent = jnp.tanh(hidden * (GELU_A + GELU_B * square))
    half = 0.5 + 0.5 * bent
    slope = half + (0.5 * hidden) * (1.0 - bent * bent) * (GELU_A + 3.0 * GELU_B * square)
    return hidden * half, slope


def lanes_of(head):
    return slice(128 * (head // 2), 128 * (head // 2) + 128)


def rows_of(head):
    return slice(HEAD_DIM * head, HEAD_DIM * head + HEAD_DIM)


def each_pair(step):
    def body(pair, carry):
        step(pl.multiple_of(pair * 2 * HEAD_DIM, 2 * HEAD_DIM), pair)
        return carry

    lax.fori_loop(0, HEADS // 2, body, 0)


def head_rows(at, odd):
    return pl.ds(pl.multiple_of(at + HEAD_DIM * odd, HEAD_DIM), HEAD_DIM)


def spread_heads(rows):
    lane = lax.broadcasted_iota(jnp.int32, rows.shape, 1)
    zero = jnp.zeros_like(rows)
    heads = range(0, HEADS * HEAD_DIM, HEAD_DIM)
    own = [jnp.logical_and(lane >= at, lane < at + HEAD_DIM) for at in heads]
    return jnp.concatenate([jnp.where(mine, rows, zero) for mine in own], axis=0)


def own_blocks(full):
    count = full.shape[1] // HEADS
    return jnp.concatenate(
        [full[HEAD_DIM * h : HEAD_DIM * (h + 1), count * h : count * (h + 1)] for h in range(HEADS)], axis=0
    )


def attend_all(keys, values_t, queries, seen):
    score = jnp.where(seen, nt(keys, queries), MASKED)
    weight = jnp.exp(score - jnp.max(score, axis=0, keepdims=True))
    prob = weight * (1.0 / jnp.sum(weight, axis=0, keepdims=True))
    return prob, own_blocks(nn(values_t, prob.astype(BF)))


def attend_all_backward(keys_t, values, queries, grads, prob):
    dprob = nt(values, grads)
    inner = jnp.sum(dprob * prob, axis=0, keepdims=True)
    dscore = (prob * (dprob - inner)).astype(BF)
    dkeys = nn(dscore, queries).astype(BF)
    dvalues = nn(prob.astype(BF), grads).astype(BF)
    return dkeys, dvalues, own_blocks(nn(keys_t, dscore)) * HEAD_DIM**-0.5


def own_lanes(pair, head):
    lane = lax.broadcasted_iota(jnp.int32, pair.shape, 1)
    mine = (lane < HEAD_DIM) if head % 2 == 0 else (lane >= HEAD_DIM)
    return jnp.where(mine, pair, jnp.zeros_like(pair))


def both_heads(pair):
    return jnp.concatenate([own_lanes(pair, 0), own_lanes(pair, 1)], axis=0)


def spare_lane(head):
    return HEAD_DIM if head % 2 == 0 else 0


def with_one(query, head):
    lane = lax.broadcasted_iota(jnp.int32, query.shape, 1)
    return jnp.where(lane == spare_lane(head), jnp.ones_like(query), query)


def with_mask(key_pair, head, length):
    lane = lax.broadcasted_iota(jnp.int32, key_pair.shape, 1)
    row = lax.broadcasted_iota(jnp.int32, key_pair.shape, 0)
    bias = jnp.where(row < length, 0.0, MASKED).astype(BF)
    return jnp.where(lane == spare_lane(head), bias, key_pair)


def part_spec(shape, layers, at):
    index = (at,) + (0,) * (len(shape) - 1)
    return pl.BlockSpec((layers,) + shape[1:], lambda *g: index, pipeline_mode=pl.Buffered(1))


def call(kernel, outs, args, scalars=(), scratch=(), flops=0, aliases=None, limit=61):
    in_specs = []
    for a in args:
        if not isinstance(a, tuple):
            in_specs.append(part_spec(a.shape, a.shape[0], 0))
        elif a[1] is None or a[1] == "vmem":
            in_specs.append(pl.BlockSpec(memory_space=pl.ANY))
        else:
            in_specs.append(part_spec(a[0].shape, None, a[1]))
    spaces = {None: pltpu.HBM, "vmem": pltpu.VMEM}
    args = [a if isinstance(a, tuple) else (a, 0) for a in args]
    args = [a[0] if isinstance(a[1], int) else pltpu.with_memory_space_constraint(a[0], spaces[a[1]]) for a in args]
    out_specs = []
    for out in outs:
        if out[-1] is None:
            out_specs.append(pl.BlockSpec(memory_space=pltpu.HBM))
        elif isinstance(out[-1], int):
            out_specs.append(part_spec(out[0], out[2], out[3]))
        else:
            out_specs.append(part_spec(out[0], out[0][0], 0))
    size = sum(a.size * a.dtype.itemsize for a in args)
    size += sum(math.prod(out[0]) * jnp.dtype(out[1]).itemsize for out in outs)
    return pl.pallas_call(
        kernel,
        grid_spec=pltpu.PrefetchScalarGridSpec(
            num_scalar_prefetch=len(scalars),
            grid=(1,),
            in_specs=in_specs,
            out_specs=out_specs,
            scratch_shapes=list(scratch),
        ),
        out_shape=[
            (pltpu.HBM if out[-1] is None else jax.ShapeDtypeStruct)(out[0], out[1]) for out in outs
        ],
        input_output_aliases=aliases or {},
        compiler_params=pltpu.CompilerParams(vmem_limit_bytes=limit * 1024 * 1024),
        cost_estimate=pl.CostEstimate(flops=flops, bytes_accessed=size, transcendentals=0),
        name=kernel.__name__,
    )(*scalars, *args)


def decoder_start(
    tok_ref, emb_ref, gain_ref, shift_ref, in_ref, in_b_ref, out_ref, out_b_ref, cross_ref,
    y1_ref, norm_c_ref, qkv_ref, ctx_t_ref, prob_ref, norm_d_ref, cross_q_ref,
):
    text = emb_ref.shape[0]
    width = emb_ref.shape[1]
    start = emb_ref[...].astype(F32) * math.sqrt(width)
    unit, _ = normalise(start)
    norm_c = (unit * gain_ref[2:3] + shift_ref[2:3]).astype(BF)
    norm_c_ref[...] = norm_c
    flat = nn(norm_c, in_ref[...])
    query = (flat[:, :width] + in_b_ref[1:2, :width]).astype(BF)
    key = flat[:, width : 2 * width].astype(BF)
    value = (flat[:, 2 * width :] + in_b_ref[1:2, width:]).astype(BF)
    qkv_ref[:, :width] = query
    qkv_ref[:, width : 2 * width] = key
    qkv_ref[:, 2 * width :] = value
    value_t = value.astype(F32).T.astype(BF)
    shape = (text, HEADS * text)
    key_at = lax.broadcasted_iota(jnp.int32, shape, 0)
    query_at = lax.rem(lax.broadcasted_iota(jnp.int32, shape, 1), text)
    seen = jnp.logical_and(key_at <= query_at, key_at < tok_ref[0])
    queries = spread_heads(query * jnp.asarray(HEAD_DIM**-0.5, BF))
    prob, ctx_t = attend_all(key, value_t, queries, seen)
    prob_ref[...] = prob
    ctx_t_ref[...] = ctx_t.astype(BF)
    y1 = start + nn(ctx_t.T.astype(BF), out_ref[...]) + out_b_ref[1:2]
    y1_ref[...] = y1
    unit, _ = normalise(y1)
    norm_d = (unit * gain_ref[3:4] + shift_ref[3:4]).astype(BF)
    norm_d_ref[...] = norm_d
    cross_q_ref[...] = (nn(norm_d, cross_ref[:, :width]) + in_b_ref[2:3, :width]).astype(BF)


def encoder_forward(
    len_ref, at_ref, x_ref, gain_ref, shift_ref, in_ref, in_b_ref, out_ref, out_b_ref,
    w1_ref, b1_ref, w2_ref, b2_ref, cin_ref,
    qkv_ref, ctx_t_ref, lse_ref, h1_ref, mem_ref, cross_ref,
    value_t, act, between,
):
    rows, width = x_ref.shape
    unit, _ = normalise(x_ref[...].astype(F32))
    norm_a = (unit * gain_ref[0:1] + shift_ref[0:1]).astype(BF)
    qkv_ref[:, :width] = (nn(norm_a, in_ref[:, :width]) + in_b_ref[0:1, :width]).astype(BF)
    key = nn(norm_a, in_ref[:, width : 2 * width]).astype(BF)
    qkv_ref[:, width : 2 * width] = key
    value = (nn(norm_a, in_ref[:, 2 * width :]) + in_b_ref[0:1, width:]).astype(BF)
    qkv_ref[:, 2 * width :] = value
    value_t[...] = value.astype(F32).T.astype(BF)

    def attend(at, pair):
        keys = qkv_ref[:, pl.ds(width + at, 128)]
        queries = qkv_ref[:, pl.ds(at, 128)] * jnp.asarray(HEAD_DIM**-0.5, BF)
        for odd in range(2):
            query = with_one(own_lanes(queries, odd), odd)
            score = nt(with_mask(keys, odd, len_ref[at_ref[0]]), query)
            highest = jnp.max(score, axis=0, keepdims=True)
            weight = jnp.exp(score - highest)
            total = jnp.sum(weight, axis=0, keepdims=True)
            context = nn(value_t[head_rows(at, odd)], weight.astype(BF)) * (1.0 / total)
            ctx_t_ref[head_rows(at, odd)] = context.astype(BF)
            lse_ref[pl.ds(2 * pair + odd, 1)] = highest + jnp.log(total)

    each_pair(attend)
    between()
    context = ctx_t_ref[...].astype(F32).T.astype(BF)
    h1 = x_ref[...].astype(F32) + nn(context, out_ref[...]) + out_b_ref[0:1]
    h1_ref[...] = h1
    unit, _ = normalise(h1)
    norm_b = (unit * gain_ref[1:2] + shift_ref[1:2]).astype(BF)

    hidden = nn(norm_b, w1_ref[...]) + b1_ref[0:1]
    act[...] = gelu_value(hidden).astype(BF)
    memory = (h1_ref[...] + nn(act[...], w2_ref[...]) + b2_ref[0:1]).astype(BF)
    mem_ref[...] = memory
    cross_ref[:, :width] = nn(memory, cin_ref[:, width : 2 * width]).astype(BF)
    cross_ref[:, width:] = (nn(memory, cin_ref[:, 2 * width :]) + in_b_ref[2:3, width:]).astype(BF)


def decoder_main(
    tok_ref, len_ref, at_ref, core_ref,
    y1_ref, norm_d_ref, cross_q_ref, cross_ref, mem_ref, cot_ref, gain_ref, shift_ref,
    in2_ref, out2_ref, out_b_ref, w1_ref, b1_ref, w2_ref, b2_ref,
    dec_ref, dmem_ref, early_ref, grad_ref, small_ref,
    probs, turned, cross_t, dkv, dq_t, fed,
):
    text, width = y1_ref.shape
    hidden_size = w1_ref.shape[1]
    slot = (core_ref[0], 1 - core_ref[0])
    small_ref[...] = jnp.zeros_like(small_ref)
    turned[...] = cross_ref[:, width:].astype(F32).T.astype(BF)

    def attend(at, pair):
        queries = both_heads(cross_q_ref[:, pl.ds(at, 128)] * jnp.asarray(HEAD_DIM**-0.5, BF))
        score = nt(cross_ref[:, pl.ds(at, 128)], queries)
        frame = lax.broadcasted_iota(jnp.int32, score.shape, 0)
        score = jnp.where(frame < len_ref[at_ref[0]], score, MASKED)
        weight = jnp.exp(score - jnp.max(score, axis=0, keepdims=True))
        prob = weight * (1.0 / jnp.sum(weight, axis=0, keepdims=True))
        probs[pair] = prob
        full = nn(turned[pl.ds(at, 128)], prob.astype(BF))
        for odd in range(2):
            cross_t[head_rows(at, odd)] = full[HEAD_DIM * odd : HEAD_DIM * odd + HEAD_DIM, text * odd : text * odd + text]

    each_pair(attend)
    context_t = cross_t[...]
    y2 = y1_ref[...] + nn(context_t.T.astype(BF), out2_ref[...]) + out_b_ref[2:3]
    unit_e, scale_e = normalise(y2)
    norm_e = (unit_e * gain_ref[4:5] + shift_ref[4:5]).astype(BF)
    norm_e_t = norm_e.astype(F32).T.astype(BF)
    valid = lax.broadcasted_iota(jnp.int32, (text, 1), 0) < tok_ref[0]
    grad_low = jnp.where(valid, cot_ref[...], jnp.zeros_like(cot_ref))
    grad = grad_low.astype(F32)
    grad_low_t = grad.T.astype(BF)
    chunk = 512

    def feed(index, sums):
        part = pl.ds(pl.multiple_of(index * chunk, chunk), chunk)
        hidden = nn(norm_e, w1_ref[:, part]) + b1_ref[1:2, part]
        value, slope = gelu_both(hidden)
        active = value.astype(BF)
        grad_hidden = (nt(grad_low, w2_ref[part]) * slope).astype(BF)
        bias = col_sum(grad_hidden)
        first = nn(norm_e_t, grad_hidden).astype(BF)
        for sub in range(chunk // width):
            row = index * (chunk // width) + sub
            small_ref[pl.ds(16 + row, 1)] = bias[:, width * sub : width * sub + width]
            at = pl.multiple_of(row * width, width)
            early_ref[slot[0], pl.ds(at, width)] = first[:, width * sub : width * sub + width]
        second = nn(grad_low_t, active).T.astype(BF)
        at = pl.multiple_of(jnp.where(index == 0, hidden_size, (index - 1) * chunk), chunk)
        early_ref[jnp.where(index == 0, slot[0], slot[1]), pl.ds(at, chunk)] = second
        return sums[0] + nn(active, w2_ref[part]), sums[1] + nt(grad_hidden, w1_ref[:, part])

    zeros = jnp.zeros((text, width), F32)
    feed_out, grad_norm = lax.fori_loop(0, hidden_size // chunk, feed, (zeros, zeros))
    fed()
    y3 = y2 + b2_ref[1:2] + feed_out
    dec_ref[...] = jnp.where(valid, y3, 0.0).astype(BF)
    small_ref[4:5] = col_sum(grad)
    grad_x, small_ref[0:1], small_ref[1:2] = norm_backward(grad_norm, unit_e, scale_e, gain_ref[4:5])
    grad = grad + grad_x
    grad_low = grad.astype(BF)
    small_ref[5:6] = col_sum(grad_low)
    base = hidden_size - chunk
    early_ref[slot[1], base + 3 * width :] = nn(context_t.astype(BF), grad_low).astype(BF)
    grad_ctx = nt(grad_low, out2_ref[...]).astype(BF)
    turned[...] = cross_ref[:, :width].astype(F32).T.astype(BF)
    mem_t = mem_ref[...].astype(F32).T.astype(BF)
    grad_ref[...] = grad_ctx.astype(F32)

    def attend_backward(at, pair):
        queries = both_heads(cross_q_ref[:, pl.ds(at, 128)] * jnp.asarray(HEAD_DIM**-0.5, BF))
        grads = both_heads(grad_ref[:, pl.ds(at, 128)].astype(BF))
        prob = probs[pair]
        dprob = nt(cross_ref[:, pl.ds(width + at, 128)], grads)
        inner = jnp.sum(dprob * prob, axis=0, keepdims=True)
        dscore = (prob * (dprob - inner)).astype(BF)
        dkv[:, pl.ds(at, 128)] = nn(dscore, queries).astype(BF)
        dkv[:, pl.ds(width + at, 128)] = nn(prob.astype(BF), grads).astype(BF)
        full = nn(turned[pl.ds(at, 128)], dscore)
        for odd in range(2):
            dq_t[head_rows(at, odd)] = full[HEAD_DIM * odd : HEAD_DIM * odd + HEAD_DIM, text * odd : text * odd + text]

    each_pair(attend_backward)
    dq = (dq_t[...] * HEAD_DIM**-0.5).T.astype(BF)
    small_ref[6:7] = col_sum(dq)
    small_ref[7:8] = col_sum(dkv[:, width:])
    norm_d = norm_d_ref[...]
    early_ref[slot[1], base : base + width] = nn(norm_d.astype(F32).T.astype(BF), dq).astype(BF)
    pairs = nn(mem_t, dkv[...]).astype(BF)
    early_ref[slot[1], base + width : base + 2 * width] = pairs[:, :width]
    early_ref[slot[1], base + 2 * width : base + 3 * width] = pairs[:, width:]
    dmem_ref[...] = nt(dkv[...], in2_ref[:, width:]).astype(BF)
    unit, scale = normalise(y1_ref[...])
    grad_x, small_ref[8:9], small_ref[9:10] = norm_backward(
        nt(dq, in2_ref[:, :width]), unit, scale, gain_ref[3:4]
    )
    grad_ref[...] = grad + grad_x


def decoder_self_backward(
    emb_ref, norm_c_ref, qkv_ref, ctx_t_ref, prob_ref, grad_ref, small_ref, gain_ref, in1_ref, out1_ref,
    late_ref, swap_ref,
):
    text, width = emb_ref.shape
    grad = grad_ref[...]
    grad_low = grad.astype(BF)
    small_ref[10:11] = col_sum(grad_low)
    dout1 = nn(ctx_t_ref[...], grad_low).astype(BF)
    late_ref[3 * width :] = dout1[: width - SPILL]
    swap_ref[text + SMALL :] = dout1[width - SPILL :]
    grad_ctx = nt(grad_low, out1_ref[...]).astype(BF)
    keys_t = qkv_ref[:, width : 2 * width].astype(F32).T.astype(BF)
    queries = spread_heads(qkv_ref[:, :width] * jnp.asarray(HEAD_DIM**-0.5, BF))
    dkeys, dvalues, dq_t = attend_all_backward(
        keys_t, qkv_ref[:, 2 * width :], queries, spread_heads(grad_ctx), prob_ref[...]
    )
    dqkv = jnp.concatenate([dq_t.T.astype(BF), dkeys, dvalues], axis=1)
    small_ref[11:12] = col_sum(dqkv[:, :width])
    small_ref[12:13] = col_sum(dqkv[:, 2 * width :])
    din1 = nn(norm_c_ref[...].astype(F32).T.astype(BF), dqkv).astype(BF)
    for part in range(3):
        late_ref[width * part : width * part + width] = din1[:, width * part : width * part + width]
    unit, scale = normalise(emb_ref[...].astype(F32) * math.sqrt(width))
    grad_x, small_ref[13:14], small_ref[14:15] = norm_backward(
        nt(dqkv, in1_ref[...]), unit, scale, gain_ref[2:3]
    )
    swap_ref[:text] = ((grad + grad_x) * math.sqrt(width)).astype(BF)
    swap_ref[text : text + SMALL] = small_ref[...].astype(BF)


def forward_and_decoder(
    tok_ref, len_ref, at_ref, core_ref,
    x_ref, in0, gain_ref, shift_ref, in_b_ref, out_b_ref, b1_ref, b2_ref,
    in_from, out_from, w1_from, w2_from,
    emb_from, y1_from, norm_c_from, dec_qkv_from, dec_ctx_t_from, prob_from, norm_d_from, cross_q_from, cot_from,
    qkv_to, ctx_t_to, h1_to, lse_ref, dec_ref, dmem_to, late_ref, swap_ref, keep_ref, send_ref,
    value_t, act, mem, cross, probs, cross_t, dkv, dq_t, grad, small, early,
    qkv_ref, ctx_t_ref, h1_ref, dmem_ref,
    in_ref, out_ref, w1_ref, w2_ref,
    emb_ref, y1_ref, norm_c_ref, dec_qkv_ref, dec_ctx_t_ref, prob_ref, norm_d_ref, cross_q_ref, cot_ref,
    load_sems, store_sems,
):
    loads = fetch(
        load_sems, (out_from, out_ref), (w1_from, w1_ref), (w2_from, w2_ref), (in_from.at[1:], in_ref),
        (emb_from, emb_ref), (y1_from, y1_ref), (norm_c_from, norm_c_ref), (dec_qkv_from, dec_qkv_ref),
        (dec_ctx_t_from, dec_ctx_t_ref), (prob_from, prob_ref), (norm_d_from, norm_d_ref),
        (cross_q_from, cross_q_ref), (cot_from, cot_ref),
    )
    stores = []

    def send(*pairs):
        for held, ref in pairs:
            stores.append(pltpu.make_async_copy(held, ref, store_sems.at[len(stores)]))
            stores[-1].start()

    def arrived():
        for load in loads:
            load.wait()
        send((qkv_ref, qkv_to), (ctx_t_ref, ctx_t_to))

    in1, in2 = in_ref.at[0], in_ref.at[1]
    out0, out1, out2 = (out_ref.at[i] for i in range(3))
    encoder_forward(
        len_ref, at_ref, x_ref, gain_ref, shift_ref, in0, in_b_ref, out0, out_b_ref,
        w1_ref.at[0], b1_ref, w2_ref.at[0], b2_ref, in2,
        qkv_ref, ctx_t_ref, lse_ref, h1_ref, mem, cross,
        value_t, act, arrived,
    )
    half = early.shape[1]
    full = half - 4 * x_ref.shape[1]
    places = (keep_ref, send_ref)

    def fed():
        send((h1_ref, h1_to), *[(early.at[i, :full], places[i].at[:full]) for i in range(2)])

    decoder_main(
        tok_ref, len_ref, at_ref, core_ref,
        y1_ref, norm_d_ref, cross_q_ref, cross, mem, cot_ref, gain_ref, shift_ref,
        in2, out2, out_b_ref, w1_ref.at[1], b1_ref, w2_ref.at[1], b2_ref,
        dec_ref, dmem_ref, early, grad, small,
        probs, value_t, cross_t, dkv, dq_t, fed,
    )
    send((dmem_ref, dmem_to), *[(early.at[i, full:], places[i].at[full:half]) for i in range(2)])
    decoder_self_backward(
        emb_ref, norm_c_ref, dec_qkv_ref, dec_ctx_t_ref, prob_ref, grad, small, gain_ref, in1, out1,
        late_ref, swap_ref,
    )
    send((swap_ref, send_ref.at[half:]))
    for store in stores:
        store.wait()


def encoder_backward(
    len_ref, at_ref, core_ref,
    h1_ref, dmem_ref, lse_ref, gain_ref, shift_ref, w1_ref, b1_ref, w2_ref,
    x_from, ctx_t_from, qkv_from, late_from, in_from, out_from,
    dx_ref, keep_ref, send_ref,
    grad_hid, dh1, dctx, key_t, dq_t, dqkv, small, feed, attn,
    x_ref, ctx_t_ref, qkv_ref, late_ref, in_ref, out_ref, load_sems, store_sems,
):
    loads = fetch(
        load_sems, (ctx_t_from, ctx_t_ref), (late_from, late_ref), (out_from.at[0], out_ref),
        (qkv_from, qkv_ref), (x_from, x_ref), (in_from.at[0], in_ref),
    )
    hidden = w1_ref.shape[1]
    places = (keep_ref, send_ref)
    stores = []

    def send(*pairs):
        for held, ref in pairs:
            stores.append(pltpu.make_async_copy(held, ref, store_sems.at[len(stores)]))
            stores[-1].start()

    def fed():
        for load in loads:
            load.wait()
        send(*[(feed.at[i, :hidden], places[i].at[:hidden]) for i in range(2)])

    encoder_feed_backward(
        core_ref, h1_ref, dmem_ref, ctx_t_ref, gain_ref, shift_ref, w1_ref, b1_ref, w2_ref, out_ref, late_ref,
        dh1, dctx, feed, small,
        grad_hid, fed,
    )
    cut = feed.shape[1]
    encoder_attention_backward(
        len_ref, at_ref, core_ref, x_ref, qkv_ref, lse_ref, dctx, dh1, gain_ref, shift_ref, in_ref,
        dx_ref, attn,
        key_t, dq_t, dqkv, small,
    )
    send(*[(feed.at[i, hidden:], places[i].at[hidden:cut]) for i in range(2)])
    send(*[(attn.at[i], places[i].at[cut:]) for i in range(2)])
    for store in stores:
        store.wait()


def fetch(sems, *pairs):
    copies = [pltpu.make_async_copy(ref, held, sems.at[i]) for i, (ref, held) in enumerate(pairs)]
    for copy in copies:
        copy.start()
    return copies


def early_merge(
    core_ref, ids_ref, swap_from, keep_ref, other_ref, out_ref, swap_ref, keep, other, swapped_ref, out, sems, out_sems
):
    core = core_ref[0]
    text = ids_ref.shape[1] // 2
    half = keep.shape[0]
    chunk = half // 4
    loads = fetch(
        sems, (swap_from, swap_ref), (other_ref.at[half:], swapped_ref), (keep_ref, keep),
        (other_ref.at[:half], other),
    )
    loads[0].wait()
    loads[1].wait()
    grad = jnp.concatenate([swap_ref[:text], swapped_ref[:text]], axis=0)
    for at in range(0, half, chunk):
        row = lax.broadcasted_iota(jnp.int32, (chunk, 2 * text), 0) + (core * half + at)
        hot = jnp.where(row == ids_ref[...], 1.0, 0.0).astype(BF)
        out[half + at : half + at + chunk] = nn(hot, grad).astype(BF)

    @pl.when(core == 1)
    def _():
        rest = swap_ref[text:].astype(F32) + swapped_ref[text:].astype(F32)
        out[2 * half - rest.shape[0] :] = rest.astype(BF)

    table = pltpu.make_async_copy(out.at[half:], out_ref.at[half:], out_sems.at[0])
    table.start()
    for load in loads[2:]:
        load.wait()
    out[:half] = (keep[...].astype(F32) + other[...].astype(F32)).astype(BF)
    sums = pltpu.make_async_copy(out.at[:half], out_ref.at[:half], out_sems.at[1])
    sums.start()
    table.wait()
    sums.wait()


def late_merge(keep_ref, other_ref, early_ref, out_ref, keep, other, early, out, sems, out_sems):
    count, size, width = out.shape
    size = size - early.shape[1]
    loads = fetch(sems, (early_ref, early), (keep_ref, keep), (other_ref, other))
    loads[0].wait()
    own = jnp.sum(early[...].astype(F32), axis=0).astype(BF)
    for load in loads[1:]:
        load.wait()
    stores = []
    part = count // 4
    for step in range(4):
        rows = slice(step * part * size, (step + 1) * part * size)
        places = slice(step * part, step * part + part)
        late = (keep[rows].astype(F32) + other[rows].astype(F32)).astype(BF)
        out[places, :size] = late.reshape(part, size, width)
        for place in range(step * part, step * part + part):
            out[place, size:] = own
        stores.append(pltpu.make_async_copy(out.at[places], out_ref.at[places], out_sems.at[step]))
        stores[-1].start()
    for store in stores:
        store.wait()


def late_spread(parts_ref, out_ref, parts, out, sems, out_sems):
    size = out.shape[1]
    half = out.shape[0] // 2
    ends = (slice(0, half), slice(half, 2 * half))
    loads = fetch(sems, *[(parts_ref.at[end, :size], parts.at[end]) for end in ends])
    total = 0.0
    for load, end in zip(loads, ends):
        load.wait()
        total = total + jnp.sum(parts[end].astype(F32), axis=0)
    late = total.astype(BF)
    stores = []
    for step, end in enumerate(ends):
        for place in range(end.start, end.stop):
            out[place] = late
        stores.append(pltpu.make_async_copy(out.at[end], out_ref.at[end], out_sems.at[step]))
        stores[-1].start()
    for store in stores:
        store.wait()


def early_outputs(
    core_ref, rate_ref, mine_ref, other_ref,
    table_ref, in_ref, out_ref, w1_ref, w2_ref, rest_ref,
    grads, table, sems,
):
    rate = rate_ref[0]
    first = core_ref[0] == 0
    count, size, width = mine_ref.shape
    hidden = w2_ref.shape[1]
    half = grads.shape[0] // 2
    each = 2 * half // count
    skip = size - each

    def chunk(index, carry):
        at = pl.multiple_of(index * each, each)
        for part, held in ((0, grads), (count // 2, table)):
            mine, other = mine_ref[part + index, skip:], other_ref[part + index, skip:]
            held[pl.ds(at, each)] = jnp.where(first, mine, other).astype(F32) * rate
            held[pl.ds(half + at, each)] = jnp.where(first, other, mine).astype(F32) * rate
        return carry

    lax.fori_loop(0, count // 2, chunk, 0)
    tail = mine_ref[count - 2 :, skip:].reshape(2 * each, width)
    other_tail = other_ref[count - 2 :, skip:].reshape(2 * each, width)
    rest_ref[...] = jnp.where(first, other_tail, tail)[2 * each - rest_ref.shape[0] :]
    base = 2 * hidden
    pairs = [(table.at[: table_ref.shape[0]], table_ref), (grads.at[hidden:base], w2_ref.at[1])]
    pairs += [(grads.at[at : at + width], w1_ref.at[1, :, at : at + width]) for at in range(0, hidden, width)]
    pairs += [
        (grads.at[base + at : base + at + width], in_ref.at[2, :, at : at + width])
        for at in range(0, 3 * width, width)
    ]
    pairs.append((grads.at[base + 3 * width :], out_ref.at[2]))
    hand_out(sems, *pairs)


def late_outputs(
    half_ref, rate_ref, early_ref, rows_ref, in_in, out_in, w1_in, w2_in,
    in_ref, out_ref, w1_ref, w2_ref, rest_ref,
    rows, grads, sems, out_sems,
):
    size, width = rows.shape
    hidden = w2_ref.shape[1]
    cut = (width - SPILL) // 2
    base = hidden + 2 * width
    attn = base + cut
    over = size - attn - width
    (load,) = fetch(sems, (rows_ref, rows))
    load.wait()

    def scale(index, carry):
        part = pl.ds(pl.multiple_of(index * width, width), width)
        grads[part] = rows[part].astype(F32) * rate_ref[0]
        return carry

    lax.fori_loop(0, size // width, scale, 0)
    grads[size:] = early_ref[SMALL:].astype(F32) * rate_ref[0]
    rest_ref[...] = rows[size - 2 * SMALL : size - SMALL]

    def block(at, rows=width):
        return grads.at[at : at + rows]

    def first():
        pairs = [(block(at), w1_ref.at[0, :, at : at + width]) for at in range(0, hidden, width)]
        pairs += [(block(hidden + at), in_ref.at[1, :, at : at + width]) for at in (0, width)]
        pairs.append((block(base, cut), out_ref.at[1, :cut]))
        pairs.append((block(attn), in_ref.at[0, :, :width]))
        pairs.append((block(attn + width, over), in_ref.at[0, :over, width : 2 * width]))
        return pairs

    def second():
        pairs = [(block(0, hidden), w2_ref.at[0])]
        pairs.append((block(hidden), in_ref.at[1, :, 2 * width :]))
        pairs.append((block(hidden + width), out_ref.at[0]))
        pairs.append((block(base, cut), out_ref.at[1, cut : 2 * cut]))
        pairs.append((block(size, SPILL), out_ref.at[1, 2 * cut :]))
        pairs.append((block(attn, width - over), in_ref.at[0, over:, width : 2 * width]))
        pairs.append((block(attn + width - over), in_ref.at[0, :, 2 * width :]))
        return pairs

    @pl.when(half_ref[0] == 0)
    def _():
        hand_out(out_sems, *first())

    @pl.when(half_ref[0] == 1)
    def _():
        hand_out(out_sems, *second())


def small_outputs(
    core_ref, rate_ref, mine_ref, other_ref, early_ref,
    gain_ref, shift_ref, in_b_ref, out_b_ref, b1_ref, b2_ref,
):
    width = mine_ref.shape[1]
    rate = rate_ref[0]
    enc = jnp.where(core_ref[0] == 1, mine_ref[...], other_ref[...]).astype(F32) * rate
    dec = early_ref[:SMALL].astype(F32) * rate
    for row, (part, at) in enumerate(((enc, 0), (enc, 8), (dec, 13), (dec, 8), (dec, 0))):
        gain_ref[row : row + 1] = part[at : at + 1]
        shift_ref[row : row + 1] = part[at + 1 : at + 2]
    for row, (part, at, next_at) in enumerate(((enc, 2, 3), (dec, 11, 12), (dec, 6, 7))):
        in_b_ref[row : row + 1, :width] = part[at : at + 1]
        in_b_ref[row : row + 1, width:] = part[next_at : next_at + 1]
    for row, (part, at) in enumerate(((enc, 11), (dec, 10), (dec, 5))):
        out_b_ref[row : row + 1] = part[at : at + 1]
    for row, (part, at) in enumerate(((enc, 10), (dec, 4))):
        b2_ref[row : row + 1] = part[at : at + 1]
    for row, part in enumerate((enc, dec)):
        for block in range(b1_ref.shape[1] // width):
            b1_ref[row : row + 1, width * block : width * block + width] = part[16 + block : 17 + block]


def frames_back(place_ref, own_ref, next_ref, second_ref, third_ref, out_ref):
    count = out_ref.shape[0]
    for shift, ref in enumerate((own_ref, next_ref, second_ref, third_ref)):
        out_ref[lax.rem(place_ref[0] + (count - shift), count)] = ref[...].astype(F32)


def encoder_feed_backward(
    core_ref, h1_ref, dmem_ref, ctx_t_ref, gain_ref, shift_ref, w1_ref, b1_ref, w2_ref, out_ref, late_ref,
    dh1_ref, dctx_ref, feed_ref, small_ref,
    grad_hid, fed,
):
    width = h1_ref.shape[1]
    hidden_size = w1_ref.shape[1]
    slot = (core_ref[0], 1 - core_ref[0])
    cut = (width - SPILL) // 2
    small_ref[...] = jnp.zeros_like(small_ref)
    unit, _ = normalise(h1_ref[...])
    norm_b = unit * gain_ref[1:2] + shift_ref[1:2]
    norm_b_t = norm_b.T.astype(BF)
    norm_b = norm_b.astype(BF)
    grad_low = dmem_ref[...]
    grad_low_t = grad_low.astype(F32).T.astype(BF)
    chunk = FEED_CHUNK

    def feed(index, carry):
        part = pl.ds(pl.multiple_of(index * chunk, chunk), chunk)
        hidden = nn(norm_b, w1_ref[:, part]) + b1_ref[0:1, part]
        value, slope = gelu_both(hidden)
        grad_hidden = (nt(grad_low, w2_ref[part]) * slope).astype(BF)
        grad_hid[:, part] = grad_hidden
        bias = col_sum(grad_hidden)
        first = nn(norm_b_t, grad_hidden).astype(BF)
        for sub in range(chunk // width):
            row = index * (chunk // width) + sub
            small_ref[pl.ds(16 + row, 1)] = bias[:, width * sub : width * sub + width]
            at = pl.multiple_of(row * width, width)
            feed_ref[slot[0], pl.ds(at, width)] = first[:, width * sub : width * sub + width]
        feed_ref[slot[1], part] = nn(grad_low_t, value.astype(BF)).T.astype(BF)
        return carry

    lax.fori_loop(0, hidden_size // chunk, feed, 0)
    fed()
    feed_ref[slot[0], hidden_size : hidden_size + 2 * width] = late_ref[: 2 * width]
    feed_ref[slot[1], hidden_size : hidden_size + width] = late_ref[2 * width : 3 * width]
    feed_ref[slot[0], hidden_size + 2 * width :] = late_ref[3 * width : 3 * width + cut]
    feed_ref[slot[1], hidden_size + 2 * width :] = late_ref[3 * width + cut :]
    grad = grad_low.astype(F32)
    small_ref[10:11] = col_sum(grad)
    unit, scale = normalise(h1_ref[...])
    grad_x, small_ref[8:9], small_ref[9:10] = norm_backward(
        nt(grad_hid[...], w1_ref[...]), unit, scale, gain_ref[1:2]
    )
    grad = grad + grad_x
    dh1_ref[...] = grad
    grad_low = grad.astype(BF)
    small_ref[11:12] = col_sum(grad_low)
    feed_ref[slot[1], hidden_size + width : hidden_size + 2 * width] = nn(ctx_t_ref[...], grad_low).astype(BF)
    dctx_ref[...] = nt(grad_low, out_ref[...]).astype(BF)


def encoder_attention_backward(
    len_ref, at_ref, core_ref, x_ref, qkv_ref, lse_ref, dctx_ref, dh1_ref, gain_ref, shift_ref, in_ref,
    dx_ref, attn_ref,
    key_t, dq_t, dqkv, small_ref,
):
    rows, width = x_ref.shape
    key_t[...] = qkv_ref[:, width : 2 * width].astype(F32).T.astype(BF)

    def attend_backward(at, pair):
        keys = qkv_ref[:, pl.ds(width + at, 128)]
        values = qkv_ref[:, pl.ds(2 * width + at, 128)]
        queries = qkv_ref[:, pl.ds(at, 128)] * jnp.asarray(HEAD_DIM**-0.5, BF)
        grads = dctx_ref[:, pl.ds(at, 128)]
        dkey = 0.0
        dvalue = 0.0
        for odd in range(2):
            query = own_lanes(queries, odd)
            score = nt(with_mask(keys, odd, len_ref[at_ref[0]]), with_one(query, odd))
            prob = jnp.exp(score - lse_ref[pl.ds(2 * pair + odd, 1)])
            own_grad = own_lanes(grads, odd)
            dprob = nt(values, own_grad)
            inner = jnp.sum(dprob * prob, axis=0, keepdims=True)
            dscore = (prob * (dprob - inner)).astype(BF)
            dkey = dkey + nn(dscore, query)
            dvalue = dvalue + nn(prob.astype(BF), own_grad)
            dq_t[head_rows(at, odd)] = nn(key_t[head_rows(at, odd)], dscore)
        dqkv[:, pl.ds(width + at, 128)] = dkey.astype(BF)
        dqkv[:, pl.ds(2 * width + at, 128)] = dvalue.astype(BF)

    each_pair(attend_backward)
    dqkv[:, :width] = (dq_t[...].T * HEAD_DIM**-0.5).astype(BF)
    small_ref[2:3] = col_sum(dqkv[:, :width])
    small_ref[3:4] = col_sum(dqkv[:, 2 * width :])
    unit, scale = normalise(x_ref[...].astype(F32))
    norm_a = unit * gain_ref[0:1] + shift_ref[0:1]
    din = nn(norm_a.T.astype(BF), dqkv[...]).astype(BF)
    blocks = [din[:, width * part : width * part + width] for part in range(3)]
    grad_x, small_ref[0:1], small_ref[1:2] = norm_backward(
        nt(dqkv[...], in_ref[...]), unit, scale, gain_ref[0:1]
    )
    dx_ref[...] = (dh1_ref[...] + grad_x).astype(BF)
    small = small_ref[...].astype(BF)
    packed = jnp.concatenate(blocks + [small, jnp.zeros_like(small)], axis=0)
    half = attn_ref.shape[1]
    attn_ref[core_ref[0]] = packed[:half]
    attn_ref[1 - core_ref[0]] = packed[half:]


def swap_cores(array):
    return lax.ppermute(array, "core", [(0, 1), (1, 0)])


def body(
    frames, utt_len, token_ids, tok_len, step, embed, norm_gain, norm_bias, attn_in, attn_in_bias,
    attn_out, attn_out_bias, ff_in, ff_in_bias, ff_out, ff_out_bias, cotangent,
):
    ring = ("frame", "pair")
    devices = lax.axis_size(ring)
    core = lax.axis_index("core")
    core_of = core[None]
    frame_at = lax.axis_index("frame")
    vocab, width = embed.shape
    hidden = ff_in.shape[2]
    frame_count = lax.axis_size("frame")
    local_len = frames.shape[2]
    rows = local_len * frame_count
    text = token_ids.shape[2]
    lengths = utt_len[0]
    frame_of = frame_at[None]
    my_tok = tok_len[0]
    arrived = lax.all_to_all(frames[0], "frame", split_axis=0, concat_axis=1, tiled=True)
    source = arrived.reshape(rows, width)
    ids = token_ids[0, 0]
    both_ids = jnp.concatenate([ids, swap_cores(ids)])[None]
    rows_in, both_ids = lax.optimization_barrier((embed[ids], both_ids))
    count_step = step[0].astype(F32)
    rate = jnp.minimum(lax.rsqrt(count_step), count_step * WARMUP ** (-1.5)) * WARMUP**0.5
    rate = rate[None]

    y1, norm_c, dec_qkv, dec_ctx_t, dec_prob, norm_d, cross_q = call(
        decoder_start,
        [
            ((text, width), F32), ((text, width), BF), ((text, 3 * width), BF), ((width, text), BF),
            ((text, HEADS * text), F32), ((text, width), BF), ((text, width), BF),
        ],
        [
            rows_in, norm_gain, norm_bias, (attn_in, 1), attn_in_bias, (attn_out, 1),
            attn_out_bias, (attn_in, 2),
        ],
        [my_tok],
        flops=2 * text * width * width * 5,
    )
    half = 2 * width + hidden
    swap_rows = text + SMALL + SPILL
    decoder_args = [rows_in, y1, norm_c, dec_qkv, dec_ctx_t, dec_prob, norm_d, cross_q, cotangent[0, 0]]
    enc_qkv, enc_ctx_t, h1, lse, dec_out, dmem, self_grads, swap, early, early_send = call(
        forward_and_decoder,
        [
            ((rows, 3 * width), BF, None), ((width, rows), BF, None), ((rows, width), F32, None),
            ((8, rows), F32), ((text, width), BF), ((rows, width), BF, None), ((4 * width - SPILL, width), BF),
            ((swap_rows, width), BF), ((half, width), BF, None), ((half + swap_rows, width), BF, None),
        ],
        [
            source, (attn_in, 0), norm_gain, norm_bias, attn_in_bias, attn_out_bias, ff_in_bias, ff_out_bias,
            (attn_in, None), (attn_out, None), (ff_in, None), (ff_out, None),
        ]
        + [(arg, None) for arg in decoder_args],
        [my_tok, lengths, frame_of, core_of],
        [
            pltpu.VMEM((width, rows), BF), pltpu.VMEM((rows, hidden), BF), pltpu.VMEM((rows, width), BF),
            pltpu.VMEM((rows, 2 * width), BF), pltpu.VMEM((HEADS // 2, rows, 2 * text), F32),
            pltpu.VMEM((width, text), F32), pltpu.VMEM((rows, 2 * width), BF),
            pltpu.VMEM((width, text), F32), pltpu.VMEM((text, width), F32),
            pltpu.VMEM((SMALL, width), F32), pltpu.VMEM((2, half, width), BF),
            pltpu.VMEM((rows, 3 * width), BF), pltpu.VMEM((width, rows), BF), pltpu.VMEM((rows, width), F32),
            pltpu.VMEM((rows, width), BF),
            pltpu.VMEM((2,) + attn_in.shape[1:], BF), pltpu.VMEM(attn_out.shape, BF),
            pltpu.VMEM(ff_in.shape, BF), pltpu.VMEM(ff_out.shape, BF),
        ]
        + [pltpu.VMEM(arg.shape, arg.dtype) for arg in decoder_args]
        + [pltpu.SemaphoreType.DMA((13,)), pltpu.SemaphoreType.DMA((9,))],
        flops=2 * rows * width * (10 * width + 2 * rows + 2 * hidden)
        + 2 * text * width * (6 * hidden + 7 * rows + 26 * width),
    )
    (early_sum,) = call(
        early_merge,
        [((2 * half, width), BF, None)],
        [both_ids, (swap, None), (early, None), (swap_cores(early_send), "vmem")],
        [core_of],
        [
            pltpu.VMEM((swap_rows, width), BF), pltpu.VMEM((half, width), BF), pltpu.VMEM((half, width), BF),
            pltpu.VMEM((swap_rows, width), BF), pltpu.VMEM((2 * half, width), BF),
            pltpu.SemaphoreType.DMA((4,)), pltpu.SemaphoreType.DMA((2,)),
        ],
        flops=4 * half * width * text,
        limit=20,
    )
    early_sum, dmem = lax.optimization_barrier((early_sum, dmem))
    early_parts = lax.all_to_all(
        early_sum.reshape(devices, -1, width), ring, split_axis=0, concat_axis=0, tiled=True
    )
    early_own = jnp.sum(early_parts.astype(F32), axis=0).astype(BF)

    feed_half = (5 * width - SPILL) // 2 + hidden
    attn_half = 3 * width // 2 + SMALL
    late_half = feed_half + attn_half
    dx, late, late_send = call(
        encoder_backward,
        [((rows, width), BF), ((late_half, width), BF, None), ((late_half, width), BF, None)],
        [
            h1, dmem, lse, norm_gain, norm_bias, (ff_in, 0), ff_in_bias, (ff_out, 0), (source, None),
            (enc_ctx_t, None), (enc_qkv, None), (self_grads, None), (attn_in, None), (attn_out, None),
        ],
        [lengths, frame_of, core_of],
        [
            pltpu.VMEM((rows, hidden), BF), pltpu.VMEM((rows, width), F32), pltpu.VMEM((rows, width), BF),
            pltpu.VMEM((width, rows), BF), pltpu.VMEM((width, rows), F32), pltpu.VMEM((rows, 3 * width), BF),
            pltpu.VMEM((SMALL, width), F32), pltpu.VMEM((2, feed_half, width), BF),
            pltpu.VMEM((2, attn_half, width), BF),
            pltpu.VMEM((rows, width), BF), pltpu.VMEM((width, rows), BF), pltpu.VMEM((rows, 3 * width), BF),
            pltpu.VMEM(self_grads.shape, BF), pltpu.VMEM((width, 3 * width), BF), pltpu.VMEM((width, width), BF),
            pltpu.SemaphoreType.DMA((6,)), pltpu.SemaphoreType.DMA((6,)),
        ],
        flops=2 * rows * width * (5 * hidden + 5 * rows + 8 * width),
    )
    late_size = late_half // devices
    early_size = 2 * half // devices
    mixed_shape = (devices, late_size + early_size, width)
    (mixed,) = call(
        late_merge,
        [(mixed_shape, BF, None)],
        [(late, None), (swap_cores(late_send), None), (early_parts, None)],
        scratch=[
            pltpu.VMEM((late_half, width), BF), pltpu.VMEM((late_half, width), BF),
            pltpu.VMEM((devices, early_size, width), BF), pltpu.VMEM(mixed_shape, BF),
            pltpu.SemaphoreType.DMA((3,)), pltpu.SemaphoreType.DMA((4,)),
        ],
        limit=24,
    )
    mixed = lax.all_to_all(mixed, ring, split_axis=0, concat_axis=0, tiled=True)
    chunks = dx.reshape(frame_count, local_len, width)
    moved = []
    for shift in range(frame_count):
        target = lax.rem(frame_at + shift, frame_count)
        chunk = lax.dynamic_index_in_dim(chunks, target, keepdims=False)
        if shift:
            chunk = lax.ppermute(chunk, "frame", [(i, (i + shift) % frame_count) for i in range(frame_count)])
        moved.append(chunk)
    mixed, moved = lax.optimization_barrier((mixed, moved))
    late_shape = (devices, late_size, width)
    (late_own,) = call(
        late_spread,
        [(late_shape, BF, None)],
        [(mixed, None)],
        scratch=[
            pltpu.VMEM(late_shape, BF), pltpu.VMEM(late_shape, BF),
            pltpu.SemaphoreType.DMA((2,)), pltpu.SemaphoreType.DMA((2,)),
        ],
    )
    early_other = swap_cores(mixed)
    (frames_grad,) = call(
        frames_back, [((frame_count, local_len, width), F32)], moved, [frame_of], limit=16
    )
    late_mine = lax.all_to_all(late_own, ring, split_axis=0, concat_axis=0, tiled=True)
    in_shape = (3, width, 3 * width)
    out_shape = (3, width, width)
    w1_shape = (2, width, hidden)
    w2_shape = (2, hidden, width)
    table_grad, in_grad, out_grad, w1_grad, w2_grad, early_rest = call(
        early_outputs,
        [
            ((vocab, width), F32, None), (in_shape, F32, None), (out_shape, F32, None),
            (w1_shape, F32, None), (w2_shape, F32, None), ((SMALL + SPILL, width), BF),
        ],
        [mixed, early_other],
        [core_of, rate],
        [
            pltpu.VMEM((2 * half, width), F32), pltpu.VMEM((2 * half, width), F32),
            pltpu.SemaphoreType.DMA((14,)),
        ],
        limit=40,
    )
    late_mine, early_rest, frames_grad = lax.optimization_barrier((late_mine, early_rest, frames_grad))
    late_mine = late_mine.reshape(late_half, width)
    late_other = swap_cores(late_mine)
    results = (in_grad, out_grad, w1_grad, w2_grad)
    rests = []
    for rows_of_half, which in ((late_mine, core_of), (late_other, 1 - core_of)):
        *results, rest = call(
            late_outputs,
            [
                (in_shape, F32, None), (out_shape, F32, None), (w1_shape, F32, None),
                (w2_shape, F32, None), ((SMALL, width), BF),
            ],
            [early_rest, (rows_of_half, "vmem")] + [(result, None) for result in results],
            [which, rate],
            [
                pltpu.VMEM((late_half, width), BF), pltpu.VMEM((late_half + SPILL, width), F32),
                pltpu.SemaphoreType.DMA((1,)), pltpu.SemaphoreType.DMA((16,)),
            ],
            aliases={4: 0, 5: 1, 6: 2, 7: 3},
            limit=16,
        )
        rests.append(rest)
    in_grad, out_grad, w1_grad, w2_grad = results
    gain_grad, shift_grad, in_b_grad, out_b_grad, b1_grad, b2_grad = call(
        small_outputs,
        [
            ((5, width), F32), ((5, width), F32), ((3, 2 * width), F32), ((3, width), F32),
            ((2, hidden), F32), ((2, width), F32),
        ],
        rests + [early_rest],
        [core_of, rate],
        limit=32,
    )
    return (
        dec_out[None, None],
        frames_grad[None],
        table_grad,
        gain_grad,
        shift_grad,
        in_grad,
        in_b_grad,
        out_grad,
        out_b_grad,
        w1_grad,
        b1_grad,
        w2_grad,
        b2_grad,
    )


def solution(mesh):
    groups = ("pair", "core")
    frames, batch = mesh.devices.shape
    split = Mesh(mesh.devices.reshape(frames, batch // 2, 2), ("frame",) + groups)
    placed = (
        P(groups, None, "frame", None),
        P(groups, None),
        P(groups, "frame", None),
        P(groups, "frame"),
    ) + (P(),) * 12 + (P(groups, "frame", None, None),)
    results = (P(groups, "frame", None, None), P(groups, None, "frame", None)) + (P(),) * 11
    return jax.shard_map(body, mesh=split, in_specs=placed, out_specs=results, check_vma=False)
```
